128 devices in a mesh: tok: 32 (over z, y, core), exp: 4 (over x).
Axes of the slice: x: 4, y: 4, z: 4, core: 2. Of those that a mesh axis runs over, the one named last changes fastest.
Arguments:
- tokens: bfloat16 [2, 32, 576, 384], P(None, 'tok', 'exp'), may hold values from -6 to 6
- patch_counts: int32 [2, 32], P(None, 'tok'), may hold values from 196 to 576, as said below
- attn_routes: int32 [2, 32, 576, 4], P(None, 'tok', 'exp'), may hold values from 0 to 11, all different within a row; in each aligned block of 144 rows (0 to 143, 144 to 287, ..., all dimensions but the last counted through in order) at most 64 rows name the same one
- mlp_routes: int32 [2, 32, 576, 4], P(None, 'tok', 'exp'), may hold values from 0 to 11, all different within a row; in each aligned block of 144 rows (0 to 143, 144 to 287, ..., all dimensions but the last counted through in order) at most 64 rows name the same one
- norm1_gain: bfloat16 [384], P(('tok', 'exp')), may hold values from 0.5 to 1.5
- norm1_bias: bfloat16 [384], P(('tok', 'exp')), may hold values from -1.1953125 to 1.1953125
- norm2_gain: bfloat16 [384], P(('tok', 'exp')), may hold values from 0.5 to 1.5
- norm2_bias: bfloat16 [384], P(('tok', 'exp')), may hold values from -1.1953125 to 1.1953125
- key_value_weight: bfloat16 [384, 768], P(('tok', 'exp')), may hold values from -0.3125 to 0.3125
- attn_router: bfloat16 [384, 12], P(('tok', 'exp')), may hold values from -0.15625 to 0.15625
- mlp_router: bfloat16 [384, 12], P(('tok', 'exp')), may hold values from -0.15625 to 0.15625
- query_weight: bfloat16 [12, 384, 384], P('exp', 'tok'), may hold values from -0.3125 to 0.3125
- output_weight: bfloat16 [12, 384, 384], P('exp', 'tok'), may hold values from -2.5 to 2.5
- up_weight: bfloat16 [12, 384, 1536], P('exp', 'tok'), may hold values from -0.3125 to 0.3125
- down_weight: bfloat16 [12, 1536, 384], P('exp', 'tok'), may hold values from -0.15625 to 0.15625
- cotangent: bfloat16 [2, 32, 576, 384], P(None, 'tok', 'exp'), may hold values from -6 to 6
Outputs:
- layer_out: bfloat16 [2, 32, 576, 384], P(None, 'tok', 'exp')
- tokens_grad: bfloat16 [2, 32, 576, 384], P(None, 'tok', 'exp')
- norm1_gain_grad: float32 [384], P(('tok', 'exp'))
- norm1_bias_grad: float32 [384], P(('tok', 'exp'))
- norm2_gain_grad: float32 [384], P(('tok', 'exp'))
- norm2_bias_grad: float32 [384], P(('tok', 'exp'))
- key_value_grad: float32 [384, 768], P(('tok', 'exp'))
- attn_router_grad: float32 [384, 12], P(('tok', 'exp'))
- mlp_router_grad: float32 [384, 12], P(('tok', 'exp'))
- query_grad: float32 [12, 384, 384], P('exp', 'tok')
- output_grad: float32 [12, 384, 384], P('exp', 'tok')
- up_grad: float32 [12, 384, 1536], P('exp', 'tok')
- down_grad: float32 [12, 1536, 384], P('exp', 'tok')
The draws below stay inside these ranges and needn't reach their ends.
Inputs may be any that keep to these rules, and one draw needn't show every extreme that they name: `patch_counts`: each image has 196 or 576 real patches, its first slots; among the images that one index of tok holds, at least one has 576. `attn_routes`: each token names 4 different experts; within each aligned block of 144 slots (one image's slots on one index of exp) no expert is named by more than 64 tokens, a bound that some block reaches. `mlp_routes`: as for attn_routes: 4 different experts a token, at most 64 tokens of an aligned block of 144 slots for one expert, reached in some blocks.
All inputs are finite; a program needn't handle non-finite values.
Results may differ from the reference program's by a relative error of at most 0.025.
Values may be sent and summed in bfloat16 or wider, within the bound.
No kernel may reach another device: no remote copies, remote signals or barrier semaphores. Data moves between devices by JAX's collectives and lax.ppermute only.
A program may use at most 256 MiB of HBM per device.

```python
import math
import jax
import jax.numpy as jnp
import numpy as np
from jax import lax

D = 384
HEADS = 6
HEAD_DIM = 64
FF = 1536
TOP = 4
SLOTS = 576
SHORT = 196
CAP = 64
MB = 2
IMGS = 1
ATT = 384
EXPERTS = 12
IMAGES = 32
SQ = 144
N_EXP = 4


def draw_patch_counts(key, part):
    key = jax.random.fold_in(key, 11)
    first_key, second_key = jax.random.split(key)
    group_count = IMAGES // IMGS
    coin_flips = jax.random.randint(first_key, (MB, IMAGES), 0, 2)
    forced = jax.random.randint(second_key, (group_count,), 0, MB * IMGS)
    ordinal = jnp.arange(MB, dtype=jnp.int32)[:, None, None] * IMGS + jnp.arange(IMGS, dtype=jnp.int32)[None, None, :]
    chosen = (ordinal == forced[None, :, None]).astype(jnp.int32).reshape(MB, IMAGES)
    longer = jnp.maximum(coin_flips, chosen)
    return jnp.where(longer == 1, SLOTS, SHORT).astype(jnp.int32)


def level_of(rng, dims, pieces, least, top_value):
    level, own = 1.0, jax.random.fold_in(rng, 6)
    for dim, blocks in pieces:
        steps = jnp.exp(jax.random.uniform(jax.random.fold_in(own, dim), (blocks,), jnp.float32, least / len(pieces), top_value / len(pieces)))
        level = level * jnp.repeat(steps, dims[dim] // blocks).reshape([-1 if axis == dim else 1 for axis in range(len(dims))])
    return level


def assign_block(stream_key, own, number, rows, number_of, top, reach, slope):
    order = jax.random.permutation(stream_key, number_of)
    heavy_load, ordinary = portions_of(number_of, rows * top, reach, slope, True), portions_of(number_of, rows * top, reach, slope, False)
    places = jnp.arange(number_of)

    def named(lengths, rotation):
        used = int((lengths > 0).sum())
        fixed = max(1, used // 4)
        passed = fixed + (places - fixed + rotation * (used - fixed)) % max(1, number_of - fixed)
        return jnp.zeros((number_of,), jnp.int32).at[order[jnp.where(places < fixed, places, passed)]].set(jnp.asarray(lengths, jnp.int32))

    lengths = jnp.where(number % 4 == 0, named(heavy_load, number // 4), named(ordinary, number - number // 4 - 1))
    mixed = jax.random.permutation(jax.random.fold_in(own, 3), number_of)
    source_of, taker = mixed[0:number_of // 2 * 2:2], mixed[1:number_of // 2 * 2:2]
    margin = jnp.minimum(lengths[source_of] - 1, reach - lengths[taker]) // 2
    margin = jnp.where((source_of == order[0]) | (taker == order[0]) | (lengths[taker] == 0), 0, jnp.maximum(margin, 0))
    passed = jax.random.randint(jax.random.fold_in(own, 4), (number_of // 2,), 0, 1 << 20) % (margin + 1)
    lengths = lengths.at[source_of].add(-passed).at[taker].add(passed)
    members = jnp.searchsorted(jnp.cumsum(lengths), jnp.arange(rows * top), side="right").astype(jnp.int32)
    grid = members.reshape(top, rows).T
    grid = grid[jax.random.permutation(jax.random.fold_in(own, 1), rows)]
    rotation = jax.random.randint(jax.random.fold_in(own, 2), (rows, 1), 0, top)
    return jnp.take_along_axis(grid, (jnp.arange(top)[None, :] + rotation) % top, axis=1)


def portions_of(count, total, bound, lean, full):
    portions = [(1 << 20) // math.isqrt(grade ** lean) + 1 for grade in range(1, count + 1)]
    largest = bound if full else min(bound, max(-(-total // count), total * portions[0] // sum(portions)))
    least = 1 if total - largest >= count - 1 else 0
    counts, surplus = [largest] + [least] * (count - 1), total - largest - least * (count - 1)
    while surplus > 0:
        movable = [i for i in range(1, count) if counts[i] < largest] or [i for i in range(1, count) if counts[i] < bound]
        pool, remaining = sum([portions[i] for i in movable]), surplus
        for i in movable:
            addition = min(bound - counts[i], max(1, remaining * portions[i] // pool), surplus)
            counts[i] = counts[i] + addition
            surplus = surplus - addition
    return np.array(counts)


def bell_draw(rng, extent, deviation, most, cuts=(), kind=jnp.bfloat16):
    values = jax.random.normal(rng, extent, jnp.float32) * deviation
    if len(cuts) > 0:
        values = level_of(rng, extent, cuts, -0.22, 0.18) * values
    return jnp.clip(values, min=-most, max=most).astype(kind)


def setup_inputs(seed: int = 0) -> dict:
    arg_keys = jax.random.split(jax.random.key(seed), 17)
    tokens = bell_draw(arg_keys[0], (MB, IMAGES, SLOTS, D), 1.0, 6.0, ((1, 32), (2, 4)))
    patch_counts = draw_patch_counts(jax.random.fold_in(arg_keys[16], 71), 0)
    attn_routes_keys = jax.random.split(jax.random.fold_in(arg_keys[2], 1), MB * IMAGES * SLOTS // SQ)
    attn_routes_turns = jax.random.permutation(jax.random.fold_in(arg_keys[2], 3), MB * IMAGES * SLOTS // SQ)
    attn_routes = jax.vmap(lambda own, number: assign_block(jax.random.fold_in(arg_keys[2], 2), own, number, SQ, EXPERTS, TOP, CAP, 1))(attn_routes_keys, attn_routes_turns).reshape((MB, IMAGES, SLOTS, TOP))
    mlp_routes_keys = jax.random.split(jax.random.fold_in(arg_keys[3], 1), MB * IMAGES * SLOTS // SQ)
    mlp_routes_turns = jax.random.permutation(jax.random.fold_in(arg_keys[3], 3), MB * IMAGES * SLOTS // SQ)
    mlp_routes = jax.vmap(lambda own, number: assign_block(jax.random.fold_in(arg_keys[3], 2), own, number, SQ, EXPERTS, TOP, CAP, 2))(mlp_routes_keys, mlp_routes_turns).reshape((MB, IMAGES, SLOTS, TOP))
    norm1_gain = jnp.clip(1.0 + 0.1 * jax.random.normal(arg_keys[4], (D,), jnp.float32), 0.5, 1.5).astype(jnp.bfloat16)
    norm1_bias = bell_draw(arg_keys[5], (D,), 0.2, 1.1953125, ((0, 128),))
    norm2_gain = jnp.clip(1.0 + 0.1 * jax.random.normal(arg_keys[6], (D,), jnp.float32), 0.5, 1.5).astype(jnp.bfloat16)
    norm2_bias = bell_draw(arg_keys[7], (D,), 0.2, 1.1953125, ((0, 128),))
    key_value_weight = bell_draw(arg_keys[8], (D, 2 * ATT), D ** -0.5, 0.3125, ((0, 128),))
    attn_router = bell_draw(arg_keys[9], (D, EXPERTS), (4 * D) ** -0.5, 0.15625, ((0, 128),))
    mlp_router = bell_draw(arg_keys[10], (D, EXPERTS), (4 * D) ** -0.5, 0.15625, ((0, 128),))
    query_weight = bell_draw(arg_keys[11], (EXPERTS, D, ATT), D ** -0.5, 0.3125, ((0, 4), (1, 32)))
    output_weight = bell_draw(arg_keys[12], (EXPERTS, ATT, D), (max(1, ATT // 64)) ** -0.5, 2.5, ((0, 4), (1, 32)))
    up_weight = bell_draw(arg_keys[13], (EXPERTS, D, FF), D ** -0.5, 0.3125, ((0, 4), (1, 32)))
    down_weight = bell_draw(arg_keys[14], (EXPERTS, FF, D), FF ** -0.5, 0.15625, ((0, 4), (1, 32)))
    cotangent = bell_draw(arg_keys[15], (MB, IMAGES, SLOTS, D), 1.0, 6.0, ((1, 32), (2, 4)))
    return dict(tokens=tokens, patch_counts=patch_counts, attn_routes=attn_routes, mlp_routes=mlp_routes, norm1_gain=norm1_gain, norm1_bias=norm1_bias, norm2_gain=norm2_gain, norm2_bias=norm2_bias, key_value_weight=key_value_weight, attn_router=attn_router, mlp_router=mlp_router, query_weight=query_weight, output_weight=output_weight, up_weight=up_weight, down_weight=down_weight, cotangent=cotangent)


@jax.custom_vjp
def low(v):
    return lax.optimization_barrier(v.astype(jnp.bfloat16)).astype(jnp.float32)

@jax.custom_vjp
def low_back(v):
    return v

def low_keep(v):
    return (low(v), None)

def low_pass(kept, grad):
    return (grad,)

def back_keep(v):
    return (v, None)

def back_low(kept, grad):
    return (low(grad),)
low.defvjp(low_keep, low_pass)
low_back.defvjp(back_keep, back_low)
EPSILON = 1e-06
PRECISE = lax.Precision.HIGHEST
MASKED = -1e+30

def normalize(values, gain_row, bias_row):
    average = lax.optimization_barrier(jnp.mean(values, -1, keepdims=True))
    centered = values - average
    variance = lax.optimization_barrier(jnp.mean(centered * centered, -1, keepdims=True))
    return centered * lax.rsqrt(variance + EPSILON) * gain_row + bias_row

def choose(logits, routes):
    one_hot = (routes[..., None] == jnp.arange(EXPERTS, dtype=jnp.int32)).astype(jnp.float32)
    chosen = lax.optimization_barrier(jnp.sum(one_hot * logits[:, None, :], -1))
    return jax.nn.softmax(chosen, -1)

def destinations(routes, capacity):
    flat_routes = routes.reshape(-1)
    one_hot = (flat_routes[:, None] == jnp.arange(EXPERTS, dtype=jnp.int32)[None, :]).astype(jnp.int32)
    position = lax.optimization_barrier(jnp.sum((jnp.cumsum(one_hot, 0) - 1) * one_hot, 1)).astype(jnp.int32)
    return (flat_routes * capacity + position).astype(jnp.int32)

def dispatch(values, target, capacity):
    copies = low_back(jnp.broadcast_to(values[:, None, :], (SLOTS, TOP, D))).reshape(SLOTS * TOP, D)
    buffer = jnp.zeros((EXPERTS * capacity, D), jnp.float32).at[target].set(copies)
    return buffer.reshape(EXPERTS, capacity, D)

def image_layer(weights, image_data):
    gain_one, bias_one, gain_two, bias_two, kv_weight, router_attn, router_mlp, query_w, output_w, up_w, down_w = weights
    inputs, length, routes_attn, routes_mlp = image_data
    capacity = N_EXP * CAP
    attn_in = low(normalize(inputs, gain_one, bias_one))
    key_values = low(low_back(jnp.dot(attn_in, kv_weight, precision=PRECISE)))
    keys_all = key_values[:, :ATT].reshape(SLOTS, HEADS, HEAD_DIM)
    values_all = key_values[:, ATT:].reshape(SLOTS, HEADS, HEAD_DIM)
    gates_attn = choose(jnp.dot(attn_in, router_attn, precision=PRECISE), routes_attn)
    target_attn = destinations(routes_attn, capacity)
    rows_attn = dispatch(attn_in, target_attn, capacity)
    queries = low(low_back(jnp.einsum('ecd,edf->ecf', rows_attn, query_w, precision=PRECISE)))
    queries = queries.reshape(EXPERTS, capacity, HEADS, HEAD_DIM)
    scores = low_back(jnp.einsum('echd,jhd->ehcj', queries, keys_all, precision=PRECISE) * HEAD_DIM ** (-0.5))
    visible = jnp.arange(SLOTS, dtype=jnp.int32) < length
    probs_low = low(jax.nn.softmax(jnp.where(visible, scores, MASKED), -1))
    attended = low(low_back(jnp.einsum('ehcj,jhd->echd', probs_low, values_all, precision=PRECISE)))
    attended = attended.reshape(EXPERTS, capacity, ATT)
    branch_attn = low(low_back(jnp.einsum('ecf,efd->ecd', attended, output_w, precision=PRECISE)))
    branch_attn = branch_attn.reshape(EXPERTS * capacity, D)
    mixed = inputs + lax.optimization_barrier(jnp.sum(gates_attn[..., None] * branch_attn[target_attn].reshape(SLOTS, TOP, D), 1))
    mlp_in = low(normalize(mixed, gain_two, bias_two))
    gates_mlp = choose(jnp.dot(mlp_in, router_mlp, precision=PRECISE), routes_mlp)
    target_mlp = destinations(routes_mlp, capacity)
    rows_mlp = dispatch(mlp_in, target_mlp, capacity)
    hidden_pre = low_back(jnp.einsum('ecd,edf->ecf', rows_mlp, up_w, precision=PRECISE))
    hidden = low(jax.nn.gelu(hidden_pre, approximate=False))
    branch_mlp = low(low_back(jnp.einsum('ecf,efd->ecd', hidden, down_w, precision=PRECISE)))
    branch_mlp = branch_mlp.reshape(EXPERTS * capacity, D)
    return mixed + lax.optimization_barrier(jnp.sum(gates_mlp[..., None] * branch_mlp[target_mlp].reshape(SLOTS, TOP, D), 1))

def reference(tokens, patch_counts, attn_routes, mlp_routes, norm1_gain, norm1_bias, norm2_gain, norm2_bias, key_value_weight, attn_router, mlp_router, query_weight, output_weight, up_weight, down_weight, cotangent):
    weights = tuple((member.astype(jnp.float32) for member in (norm1_gain, norm1_bias, norm2_gain, norm2_bias, key_value_weight, attn_router, mlp_router, query_weight, output_weight, up_weight, down_weight)))
    images_all = MB * IMAGES
    inputs = tokens.astype(jnp.float32).reshape(images_all, SLOTS, D)
    extras = (patch_counts.reshape(images_all), attn_routes.reshape(images_all, SLOTS, TOP), mlp_routes.reshape(images_all, SLOTS, TOP))
    layer_step = jax.checkpoint(image_layer)

    def forward(layer_inputs, layer_weights):
        return lax.map(lambda image_data: layer_step(layer_weights, image_data), (layer_inputs,) + extras)
    result, pullback = jax.vjp(forward, inputs, weights)
    input_grad, weight_grads = pullback(cotangent.astype(jnp.float32).reshape(images_all, SLOTS, D))
    shape_out = (MB, IMAGES, SLOTS, D)
    return (result.reshape(shape_out).astype(jnp.bfloat16), input_grad.reshape(shape_out).astype(jnp.bfloat16), weight_grads[0], weight_grads[1], weight_grads[2], weight_grads[3], weight_grads[4], weight_grads[5], weight_grads[6], weight_grads[7], weight_grads[8], weight_grads[9], weight_grads[10])
```

```python
import jax
import jax.numpy as jnp
from jax import lax
from jax.experimental import pallas as pl
from jax.experimental.pallas import tpu as pltpu
from jax.sharding import Mesh, PartitionSpec as P

BF = jnp.bfloat16
F32 = jnp.float32
EPSILON = 1e-06
MASKED = -1e30
MB, NX, SQ, SLOTS, D = 2, 4, 144, 576, 384
EXP, CAP, HEADS, FF = 3, 256, 6, 1536
PACK = 160
TOKS = ("z", "y", "c")
VMEM = 62 * 1024 * 1024


def params(n):
    return pltpu.CompilerParams(
        dimension_semantics=("arbitrary",) * n, vmem_limit_bytes=VMEM
    )


def dot(a, b):
    return jnp.dot(a, b, preferred_element_type=F32)


def dot_nt(a, b):
    return lax.dot_general(a, b, (((1,), (1,)), ((), ())), preferred_element_type=F32)


def dot_tn(a, b):
    return lax.dot_general(a, b, (((0,), (0,)), ((), ())), preferred_element_type=F32)


def iota(shape, dim):
    return lax.broadcasted_iota(jnp.int32, shape, dim)


def hot(cond):
    return jnp.where(cond, 1.0, 0.0).astype(BF)


def eye(n):
    return hot(iota((n, n), 0) == iota((n, n), 1))


def flip(a):
    return dot_nt(eye(a.shape[1]), a)


def tok_of(place, sc):
    z = (sc[2] + (place & 3)) & 3
    y = (sc[3] + ((place >> 2) & 3)) & 3
    c = (sc[1] + (place >> 4)) & 1
    return z * 8 + y * 2 + c


def third(v):
    return (v * 11) >> 5


def padded_feature(col, sc):
    r = col & 15
    feature = tok_of(col >> 4, sc) * 12 + r
    return jnp.where(r < 12, feature, -1)


def canonical_feature(col):
    r = col & 15
    return jnp.where(r < 12, (col >> 4) * 12 + r, -1)


def native_lane(sc):
    j = iota((1, 128), 1)
    n = j + 3 * sc[0]
    n = jnp.where(n >= 12, n - 12, n)
    return jnp.where(j < 12, n, -1)


def router_turn(sc, offset):
    n = native_lane(sc)
    return hot((iota((128, 128), 0) == n + offset) & (n >= 0))


def norm_parts(x):
    mu = jnp.mean(x, -1, keepdims=True)
    c = x - mu
    var = jnp.mean(c * c, -1, keepdims=True)
    inv = lax.rsqrt(var + EPSILON)
    return c * inv, inv


def norm_back(grad, normed, inv, gain):
    u = grad * gain
    a = jnp.mean(u, -1, keepdims=True)
    b = jnp.mean(u * normed, -1, keepdims=True)
    return (u - a - normed * b) * inv


def routing(rcol, first, x, router, sc):
    nat = native_lane(sc).astype(F32)
    member = jnp.zeros((SLOTS, 128), F32)
    for k in range(4):
        member = member + jnp.where(rcol[:, first + k : first + k + 1] == nat, 1.0, 0.0)
    inside = member > 0.5
    logits = jnp.where(inside, dot(x, router), MASKED)
    top = jnp.max(logits, -1, keepdims=True)
    ex = jnp.where(inside, jnp.exp(logits - top), 0.0)
    gates = ex / jnp.sum(ex, -1, keepdims=True)
    mb = member.astype(BF)
    lower = hot(iota((SLOTS, SLOTS), 1) < iota((SLOTS, SLOTS), 0))
    mt = dot_nt(hot(iota((16, 128), 0) == iota((16, 128), 1)), mb)
    posc = jnp.where(inside, dot(lower, mb), -1.0)
    posr = jnp.where(mt > 0.5, dot_nt(mt.astype(BF), lower), -1.0)
    return gates, posc, posr


def route_columns(refs, m):
    unit = hot(iota((SQ, 256), 0) == iota((SQ, 256), 1))
    return jnp.concatenate([dot_nt(unit, r[m, SQ:PACK, 0:256]) for r in refs], 0)


def gate_lanes(gates):
    hi = gates.astype(BF).astype(F32)
    lo = pltpu.roll(gates - hi, 64, 1)
    return jnp.where(iota(gates.shape, 1) < 64, hi, lo).astype(BF)


def pick(ext, e):
    lane = iota(ext.shape, 1)
    return jnp.sum(jnp.where((lane == e) | (lane == 64 + e), ext, 0.0), -1, keepdims=True)


def split_lanes(col, e):
    hi = col.astype(BF).astype(F32)
    lane = iota((col.shape[0], 128), 1)
    both = jnp.where(lane == e, hi, 0.0) + jnp.where(lane == 64 + e, col - hi, 0.0)
    return both.astype(BF)


def gather_matrix(row):
    return hot(row == iota((CAP, SLOTS), 0).astype(F32))


def scatter_matrix(posc, e):
    col = jnp.sum(jnp.where(iota(posc.shape, 1) == e, posc, 0.0), -1, keepdims=True)
    return hot(col == iota((SLOTS, CAP), 1).astype(F32))


def router_grad(gates, lanes):
    t = lanes + pltpu.roll(lanes, 64, 1)
    inner = jnp.sum(gates * t, -1, keepdims=True)
    return (gates * (t - inner)).astype(BF)


def smem():
    return pl.BlockSpec(memory_space=pltpu.SMEM)


def full(shape):
    return pl.BlockSpec(shape, lambda *_: (0,) * len(shape))


def sds(shape, dtype):
    return jax.ShapeDtypeStruct(shape, dtype)


def prep_kernel(sc, w0, w1, wq, wo, wkv, wkvt, sm, vec):
    col = iota((1, 512), 1)
    take = hot(iota((D, 512), 0) == padded_feature(col, sc))
    for e in range(EXP):
        rows = jnp.concatenate(
            [w[:, 16 * e : 16 * e + 16, 0:768].reshape(256, 768) for w in (w0, w1)], 0
        )
        nat = dot(take, rows).astype(BF)
        wq[e] = nat[:, :D]
        wo[e] = nat[:, D:]
    k = iota((1, 1536), 1)
    place = (k * 1366) >> 16
    r48 = k - place * 48
    base = tok_of(place, sc) * 12

    def feature(idx, ok):
        s = third(idx)
        return jnp.where(ok, base + ((sc[0] + s) & 3) * 3 + idx - 3 * s, -1)

    r16 = r48 & 15
    kv_feature = feature((r48 >> 4) * 4 + r16 - 12, r16 >= 12)
    sm_feature = feature(r48, r48 < 12)
    everything = jnp.concatenate([w[...].reshape(768, 896) for w in (w0, w1)], 0)
    d = iota((D, 1536), 0)
    kv = dot(hot(d == kv_feature), everything[:, :768]).astype(BF)
    wkv[...] = kv
    wkvt[...] = flip(kv).astype(BF)
    small = dot(hot(d == sm_feature), everything[:, 768:]).astype(BF)
    sm[...] = small
    vec[...] = dot_nt(hot(iota((8, 128), 1) == iota((8, 128), 0) + 24), small)


def prep(sc, w0, w1):
    return pl.pallas_call(
        prep_kernel,
        grid=(1,),
        in_specs=[smem(), full((16, 48, 896)), full((16, 48, 896))],
        out_specs=[
            full((EXP, D, D)),
            full((EXP, D, D)),
            full((D, 768)),
            full((768, D)),
            full((D, 128)),
            full((8, D)),
        ],
        out_shape=[
            sds((EXP, D, D), BF),
            sds((EXP, D, D), BF),
            sds((D, 768), BF),
            sds((768, D), BF),
            sds((D, 128), BF),
            sds((8, D), F32),
        ],
        compiler_params=params(1),
        name="prep",
    )(sc, w0, w1)


def attend_kernel(
    sc, t0, t1, t2, t3, wq, wo, wkv, wkvt, sm, vec,
    o0, o1, o2, o3, xo, kvo, kto, gateo, poso, posco, rowso, qo, atto, bro, grow, pro,
    xe, acc,
):
    m, e = pl.program_id(0), pl.program_id(1)
    toks = (t0, t1, t2, t3)

    @pl.when(e == 0)
    def _():
        x = jnp.concatenate([t[0, 0:SQ, :].astype(F32) for t in toks], 0)
        n, _ = norm_parts(x)
        a = (n * vec[0:1, :] + vec[1:2, :]).astype(BF)
        xo[0] = a
        router = dot(sm[...], router_turn(sc, 0)).astype(BF)
        gates, posc, posr = routing(route_columns(toks, 0), 0, a, router, sc)
        gateo[0] = gates
        posco[0] = posc
        poso[0] = posr
        xe[:, 0:D] = a
        xe[:, D:512] = gate_lanes(gates)
        kvo[0] = dot(a, wkv[...]).astype(BF)
        kto[0] = dot_nt(wkvt[...], a).astype(BF)
        acc[...] = jnp.zeros_like(acc)

    g = gather_matrix(poso[0, pl.ds(e, 1), :])
    ext = dot(g, xe[...])
    rows = ext[:, 0:D].astype(BF)
    gate = pick(ext[:, D:512], e)
    rowso[0, 0] = rows
    grow[0, 0] = jnp.broadcast_to(gate, (CAP, 128))
    q = dot(rows, wq[0]).astype(BF)
    qo[0, 0] = q
    qs = q * jnp.asarray(0.125, BF)
    slot = iota((1, SLOTS), 1) + SQ * sc[0]
    slot = jnp.where(slot >= SLOTS, slot - SLOTS, slot)
    bias = jnp.where(slot < sc[4 + m], 0.0, MASKED)
    half = iota((CAP, 128), 1) < 64
    zero = jnp.zeros((CAP, 128), BF)
    for hp in range(3):
        span = slice(128 * hp, 128 * hp + 128)
        qp = qs[:, span]
        kt = kto[0, 128 * hp : 128 * hp + 128, :]
        v = kvo[0, :, D + 128 * hp : D + 128 * hp + 128]
        outs = []
        for side in range(2):
            mine = half if side == 0 else ~half
            s = dot(jnp.where(mine, qp, zero), kt) + bias
            ex = jnp.exp(s - jnp.max(s, -1, keepdims=True))
            p = (ex * (1.0 / jnp.sum(ex, -1, keepdims=True))).astype(BF)
            pro[0, 0, 2 * hp + side] = p
            outs.append(dot(p, v))
        atto[0, 0, :, span] = jnp.where(half, outs[0], outs[1]).astype(BF)
    br = dot(atto[0, 0], wo[0]).astype(BF)
    bro[0, 0] = br
    acc[...] += dot(scatter_matrix(posco[0], e), (gate * br.astype(F32)).astype(BF))

    @pl.when(e == EXP - 1)
    def _():
        for s, o in enumerate((o0, o1, o2, o3)):
            o[0] = acc[SQ * s : SQ * s + SQ, :].astype(BF)


def per_m(*shape):
    return pl.BlockSpec((1,) + shape, lambda m, e: (m,) + (0,) * len(shape))


def per_me(*shape):
    return pl.BlockSpec((1, 1) + shape, lambda m, e: (m, e) + (0,) * len(shape))


def per_e(*shape):
    return pl.BlockSpec((1,) + shape, lambda m, e: (e,) + (0,) * len(shape))


def attend(sc, toks, weights):
    saved = [
        (per_m(SLOTS, D), sds((MB, SLOTS, D), BF)),
        (per_m(SLOTS, 768), sds((MB, SLOTS, 768), BF)),
        (per_m(768, SLOTS), sds((MB, 768, SLOTS), BF)),
        (per_m(SLOTS, 128), sds((MB, SLOTS, 128), F32)),
        (per_m(16, SLOTS), sds((MB, 16, SLOTS), F32)),
        (per_m(SLOTS, 128), sds((MB, SLOTS, 128), F32)),
        (per_me(CAP, D), sds((MB, EXP, CAP, D), BF)),
        (per_me(CAP, D), sds((MB, EXP, CAP, D), BF)),
        (per_me(CAP, D), sds((MB, EXP, CAP, D), BF)),
        (per_me(CAP, D), sds((MB, EXP, CAP, D), BF)),
        (per_me(CAP, 128), sds((MB, EXP, CAP, 128), F32)),
        (per_me(HEADS, CAP, SLOTS), sds((MB, EXP, HEADS, CAP, SLOTS), BF)),
    ]
    piece = [(per_m(SQ, D), sds((MB, SQ, D), BF))] * 4
    out = pl.pallas_call(
        attend_kernel,
        grid=(MB, EXP),
        in_specs=[smem()]
        + [per_m(PACK, D)] * 4
        + [per_e(D, D), per_e(D, D), full((D, 768)), full((768, D)), full((D, 128)), full((8, D))],
        out_specs=[p[0] for p in piece + saved],
        out_shape=[p[1] for p in piece + saved],
        scratch_shapes=[pltpu.VMEM((SLOTS, 512), BF), pltpu.VMEM((SLOTS, D), F32)],
        compiler_params=params(2),
        name="attend",
    )(sc, *toks, *weights)
    return out[:4], out[4:]


def mix_kernel(t, p0, p1, p2, p3, vec, mixed, mlp_in):
    for m in range(MB):
        x = t[m].astype(F32)
        for p in (p0, p1, p2, p3):
            x = x + p[m].astype(F32)
        mixed[m] = x
        n, _ = norm_parts(x)
        mlp_in[m] = (n * vec[2:3, :] + vec[3:4, :]).astype(BF)


def mix(tokens, parts, vec):
    shape = (MB, SQ, D)
    return pl.pallas_call(
        mix_kernel,
        grid=(1,),
        in_specs=[full(shape)] * 5 + [full((8, D))],
        out_specs=[full(shape)] * 2,
        out_shape=[sds(shape, F32), sds(shape, BF)],
        compiler_params=params(1),
        name="mix",
    )(tokens, *parts, vec)


def gelu_both(v):
    a = jnp.abs(v)
    t = 1.0 / (1.0 + (0.3275911 * 0.7071067811865476) * a)
    ex = jnp.exp(-0.5 * (v * v))
    poly = 0.5 * 1.061405429
    for c in (-1.453152027, 1.421413741, -0.284496736, 0.254829592):
        poly = poly * t + 0.5 * c
    tail = poly * t * ex
    phi = jnp.where(v < 0, tail, 1.0 - tail)
    return v * phi, phi + v * (ex * 0.3989422804014327)


FC = 256


def experts_kernel(
    sc, x0, x1, x2, x3, g0, g1, g2, g3, t0, t1, t2, t3, sm, up, down,
    oo0, oo1, oo2, oo3, og0, og1, og2, og3, rmlp, rowso, gbo, hido, gpo,
    xe, gin, gates, posr, posc, acco, accg,
):
    e = pl.program_id(0)
    router = None

    @pl.when(e == 0)
    def _():
        turn = dot(sm[...], router_turn(sc, 12)).astype(BF)
        pad = hot(iota((D, 512), 0) == canonical_feature(iota((1, 512), 1)))
        for m in range(MB):
            a = jnp.concatenate([x[m] for x in (x0, x1, x2, x3)], 0)
            gt, pc, pr = routing(route_columns((t0, t1, t2, t3), m), 4, a, turn, sc)
            gates[m] = gt
            posc[m] = pc
            posr[m] = pr
            xe[m, :, 0:512] = dot(a, pad).astype(BF)
            xe[m, :, 512:640] = gate_lanes(gt)
            gin[m] = jnp.concatenate([g[m] for g in (g0, g1, g2, g3)], 0)
        acco[...] = jnp.zeros_like(acco)
        accg[...] = jnp.zeros_like(accg)

    exts, grs = [], []
    for m in range(MB):
        g = gather_matrix(posr[m, pl.ds(e, 1), :])
        exts.append(dot(g, xe[m]))
        grs.append(dot(g, gin[m]))
    ext = jnp.concatenate(exts, 0)
    gr = jnp.concatenate(grs, 0)
    rows = ext[:, 0:512].astype(BF)
    gate = pick(ext[:, 512:640], e)
    gb = (gate * gr).astype(BF)
    rowso[0] = rows
    gbo[0] = gb
    branch = jnp.zeros((512, D), F32)
    back = jnp.zeros((512, 512), F32)
    for c in range(FF // FC):
        span = slice(c * FC, c * FC + FC)
        w = up[:, :, span].reshape(512, FC)
        wd = down[...].reshape(FF, D)[span, :]
        act, slope = gelu_both(dot(rows, w))
        hid = act.astype(BF)
        gp = (dot_nt(gb, wd) * slope).astype(BF)
        hido[0, :, span] = hid
        gpo[0, :, span] = gp
        branch = branch + dot(hid, wd)
        back = back + dot_nt(gp, w)
    br = branch.astype(BF).astype(F32)
    t = jnp.sum(gr * br, -1, keepdims=True)
    scaled = (gate * br).astype(BF)
    lanes = split_lanes(t, e)
    backb = back.astype(BF)
    for m in range(MB):
        r = slice(CAP * m, CAP * m + CAP)
        sca = scatter_matrix(posc[m], e)
        acco[m] += dot(sca, jnp.concatenate([scaled[r], lanes[r]], 1))
        accg[m] += dot(sca, backb[r])

    @pl.when(e == EXP - 1)
    def _():
        turn = dot(sm[...], router_turn(sc, 12)).astype(BF)
        pad = hot(iota((D, 512), 0) == canonical_feature(iota((1, 512), 1)))
        total = jnp.zeros((D, 128), F32)
        for m in range(MB):
            dl = router_grad(gates[m], acco[m, :, D:512])
            a = jnp.concatenate([x[m] for x in (x0, x1, x2, x3)], 0)
            total = total + dot(flip(a).astype(BF), dl)
            part = dot_nt(accg[m].astype(BF), pad) + dot_nt(dl, turn)
            for s, (o, og) in enumerate(zip((oo0, oo1, oo2, oo3), (og0, og1, og2, og3))):
                r = slice(SQ * s, SQ * s + SQ)
                o[m] = acco[m, r, 0:D].astype(BF)
                og[m] = part[r].astype(BF)
        rmlp[...] = total


def experts(sc, xs, gs, toks, sm, wmlp):
    piece = (full((MB, SQ, D)), sds((MB, SQ, D), BF))

    def by_e(*shape):
        return pl.BlockSpec((1,) + shape, lambda e: (e,) + (0,) * len(shape))

    saved = [
        (full((D, 128)), sds((D, 128), F32)),
        (by_e(512, 512), sds((EXP, 512, 512), BF)),
        (by_e(512, D), sds((EXP, 512, D), BF)),
        (by_e(512, FF), sds((EXP, 512, FF), BF)),
        (by_e(512, FF), sds((EXP, 512, FF), BF)),
    ]
    outs = [piece] * 8 + saved
    got = pl.pallas_call(
        experts_kernel,
        grid=(EXP,),
        in_specs=[smem()]
        + [full((MB, SQ, D))] * 8
        + [full((MB, PACK, D))] * 4
        + [
            full((D, 128)),
            pl.BlockSpec((32, 16, FF), lambda e: (0, e, 0)),
            pl.BlockSpec((32, 48, D), lambda e: (0, 0, 4 + e)),
        ],
        out_specs=[o[0] for o in outs],
        out_shape=[o[1] for o in outs],
        scratch_shapes=[
            pltpu.VMEM((MB, SLOTS, 640), BF),
            pltpu.VMEM((MB, SLOTS, D), BF),
            pltpu.VMEM((MB, SLOTS, 128), F32),
            pltpu.VMEM((MB, 16, SLOTS), F32),
            pltpu.VMEM((MB, SLOTS, 128), F32),
            pltpu.VMEM((MB, SLOTS, 512), F32),
            pltpu.VMEM((MB, SLOTS, 512), F32),
        ],
        compiler_params=params(1),
        name="experts",
    )(sc, *xs, *gs, *toks, sm, wmlp, wmlp)
    return got[:4], got[4:8], got[8], got[9:]


def expert_grads_kernel(rows, gb, hid, gp, out):
    e = pl.program_id(0)
    du = dot_tn(rows[0], gp[0]).astype(BF)
    out[:, pl.ds(pl.multiple_of(16 * e, 16), 16), 0:FF] = du.reshape(32, 16, FF)
    dd = dot_tn(hid[0], gb[0]).astype(BF)
    out[:, :, pl.ds(pl.multiple_of(FF + D * e, 128), D)] = dd.reshape(32, 48, D)


def expert_grads(saved):
    def by_e(*shape):
        return pl.BlockSpec((1,) + shape, lambda e: (e,) + (0,) * len(shape))

    return pl.pallas_call(
        expert_grads_kernel,
        grid=(EXP,),
        in_specs=[by_e(512, 512), by_e(512, D), by_e(512, FF), by_e(512, FF)],
        out_specs=full((32, 48, 2688)),
        out_shape=sds((32, 48, 2688), BF),
        compiler_params=params(1),
        name="expert_grads",
    )(*saved)


def turn_kernel(mixed, cot, p0, p1, p2, p3, vec, gmix, gmixb, gv):
    rows = [jnp.zeros((1, D), F32)] * 2
    for m in range(MB):
        n, inv = norm_parts(mixed[m])
        grad = jnp.zeros((SQ, D), F32)
        for p in (p0, p1, p2, p3):
            grad = grad + p[m].astype(F32)
        gm = cot[m].astype(F32) + norm_back(grad, n, inv, vec[2:3, :])
        gmix[m] = gm
        gmixb[m] = gm.astype(BF)
        rows[0] = rows[0] + jnp.sum(grad * n, 0, keepdims=True)
        rows[1] = rows[1] + jnp.sum(grad, 0, keepdims=True)
    gv[...] = jnp.concatenate(rows + [jnp.zeros((6, D), F32)], 0)


def turn(mixed, cot, parts, vec):
    shape = (MB, SQ, D)
    return pl.pallas_call(
        turn_kernel,
        grid=(1,),
        in_specs=[full(shape)] * 6 + [full((8, D))],
        out_specs=[full(shape), full(shape), full((8, D))],
        out_shape=[sds(shape, F32), sds(shape, BF), sds((8, D), F32)],
        compiler_params=params(1),
        name="turn",
    )(mixed, cot, *parts, vec)


def attend_back_kernel(
    sc, g0, g1, g2, g3, t0, t1, t2, t3, x, kv, kt, gates, posr, posc, rows, q, att, br, grow, pro,
    wq, wo, wkvt, sm, vec, gv, rmlp,
    o0, o1, o2, o3, kvs, dqo0, dqo1,
    gin, acc, dkvt, dwq, dwo, dwkvt, dsm, dvec,
):
    m, e = pl.program_id(0), pl.program_id(1)

    @pl.when((m == 0) & (e == 0))
    def _():
        dwq[...] = jnp.zeros_like(dwq)
        dwo[...] = jnp.zeros_like(dwo)
        dwkvt[...] = jnp.zeros_like(dwkvt)
        dsm[...] = jnp.zeros_like(dsm)
        dvec[...] = jnp.zeros_like(dvec)

    @pl.when(e == 0)
    def _():
        gin[...] = jnp.concatenate([g[0] for g in (g0, g1, g2, g3)], 0)
        acc[...] = jnp.zeros_like(acc)
        dkvt[...] = jnp.zeros_like(dkvt)

    gr = dot(gather_matrix(posr[0, pl.ds(e, 1), :]), gin[...])
    gb = (grow[0, 0][:, 0:1] * gr).astype(BF)
    t = jnp.sum(gr * br[0, 0].astype(F32), -1, keepdims=True)
    dwo[e] += dot_tn(att[0, 0], gb)
    ga = dot_nt(gb, wo[0]).astype(BF)
    gat = flip(ga).astype(BF)
    qt = flip(q[0, 0] * jnp.asarray(0.125, BF)).astype(BF)
    half = iota((CAP, 128), 1) < 64
    zero = jnp.zeros((CAP, 128), BF)
    dqs = []
    for hp in range(3):
        span = slice(128 * hp, 128 * hp + 128)
        vt = kt[0, D + 128 * hp : D + 128 * hp + 128, :]
        k = kv[0, :, span]
        gap = ga[:, span]
        inner = gap.astype(F32) * att[0, 0, :, span].astype(F32)
        outs = []
        for side in range(2):
            h = 2 * hp + side
            mine = half if side == 0 else ~half
            p = pro[0, 0, h]
            dp = dot(jnp.where(mine, gap, zero), vt)
            ri = jnp.sum(jnp.where(mine, inner, 0.0), -1, keepdims=True)
            ds = (p.astype(F32) * (dp - ri)).astype(BF)
            outs.append(dot(ds, k))
            hs = slice(64 * h, 64 * h + 64)
            dkvt[hs, :] += dot(qt[hs, :], ds)
            vs = slice(D + 64 * h, D + 64 * h + 64)
            dkvt[vs, :] += dot(gat[hs, :], p)
        dqs.append((jnp.where(half, outs[0], outs[1]) * 0.125).astype(BF))
    dq = jnp.concatenate(dqs, 1)
    dwq[e] += dot_tn(rows[0, 0], dq)
    back = dot_nt(dq, wq[0]).astype(BF)
    acc[...] += dot(scatter_matrix(posc[0], e), jnp.concatenate([back, split_lanes(t, e)], 1))

    @pl.when(e == EXP - 1)
    def _():
        dl = router_grad(gates[0], acc[:, D:512])
        router = dot(sm[...], router_turn(sc, 0)).astype(BF)
        dkvb = dkvt[...].astype(BF)
        part = acc[:, 0:D] + dot_nt(dl, router) + dot(flip(dkvb).astype(BF), wkvt[...])
        tk = jnp.concatenate([r[0, 0:SQ, :].astype(F32) for r in (t0, t1, t2, t3)], 0)
        n, _ = norm_parts(tk)
        dvec[0:1, :] += jnp.sum(part * n, 0, keepdims=True)
        dvec[1:2, :] += jnp.sum(part, 0, keepdims=True)
        dsm[...] += dot(flip(x[0]).astype(BF), dl)
        dwkvt[...] += dot(dkvb, x[0])
        for s, o in enumerate((o0, o1, o2, o3)):
            o[0] = part[SQ * s : SQ * s + SQ].astype(BF)

    @pl.when((m == MB - 1) & (e == EXP - 1))
    def _():
        small = dot_nt(dsm[...].astype(BF), router_turn(sc, 0))
        small = small + dot_nt(rmlp[...].astype(BF), router_turn(sc, 12))
        vecs = jnp.concatenate(
            [jnp.zeros((24, D), F32), dvec[0:2, :], gv[0:2, :], jnp.zeros((100, D), F32)], 0
        ).astype(BF)
        small = (small + dot_nt(eye(D), vecs)).astype(BF)
        k = iota((D, 1), 0)
        s = (k >= 96).astype(jnp.int32) + (k >= 192).astype(jnp.int32) + (k >= 288).astype(jnp.int32)
        j = k - 96 * s
        place = (j * 171) >> 9
        feature = tok_of(place, sc) * 12 + ((sc[0] + s) & 3) * 3 + j - 3 * place
        perm = hot(feature == iota((D, D), 1))
        both = jnp.concatenate([dot_nt(perm, dwkvt[...].astype(BF)), dot(perm, small)], 1)
        kvs[...] = both.astype(BF).reshape(4, 96, 896)
        back_pad = hot(padded_feature(iota((512, 1), 0), sc) == iota((512, D), 1))
        for i in range(EXP):
            both = jnp.concatenate([dwq[i], dwo[i]], 1).astype(BF)
            wide = dot(back_pad, both).astype(BF).reshape(32, 16, 768)
            dqo0[:, 16 * i : 16 * i + 16, :] = wide[0:16]
            dqo1[:, 16 * i : 16 * i + 16, :] = wide[16:32]


def attend_back(sc, gs, toks, saved, wq, wo, wkvt, sm, vec, gv, rmlp):
    piece = [(per_m(SQ, D), sds((MB, SQ, D), BF))] * 4
    outs = piece + [
        (full((4, 96, 896)), sds((4, 96, 896), BF)),
        (full((16, 48, 768)), sds((16, 48, 768), BF)),
        (full((16, 48, 768)), sds((16, 48, 768), BF)),
    ]
    got = pl.pallas_call(
        attend_back_kernel,
        grid=(MB, EXP),
        in_specs=[smem()]
        + [per_m(SQ, D)] * 4
        + [per_m(PACK, D)] * 4
        + [
            per_m(SLOTS, D), per_m(SLOTS, 768), per_m(768, SLOTS), per_m(SLOTS, 128),
            per_m(16, SLOTS), per_m(SLOTS, 128), per_me(CAP, D), per_me(CAP, D), per_me(CAP, D),
            per_me(CAP, D), per_me(CAP, 128), per_me(HEADS, CAP, SLOTS),
            per_e(D, D), per_e(D, D), full((768, D)), full((D, 128)), full((8, D)), full((8, D)),
            full((D, 128)),
        ],
        out_specs=[o[0] for o in outs],
        out_shape=[o[1] for o in outs],
        scratch_shapes=[
            pltpu.VMEM((SLOTS, D), BF),
            pltpu.VMEM((SLOTS, 512), F32),
            pltpu.VMEM((768, SLOTS), F32),
            pltpu.VMEM((EXP, D, D), F32),
            pltpu.VMEM((EXP, D, D), F32),
            pltpu.VMEM((768, D), F32),
            pltpu.VMEM((D, 128), F32),
            pltpu.VMEM((8, D), F32),
        ],
        compiler_params=params(2),
        name="attend_back",
    )(sc, *gs, *toks, *saved, wq, wo, wkvt, sm, vec, gv, rmlp)
    return got[:4], got[4], got[5], got[6]


def finish_kernel(gmix, tokens, p0, p1, p2, p3, vec, out):
    for m in range(MB):
        n, inv = norm_parts(tokens[m].astype(F32))
        grad = jnp.zeros((SQ, D), F32)
        for p in (p0, p1, p2, p3):
            grad = grad + p[m].astype(F32)
        out[m] = (gmix[m] + norm_back(grad, n, inv, vec[0:1, :])).astype(BF)


def finish(gmix, tokens, parts, vec):
    shape = (MB, SQ, D)
    return pl.pallas_call(
        finish_kernel,
        grid=(1,),
        in_specs=[full(shape)] * 6 + [full((8, D))],
        out_specs=full(shape),
        out_shape=sds(shape, BF),
        compiler_params=params(1),
        name="finish",
    )(gmix, tokens, *parts, vec)


def place_kernel(k0, k1, k2, k3, d0, d1, o0, o1):
    total = jnp.zeros((96, 896), F32)
    for k in (k0, k1, k2, k3):
        total = total + k[...].astype(F32)
    total = total.astype(BF)
    for half, (d, o) in enumerate(((d0, o0), (d1, o1))):
        mine = total[48 * half : 48 * half + 48]
        row = iota((768, 1), 0)
        place = (row * 1366) >> 16
        r = row - 48 * place
        col = iota((768, 48), 1)
        kv = hot((col == place * 3 + r - 12) & (r >= 12) & (r < 15))
        sm = hot((col == place * 3 + r - 28) & (r >= 28) & (r < 31))
        wide = dot(kv, mine[:, 0:768])
        small = dot(sm, mine[:, 768:896])
        both = jnp.concatenate([wide[:, 0:128] + small, wide[:, 128:]], 1).reshape(16, 48, 768)
        o[...] = (both + d[...].astype(F32)).astype(BF)


def place(pieces, d0, d1):
    return pl.pallas_call(
        place_kernel,
        grid=(1,),
        in_specs=[full((96, 896))] * 4 + [full((16, 48, 768))] * 2,
        out_specs=[full((16, 48, 768))] * 2,
        out_shape=[sds((16, 48, 768), BF)] * 2,
        compiler_params=params(1),
        name="place",
    )(*pieces, d0, d1)


def shift(a, axis, s):
    n = lax.axis_size(axis)
    return lax.ppermute(a, axis, [(i, (i + s) % n) for i in range(n)])


def fetch(a, axis):
    n = lax.axis_size(axis)
    return [a] + [shift(a, axis, n - s) for s in range(1, n)]


def send(parts, axis):
    return [parts[0]] + [shift(parts[s], axis, s) for s in range(1, len(parts))]


def local(
    tokens, patch_counts, attn_routes, mlp_routes, gain1, bias1, gain2, bias2, wkv, rattn, rmlp,
    wq, wo, wup, wdown, cotangent,
):
    tokens = tokens.reshape(MB, SQ, D)
    cot = cotangent.reshape(MB, SQ, D)
    index = [lax.axis_index(a) for a in ("x", "c", "z", "y")]
    sc = jnp.stack(index + [patch_counts[0, 0], patch_counts[1, 0], 0, 0]).astype(jnp.int32)

    mlp_shard = jnp.concatenate(
        [
            jnp.pad(wup, ((0, 0), (0, 4), (0, 0))).reshape(48, FF),
            jnp.moveaxis(wdown, 0, 1).reshape(48, EXP * D),
        ],
        1,
    )
    wmlp = lax.all_gather(mlp_shard, TOKS, axis=0).reshape(32, 48, 2688)

    routes = jnp.concatenate([attn_routes, mlp_routes], -1).reshape(MB, SQ, 8)
    routes = jnp.moveaxis(routes, 1, 2).astype(BF)
    packed = jnp.concatenate([tokens, jnp.pad(routes, ((0, 0), (0, 8), (0, D - SQ)))], 1)
    vecs = jnp.stack([gain1, bias1, gain2, bias2], 1)
    shared = jnp.concatenate(
        [wkv, rattn, rmlp, vecs, jnp.zeros((3, 100), BF)], 1
    )
    kv12 = jnp.concatenate(fetch(shared, "x"), 0)
    toks = fetch(packed, "x")
    qo = jnp.concatenate([wq, wo], -1)
    qo = jnp.concatenate([qo, kv12[:, :768].reshape(3, 4, 768)], 1).reshape(48, 768)
    side = jnp.pad(kv12[:, 768:], ((0, 36), (0, 0)))
    shard = jnp.concatenate([qo, side], 1)
    zs = jnp.stack(fetch(shard, "z"))
    w0 = jnp.stack(fetch(zs, "y")).reshape(16, 48, 896)
    w1 = shift(w0, "c", 1)
    fq, fo, fkv, fkvt, sm, vec = prep(sc, w0, w1)

    parts, saved = attend(sc, toks, (fq, fo, fkv, fkvt, sm, vec))
    gs = fetch(cot, "x")
    mixed, mlp_in = mix(tokens, send(parts, "x"), vec)
    xs = fetch(mlp_in, "x")
    outp, gradp, rm, kept = experts(sc, xs, gs, toks, sm, wmlp)
    gradp = send(gradp, "x")
    outp = send(outp, "x")
    dmlp = expert_grads(kept)
    dmlp = lax.psum_scatter(dmlp, TOKS, scatter_dimension=0, tiled=True).reshape(48, 2688)
    gmix, gmixb, gv = turn(mixed, cot, gradp, vec)
    result = mixed
    for o in outp:
        result = result + o.astype(F32)
    result = result.astype(BF)
    gms = fetch(gmixb, "x")
    back, kvs, d0, d1 = attend_back(sc, gms, toks, saved, fq, fo, fkvt, sm, vec, gv, rm)
    kvp = send([kvs[s] for s in range(4)], "x")
    tokens_grad = finish(gmix, tokens, send(back, "x"), vec)
    e0, e1 = place(kvp, d0, d1)
    other = shift(e1, "c", 1)
    h = (e0.astype(F32) + other.astype(F32)).astype(BF).reshape(4, 4, 48, 768)
    h = sum(p.astype(F32) for p in send([h[s] for s in range(4)], "y")).astype(BF)
    tail = sum(p.astype(F32) for p in send([h[s] for s in range(4)], "z"))

    t3 = tail.reshape(3, 16, 768)
    small = tail[28:31]
    mlp = dmlp.astype(F32)
    dup = mlp[:, :FF].reshape(3, 16, FF)[:, :12]
    ddown = jnp.moveaxis(mlp[:, FF:].reshape(48, EXP, D), 1, 0)
    shape = (MB, 1, SQ, D)
    return (
        result.reshape(shape),
        tokens_grad.reshape(shape),
        small[:, 24],
        small[:, 25],
        small[:, 26],
        small[:, 27],
        tail[12:15],
        small[:, 0:12],
        small[:, 12:24],
        t3[:, :12, :D],
        t3[:, :12, D:],
        dup,
        ddown,
    )


def solution(mesh):
    fine = Mesh(mesh.devices.reshape(4, 4, 2, 4), ("z", "y", "c", "x"))
    every = TOKS + ("x",)
    act = P(None, TOKS, "x", None)
    row, mat, own = P(every), P(every, None), P("x", TOKS, None)
    return jax.shard_map(
        local,
        mesh=fine,
        in_specs=(
            act, P(None, TOKS), act, act, row, row, row, row, mat, mat, mat, own, own, own, own, act,
        ),
        out_specs=(act, act, row, row, row, row, mat, mat, mat, own, own, own, own),
        check_vma=False,
    )
```

```python
import jax
import jax.numpy as jnp
from jax import lax
from jax.experimental import pallas as pl
from jax.experimental.pallas import tpu as pltpu
from jax.sharding import Mesh, PartitionSpec as P

BF = jnp.bfloat16
F32 = jnp.float32
EPSILON = 1e-06
MASKED = -1e30
MB, NX, SQ, SLOTS, D = 2, 4, 144, 576, 384
EXP, CAP, HEADS, FF = 3, 256, 6, 1536
PACK = 160
TOKS = ("z", "y", "c")
VMEM = 62 * 1024 * 1024


def params(n, mib=60):
    return pltpu.CompilerParams(
        dimension_semantics=("arbitrary",) * n, vmem_limit_bytes=mib * 1024 * 1024
    )


def cost(us):
    return pl.CostEstimate(flops=int(us * 1e9), bytes_accessed=0, transcendentals=0)


def dot(a, b):
    return jnp.dot(a, b, preferred_element_type=F32)


def dot_nt(a, b):
    return lax.dot_general(a, b, (((1,), (1,)), ((), ())), preferred_element_type=F32)


def dot_tn(a, b):
    return lax.dot_general(a, b, (((0,), (0,)), ((), ())), preferred_element_type=F32)


def iota(shape, dim):
    return lax.broadcasted_iota(jnp.int32, shape, dim)


def hot(cond):
    return jnp.where(cond, 1.0, 0.0).astype(BF)


def eye(n):
    return hot(iota((n, n), 0) == iota((n, n), 1))


def flip(a):
    return dot_nt(eye(a.shape[1]), a)


def tok_of(place, sc, plain=False):
    c = (sc[1] + (place >> 4)) & 1
    if plain:
        return (place & 15) * 2 + c
    z = (sc[2] + (place & 3)) & 3
    y = (sc[3] + ((place >> 2) & 3)) & 3
    return z * 8 + y * 2 + c


def third(v):
    return (v * 11) >> 5


def owned_feature(k, sc, plain=False):
    r = k & 15
    return jnp.where(r < 12, tok_of(k >> 4, sc, plain) * 12 + r, -1)


def shared_feature(place, idx, valid, sc, plain=False):
    s = third(idx)
    feature = tok_of(place, sc, plain) * 12 + ((sc[0] + s) & 3) * 3 + idx - 3 * s
    return jnp.where(valid, feature, -1)


def canonical_feature(col):
    r = col & 15
    return jnp.where(r < 12, (col >> 4) * 12 + r, -1)


def native_lane(sc):
    j = iota((1, 128), 1)
    n = j + 3 * sc[0]
    n = jnp.where(n >= 12, n - 12, n)
    return jnp.where(j < 12, n, -1)


def router_turn(sc, offset):
    n = native_lane(sc)
    return hot((iota((128, 128), 0) == n + offset) & (n >= 0))


def norm_parts(x):
    mu = jnp.mean(x, -1, keepdims=True)
    c = x - mu
    var = jnp.mean(c * c, -1, keepdims=True)
    inv = lax.rsqrt(var + EPSILON)
    return c * inv, inv


def norm_back(grad, normed, inv, gain):
    u = grad * gain
    a = jnp.mean(u, -1, keepdims=True)
    b = jnp.mean(u * normed, -1, keepdims=True)
    return (u - a - normed * b) * inv


def routing(rcol, first, x, router, sc):
    nat = native_lane(sc).astype(F32)
    member = jnp.zeros((SLOTS, 128), F32)
    for k in range(4):
        member = member + jnp.where(rcol[:, first + k : first + k + 1] == nat, 1.0, 0.0)
    inside = member > 0.5
    logits = jnp.where(inside, dot(x, router), MASKED)
    top = jnp.max(logits, -1, keepdims=True)
    ex = jnp.where(inside, jnp.exp(logits - top), 0.0)
    gates = ex / jnp.sum(ex, -1, keepdims=True)
    mb = member.astype(BF)
    lower = hot(iota((SLOTS, SLOTS), 1) < iota((SLOTS, SLOTS), 0))
    mt = dot_nt(hot(iota((16, 128), 0) == iota((16, 128), 1)), mb)
    posc = jnp.where(inside, dot(lower, mb), -1.0)
    posr = jnp.where(mt > 0.5, dot_nt(mt.astype(BF), lower), -1.0)
    return gates, posc, posr


def route_columns(refs, m):
    unit = hot(iota((SQ, 256), 0) == iota((SQ, 256), 1))
    return jnp.concatenate([dot_nt(unit, r[m, SQ:PACK, 0:256]) for r in refs], 0)


def gate_lanes(gates):
    hi = gates.astype(BF).astype(F32)
    lo = pltpu.roll(gates - hi, 64, 1)
    return jnp.where(iota(gates.shape, 1) < 64, hi, lo).astype(BF)


def pick(ext, e):
    lane = iota(ext.shape, 1)
    return jnp.sum(jnp.where((lane == e) | (lane == 64 + e), ext, 0.0), -1, keepdims=True)


def split_lanes(col, e):
    hi = col.astype(BF).astype(F32)
    lane = iota((col.shape[0], 128), 1)
    both = jnp.where(lane == e, hi, 0.0) + jnp.where(lane == 64 + e, col - hi, 0.0)
    return both.astype(BF)


def gather_matrix(row):
    return hot(row == iota((CAP, SLOTS), 0).astype(F32))


def scatter_matrix(posc, e):
    col = jnp.sum(jnp.where(iota(posc.shape, 1) == e, posc, 0.0), -1, keepdims=True)
    return hot(col == iota((SLOTS, CAP), 1).astype(F32))


def router_grad(gates, lanes):
    t = lanes + pltpu.roll(lanes, 64, 1)
    inner = jnp.sum(gates * t, -1, keepdims=True)
    return (gates * (t - inner)).astype(BF)


def smem():
    return pl.BlockSpec(memory_space=pltpu.SMEM)


def full(shape):
    return pl.BlockSpec(shape, lambda *_: (0,) * len(shape))


def sds(shape, dtype):
    return jax.ShapeDtypeStruct(shape, dtype)


def pack_kernel(wkv, rattn, rmlp, vecs, wq, wo, wup, wdown, shared, own, mlp):
    shared[...] = jnp.zeros_like(shared)
    own[...] = jnp.zeros_like(own)
    mlp[...] = jnp.zeros_like(mlp)
    shared[0:3, 0:768] = wkv[...]
    shared[0:3, 768:780] = rattn[...]
    shared[0:3, 780:792] = rmlp[...]
    lane, row = iota((3, 12), 1), iota((3, 12), 0)
    v = vecs[...].astype(F32)
    cols = [
        jnp.sum(jnp.where(lane == 3 * i + row, v, 0.0), -1, keepdims=True) for i in range(4)
    ]
    shared[0:3, 792:796] = jnp.concatenate(cols, 1).astype(BF)
    for e in range(EXP):
        own[e, 0:12, 0:D] = wq[e]
        own[e, 0:12, D : 2 * D] = wo[e]
        for g in range(4):
            mlp[e, 16 * g : 16 * g + 12, :] = wup[e, :, D * g : D * g + D]
        mlp[e, 64:112, :] = wdown[e]


def pack(wkv, rattn, rmlp, vecs, wq, wo, wup, wdown):
    shapes = [(16, 896), (EXP, 16, 768), (EXP, 112, D)]
    args = (wkv, rattn, rmlp, vecs, wq, wo, wup, wdown)
    return pl.pallas_call(
        pack_kernel,
        grid=(1,),
        in_specs=[full(v.shape) for v in args],
        out_specs=[full(v) for v in shapes],
        out_shape=[sds(v, BF) for v in shapes],
        compiler_params=params(1, 62),
        cost_estimate=cost(2),
        name="pack",
    )(*args)


def prep_kernel(sc, a0, a1, wq, wo, wkv, wkvt, sm, vec):
    take = hot(iota((D, 512), 0) == owned_feature(iota((1, 512), 1), sc))
    for e in range(EXP):
        rows = jnp.concatenate(
            [a[:, 16 * e : 16 * e + 16, 0:768].reshape(256, 768) for a in (a0, a1)], 0
        )
        nat = dot(take, rows).astype(BF)
        wq[e] = nat[:, :D]
        wo[e] = nat[:, D:]
    k = iota((1, 1536), 1)
    place = (k * 1366) >> 16
    r48 = k - place * 48
    r16 = r48 & 15
    d = iota((D, 1536), 0)
    kv_feature = shared_feature(place, (r48 >> 4) * 4 + r16 - 12, r16 >= 12, sc)
    everything = jnp.concatenate([a[:, :, 0:768].reshape(768, 768) for a in (a0, a1)], 0)
    kv = dot(hot(d == kv_feature), everything).astype(BF)
    wkv[...] = kv
    wkvt[...] = kv.T
    side = jnp.concatenate([a[:, 0:16, 768:].reshape(256, 128) for a in (a0, a1)], 0)
    k = iota((1, 512), 1)
    sm_feature = shared_feature(k >> 4, k & 15, (k & 15) < 12, sc)
    small = dot(hot(iota((D, 512), 0) == sm_feature), side).astype(BF)
    sm[...] = small
    vec[...] = dot_nt(hot(iota((8, 128), 1) == iota((8, 128), 0) + 24), small)


def prep(sc, a0, a1):
    return pl.pallas_call(
        prep_kernel,
        grid=(1,),
        in_specs=[smem()] + [full((16, 48, 896))] * 2,
        out_specs=[
            full((EXP, D, D)),
            full((EXP, D, D)),
            full((D, 768)),
            full((768, D)),
            full((D, 128)),
            full((8, D)),
        ],
        out_shape=[
            sds((EXP, D, D), BF),
            sds((EXP, D, D), BF),
            sds((D, 768), BF),
            sds((768, D), BF),
            sds((D, 128), BF),
            sds((8, D), F32),
        ],
        compiler_params=params(1, 62),
        cost_estimate=cost(5),
        name="prep",
    )(sc, a0, a1)


ROWS = EXP * CAP


def gather_all(posr):
    return jnp.concatenate([gather_matrix(posr[e : e + 1, :]) for e in range(EXP)], 0)


def scatter_all(posc):
    return jnp.concatenate([scatter_matrix(posc, e) for e in range(EXP)], 1)


def by_expert(f):
    return jnp.concatenate([f(e, slice(CAP * e, CAP * e + CAP)) for e in range(EXP)], 0)


def own_half(rows, side):
    lane = iota((rows, 128), 1)
    return lane < 64 if side == 0 else lane >= 64


def spare(side):
    return 64 if side == 0 else 0


def with_ones(v, side):
    lane, at = iota(v.shape, 1), spare(side)
    ones = jnp.where((lane == at) | (lane == at + 1), 1.0, 0.0)
    return jnp.where(own_half(v.shape[0], side), v.astype(F32), ones).astype(BF)


def attend_kernel(
    sc, t0, t1, t2, t3, wq, wo, wkv, sm, vec,
    o0, o1, o2, o3, xo, kvo, gateo, poso, posco, rowso, qo, atto, bro, grow, rin, exo,
):
    m = pl.program_id(0)
    toks = (t0, t1, t2, t3)
    x = jnp.concatenate([t[0, 0:SQ, :].astype(F32) for t in toks], 0)
    n, _ = norm_parts(x)
    a = (n * vec[0:1, :] + vec[1:2, :]).astype(BF)
    xo[0] = a
    router = dot(sm[...], router_turn(sc, 0)).astype(BF)
    gates, posc, posr = routing(route_columns(toks, 0), 0, a, router, sc)
    gateo[0] = gates
    posco[0] = posc
    poso[0] = posr
    kv = dot(a, wkv[...]).astype(BF)
    kvo[0] = kv

    ext = dot(gather_all(posr), jnp.concatenate([a, gate_lanes(gates)], 1))
    rows = ext[:, 0:D].astype(BF)
    gate = by_expert(lambda e, r: pick(ext[r, D:512], e))
    rowso[0] = rows
    grow[0] = jnp.broadcast_to(gate, (ROWS, 128))
    q = by_expert(lambda e, r: dot(rows[r], wq[e])).astype(BF)
    q = q * jnp.asarray(0.125, BF)
    qo[0] = q
    slot = iota((SLOTS, 1), 0) + SQ * sc[0]
    slot = jnp.where(slot >= SLOTS, slot - SLOTS, slot)
    bias = jnp.where(slot < sc[4 + m], 0.0, MASKED)
    lane = iota((ROWS, 128), 1)
    inv_lanes = jnp.zeros((ROWS, 128), F32)
    for hp in range(3):
        span = slice(128 * hp, 128 * hp + 128)
        halves = []
        for side in range(2):
            h = 2 * hp + side
            at = spare(side)
            ka = jnp.where(own_half(SLOTS, side), kv[:, span].astype(F32), jnp.where(iota((SLOTS, 128), 1) == at, bias, 0.0)).astype(BF)
            one = jnp.where(lane == at, 1.0, 0.0)
            qa = jnp.where(own_half(ROWS, side), q[:, span].astype(F32), one).astype(BF)
            va = with_ones(kv[:, D + 128 * hp : D + 128 * hp + 128], side)
            s = dot_nt(qa, ka)
            ex = jnp.exp(s - jnp.max(s, -1, keepdims=True)).astype(BF)
            exo[0, h] = ex
            pv = dot(ex, va)
            inv = 1.0 / pv[:, at : at + 1]
            inv_lanes = jnp.where(lane == h, inv, inv_lanes)
            halves.append(pv * inv)
        atto[0, :, span] = jnp.where(lane < 64, halves[0], halves[1]).astype(BF)
    rin[0] = inv_lanes
    br = by_expert(lambda e, r: dot(atto[0, r, :], wo[e])).astype(BF)
    bro[0] = br
    acc = dot(scatter_all(posc), (gate * br.astype(F32)).astype(BF))
    for s, o in enumerate((o0, o1, o2, o3)):
        o[0] = acc[SQ * s : SQ * s + SQ, :].astype(BF)


def per_m(*shape):
    return pl.BlockSpec((1,) + shape, lambda m: (m,) + (0,) * len(shape))


def attend(sc, toks, weights):
    saved = [
        (SLOTS, D, BF),
        (SLOTS, 768, BF),
        (SLOTS, 128, F32),
        (16, SLOTS, F32),
        (SLOTS, 128, F32),
        (ROWS, D, BF),
        (ROWS, D, BF),
        (ROWS, D, BF),
        (ROWS, D, BF),
        (ROWS, 128, F32),
        (ROWS, 128, F32),
        (HEADS, ROWS, SLOTS, BF),
    ]
    outs = [(SQ, D, BF)] * 4 + saved
    out = pl.pallas_call(
        attend_kernel,
        grid=(MB,),
        in_specs=[smem()]
        + [per_m(PACK, D)] * 4
        + [full((EXP, D, D)), full((EXP, D, D)), full((D, 768)), full((D, 128)), full((8, D))],
        out_specs=[per_m(*o[:-1]) for o in outs],
        out_shape=[sds((MB,) + o[:-1], o[-1]) for o in outs],
        compiler_params=params(1, 62),
        cost_estimate=cost(24),
        name="attend",
    )(sc, *toks, *weights)
    return out[:4], out[4:]


def mix_kernel(t, p0, p1, p2, p3, vec, mixed, mlp_in):
    for m in range(MB):
        x = t[m].astype(F32)
        for p in (p0, p1, p2, p3):
            x = x + p[m].astype(F32)
        mixed[m] = x
        n, _ = norm_parts(x)
        mlp_in[m] = (n * vec[2:3, :] + vec[3:4, :]).astype(BF)


def mix(tokens, parts, vec):
    shape = (MB, SQ, D)
    return pl.pallas_call(
        mix_kernel,
        grid=(1,),
        in_specs=[full(shape)] * 5 + [full((8, D))],
        out_specs=[full(shape)] * 2,
        out_shape=[sds(shape, F32), sds(shape, BF)],
        compiler_params=params(1, 8),
        cost_estimate=cost(2),
        name="mix",
    )(tokens, *parts, vec)


def gelu_both(v):
    phi = 0.5 + 0.5 * lax.erf(v * 0.7071067811865476)
    density = jnp.exp(-0.5 * (v * v)) * 0.3989422804014327
    return v * phi, phi + v * density


FC = 768


def experts_kernel(
    sc, x0, x1, x2, x3, g0, g1, g2, g3, t0, t1, t2, t3, sm, w_ref,
    oo0, oo1, oo2, oo3, og0, og1, og2, og3, rmlp, rowso, gbo, hido, gpo,
    xe, gin, gates, posr, posc, acco, accg,
):
    e = pl.program_id(0)
    router = None

    @pl.when(e == 0)
    def _():
        turn = dot(sm[...], router_turn(sc, 12)).astype(BF)
        pad = hot(iota((D, 512), 0) == canonical_feature(iota((1, 512), 1)))
        for m in range(MB):
            a = jnp.concatenate([x[m] for x in (x0, x1, x2, x3)], 0)
            gt, pc, pr = routing(route_columns((t0, t1, t2, t3), m), 4, a, turn, sc)
            gates[m] = gt
            posc[m] = pc
            posr[m] = pr
            xe[m, :, 0:512] = dot(a, pad).astype(BF)
            xe[m, :, 512:640] = gate_lanes(gt)
            gin[m] = jnp.concatenate([g[m] for g in (g0, g1, g2, g3)], 0)
        acco[...] = jnp.zeros_like(acco)
        accg[...] = jnp.zeros_like(accg)

    exts, grs = [], []
    for m in range(MB):
        g = gather_matrix(posr[m, pl.ds(e, 1), :])
        exts.append(dot(g, xe[m]))
        grs.append(dot(g, gin[m]))
    ext = jnp.concatenate(exts, 0)
    gr = jnp.concatenate(grs, 0)
    rows = ext[:, 0:512].astype(BF)
    gate = pick(ext[:, 512:640], e)
    gb = (gate * gr).astype(BF)
    rowso[0] = rows
    gbo[0] = gb
    branch = jnp.zeros((512, D), F32)
    back = jnp.zeros((512, 512), F32)
    for c in range(FF // FC):
        span = slice(c * FC, c * FC + FC)
        w = jnp.concatenate(
            [w_ref[:, 0, 16 * g : 16 * g + 16, :].reshape(512, D) for g in (2 * c, 2 * c + 1)], 1
        )
        wd = w_ref[16 * c : 16 * c + 16, 0, 64:112, :].reshape(FC, D)
        act, slope = gelu_both(dot(rows, w))
        hid = act.astype(BF)
        gp = (dot_nt(gb, wd) * slope).astype(BF)
        hido[0, :, span] = hid
        gpo[0, :, span] = gp
        branch = branch + dot(hid, wd)
        back = back + dot_nt(gp, w)
    br = branch.astype(BF).astype(F32)
    t = jnp.sum(gr * br, -1, keepdims=True)
    scaled = (gate * br).astype(BF)
    lanes = split_lanes(t, e)
    backb = back.astype(BF)
    for m in range(MB):
        r = slice(CAP * m, CAP * m + CAP)
        sca = scatter_matrix(posc[m], e)
        acco[m] += dot(sca, jnp.concatenate([scaled[r], lanes[r]], 1))
        accg[m] += dot(sca, backb[r])

    @pl.when(e == EXP - 1)
    def _():
        turn = dot(sm[...], router_turn(sc, 12)).astype(BF)
        pad = hot(iota((D, 512), 0) == canonical_feature(iota((1, 512), 1)))
        total = jnp.zeros((D, 128), F32)
        for m in range(MB):
            dl = router_grad(gates[m], acco[m, :, D:512])
            a = jnp.concatenate([x[m] for x in (x0, x1, x2, x3)], 0)
            total = total + dot(flip(a).astype(BF), dl)
            part = dot_nt(accg[m].astype(BF), pad) + dot_nt(dl, turn)
            for s, (o, og) in enumerate(zip((oo0, oo1, oo2, oo3), (og0, og1, og2, og3))):
                r = slice(SQ * s, SQ * s + SQ)
                o[m] = acco[m, r, 0:D].astype(BF)
                og[m] = part[r].astype(BF)
        rmlp[...] = total


def experts(sc, xs, gs, toks, sm, wmlp):
    piece = (full((MB, SQ, D)), sds((MB, SQ, D), BF))

    def by_e(*shape):
        return pl.BlockSpec((1,) + shape, lambda e: (e,) + (0,) * len(shape))

    saved = [
        (full((D, 128)), sds((D, 128), F32)),
        (by_e(512, 512), sds((EXP, 512, 512), BF)),
        (by_e(512, D), sds((EXP, 512, D), BF)),
        (by_e(512, FF), sds((EXP, 512, FF), BF)),
        (by_e(512, FF), sds((EXP, 512, FF), BF)),
    ]
    outs = [piece] * 8 + saved
    got = pl.pallas_call(
        experts_kernel,
        grid=(EXP,),
        in_specs=[smem()]
        + [full((MB, SQ, D))] * 8
        + [full((MB, PACK, D))] * 4
        + [
            full((D, 128)),
            pl.BlockSpec((32, 1, 112, D), lambda e: (0, e, 0, 0)),
        ],
        out_specs=[o[0] for o in outs],
        out_shape=[o[1] for o in outs],
        scratch_shapes=[
            pltpu.VMEM((MB, SLOTS, 640), BF),
            pltpu.VMEM((MB, SLOTS, D), BF),
            pltpu.VMEM((MB, SLOTS, 128), F32),
            pltpu.VMEM((MB, 16, SLOTS), F32),
            pltpu.VMEM((MB, SLOTS, 128), F32),
            pltpu.VMEM((MB, SLOTS, 512), F32),
            pltpu.VMEM((MB, SLOTS, 512), F32),
        ],
        compiler_params=params(1, 62),
        cost_estimate=cost(26),
        name="experts",
    )(sc, *xs, *gs, *toks, sm, wmlp)
    return got[:4], got[4:8], got[8], got[9:]


def expert_grads_kernel(rows, gb, hid, gp, out):
    du = dot_tn(rows[0], gp[0]).astype(BF)
    for g in range(4):
        out[:, 0, 16 * g : 16 * g + 16, :] = du[:, D * g : D * g + D].reshape(32, 16, D)
    out[:, 0, 64:112, :] = dot_tn(hid[0], gb[0]).astype(BF).reshape(32, 48, D)


def expert_grads(saved):
    def by_e(*shape):
        return pl.BlockSpec((1,) + shape, lambda e: (e,) + (0,) * len(shape))

    return pl.pallas_call(
        expert_grads_kernel,
        grid=(EXP,),
        in_specs=[by_e(512, 512), by_e(512, D), by_e(512, FF), by_e(512, FF)],
        out_specs=pl.BlockSpec((32, 1, 112, D), lambda e: (0, e, 0, 0)),
        out_shape=sds((32, EXP, 112, D), BF),
        compiler_params=params(1, 62),
        cost_estimate=cost(11),
        name="expert_grads",
    )(*saved)


def turn_kernel(mixed, cot, p0, p1, p2, p3, vec, gmix, gmixb, gv):
    rows = [jnp.zeros((1, D), F32)] * 2
    for m in range(MB):
        n, inv = norm_parts(mixed[m])
        grad = jnp.zeros((SQ, D), F32)
        for p in (p0, p1, p2, p3):
            grad = grad + p[m].astype(F32)
        gm = cot[m].astype(F32) + norm_back(grad, n, inv, vec[2:3, :])
        gmix[m] = gm
        gmixb[m] = gm.astype(BF)
        rows[0] = rows[0] + jnp.sum(grad * n, 0, keepdims=True)
        rows[1] = rows[1] + jnp.sum(grad, 0, keepdims=True)
    gv[...] = jnp.concatenate(rows + [jnp.zeros((6, D), F32)], 0)


def turn(mixed, cot, parts, vec):
    shape = (MB, SQ, D)
    return pl.pallas_call(
        turn_kernel,
        grid=(1,),
        in_specs=[full(shape)] * 6 + [full((8, D))],
        out_specs=[full(shape), full(shape), full((8, D))],
        out_shape=[sds(shape, F32), sds(shape, BF), sds((8, D), F32)],
        compiler_params=params(1, 8),
        cost_estimate=cost(3),
        name="turn",
    )(mixed, cot, *parts, vec)


def attend_back_kernel(
    sc, g0, g1, g2, g3, t0, t1, t2, t3, x, kv, gates, posr, posc, rows, q, att, br, grow, rin, ex,
    wq, wo, wkvt, sm, vec, gv, rmlp,
    o0, o1, o2, o3, ta0, ta1,
    dkvt, dwq, dwo, dwkvt, dsm, dvec,
):
    m = pl.program_id(0)

    @pl.when(m == 0)
    def _():
        dwq[...] = jnp.zeros_like(dwq)
        dwo[...] = jnp.zeros_like(dwo)
        dwkvt[...] = jnp.zeros_like(dwkvt)
        dsm[...] = jnp.zeros_like(dsm)
        dvec[...] = jnp.zeros_like(dvec)

    gin = jnp.concatenate([g[0] for g in (g0, g1, g2, g3)], 0)
    gr = dot(gather_all(posr[0]), gin)
    gb = (grow[0][:, 0:1] * gr).astype(BF)
    t = jnp.sum(gr * br[0].astype(F32), -1, keepdims=True)
    ga = by_expert(lambda e, r: dot_nt(gb[r], wo[e])).astype(BF)
    for e in range(EXP):
        r = slice(CAP * e, CAP * e + CAP)
        dwo[:, D * e : D * e + D] += dot_tn(att[0, r, :], gb[r])
    lane = iota((ROWS, 128), 1)
    low = lane < 64
    dqs = []
    for hp in range(3):
        span = slice(128 * hp, 128 * hp + 128)
        inv = jnp.where(low, rin[0, :, 2 * hp : 2 * hp + 1], rin[0, :, 2 * hp + 1 : 2 * hp + 2])
        gap = ga[:, span].astype(F32) * inv
        inner = gap * att[0, :, span].astype(F32)
        gapt = flip(gap.astype(BF)).astype(BF)
        qt = flip(q[0, :, span]).astype(BF)
        outs = []
        for side in range(2):
            h = 2 * hp + side
            at = spare(side)
            own = own_half(ROWS, side)
            ri = jnp.sum(jnp.where(own, inner, 0.0), -1, keepdims=True)
            hi = ri.astype(BF).astype(F32)
            rest = jnp.where(lane == at, -hi, jnp.where(lane == at + 1, hi - ri, 0.0))
            gaa = jnp.where(own, gap, rest).astype(BF)
            va = with_ones(kv[0, :, D + 128 * hp : D + 128 * hp + 128], side)
            p = ex[0, h]
            ds = (p.astype(F32) * dot_nt(gaa, va)).astype(BF)
            outs.append(dot(ds, kv[0, :, span]))
            hs = slice(64 * side, 64 * side + 64)
            dkvt[64 * h : 64 * h + 64, :] = dot(qt[hs, :], ds)
            dkvt[D + 64 * h : D + 64 * h + 64, :] = dot(gapt[hs, :], p)
        dqs.append((jnp.where(low, outs[0], outs[1]) * 0.125).astype(BF))
    dq = jnp.concatenate(dqs, 1)
    for e in range(EXP):
        r = slice(CAP * e, CAP * e + CAP)
        dwq[:, D * e : D * e + D] += dot_tn(rows[0, r, :], dq[r])
    back = by_expert(lambda e, r: dot_nt(dq[r], wq[e])).astype(BF)
    lanes = by_expert(lambda e, r: split_lanes(t[r], e))
    acc = dot(scatter_all(posc[0]), jnp.concatenate([back, lanes], 1))

    dl = router_grad(gates[0], acc[:, D:512])
    router = dot(sm[...], router_turn(sc, 0)).astype(BF)
    dkvb = dkvt[...].astype(BF)
    part = acc[:, 0:D] + dot_nt(dl, router) + dot_tn(dkvb, wkvt[...])
    tk = jnp.concatenate([r[0, 0:SQ, :].astype(F32) for r in (t0, t1, t2, t3)], 0)
    n, _ = norm_parts(tk)
    dvec[0:1, :] += jnp.sum(part * n, 0, keepdims=True)
    dvec[1:2, :] += jnp.sum(part, 0, keepdims=True)
    dsm[...] += dot_tn(x[0], dl)
    dwkvt[...] += dot(dkvb, x[0])
    for s, o in enumerate((o0, o1, o2, o3)):
        o[0] = part[SQ * s : SQ * s + SQ].astype(BF)

    @pl.when(m == MB - 1)
    def _():
        small = dot_nt(dsm[...].astype(BF), router_turn(sc, 0))
        small = small + dot_nt(rmlp[...].astype(BF), router_turn(sc, 12))
        vecs = jnp.concatenate(
            [jnp.zeros((24, D), F32), dvec[0:2, :], gv[0:2, :], jnp.zeros((100, D), F32)], 0
        ).astype(BF)
        small = (small + dot_nt(eye(D), vecs)).astype(BF)
        k, d = iota((512, 1), 0), iota((512, D), 1)
        r = k & 15
        own = hot(owned_feature(k, sc, True) == d)
        kvb = flip(dwkvt[...].astype(BF)).astype(BF)
        for e in range(EXP):
            span = slice(D * e, D * e + D)
            shared = hot(shared_feature(k >> 4, 4 * e + r - 12, r >= 12, sc, True) == d)
            weights = jnp.concatenate([dwq[:, span], dwo[:, span]], 1).astype(BF)
            wide = dot(jnp.concatenate([own, shared], 1), jnp.concatenate([weights, kvb], 0))
            wide = wide.astype(BF)
            rows = slice(16 * e, 16 * e + 16)
            for i, t in enumerate((ta0, ta1)):
                t[:, rows, 0:768] = wide[256 * i : 256 * i + 256].reshape(16, 16, 768)
            if e == 0:
                side = dot(hot(shared_feature(k >> 4, r, r < 12, sc, True) == d), small).astype(BF)
            else:
                side = jnp.zeros((512, 128), BF)
            for i, t in enumerate((ta0, ta1)):
                t[:, rows, 768:896] = side[256 * i : 256 * i + 256].reshape(16, 16, 128)


def attend_back(sc, gs, toks, saved, wq, wo, wkvt, sm, vec, gv, rmlp):
    piece = [(per_m(SQ, D), sds((MB, SQ, D), BF))] * 4
    outs = piece + [
        (full((16, 48, 896)), sds((16, 48, 896), BF)),
        (full((16, 48, 896)), sds((16, 48, 896), BF)),
    ]
    got = pl.pallas_call(
        attend_back_kernel,
        grid=(MB,),
        in_specs=[smem()]
        + [per_m(SQ, D)] * 4
        + [per_m(PACK, D)] * 4
        + [per_m(*v.shape[1:]) for v in saved]
        + [
            full((EXP, D, D)), full((EXP, D, D)), full((768, D)), full((D, 128)), full((8, D)),
            full((8, D)), full((D, 128)),
        ],
        out_specs=[o[0] for o in outs],
        out_shape=[o[1] for o in outs],
        scratch_shapes=[
            pltpu.VMEM((768, SLOTS), F32),
            pltpu.VMEM((D, EXP * D), F32),
            pltpu.VMEM((D, EXP * D), F32),
            pltpu.VMEM((768, D), F32),
            pltpu.VMEM((D, 128), F32),
            pltpu.VMEM((8, D), F32),
        ],
        compiler_params=params(1, 62),
        cost_estimate=cost(120),
        name="attend_back",
    )(sc, *gs, *toks, *saved, wq, wo, wkvt, sm, vec, gv, rmlp)
    return got[:4], got[4:]


def finish_kernel(gmix, tokens, p0, p1, p2, p3, vec, out):
    for m in range(MB):
        n, inv = norm_parts(tokens[m].astype(F32))
        grad = jnp.zeros((SQ, D), F32)
        for p in (p0, p1, p2, p3):
            grad = grad + p[m].astype(F32)
        out[m] = (gmix[m] + norm_back(grad, n, inv, vec[0:1, :])).astype(BF)


def finish(gmix, tokens, parts, vec):
    shape = (MB, SQ, D)
    return pl.pallas_call(
        finish_kernel,
        grid=(1,),
        in_specs=[full(shape)] * 6 + [full((8, D))],
        out_specs=full(shape),
        out_shape=sds(shape, BF),
        compiler_params=params(1, 8),
        cost_estimate=cost(2),
        name="finish",
    )(gmix, tokens, *parts, vec)


def shift(a, axis, s):
    n = lax.axis_size(axis)
    return lax.ppermute(a, axis, [(i, (i + s) % n) for i in range(n)])


def fetch(a, axis):
    one, three, two = [shift(a, axis, 4 - s) for s in (1, 3, 2)]
    return [a, one, two, three]


def send(parts, axis):
    two, one, three = [shift(parts[s], axis, s) for s in (2, 1, 3)]
    return [parts[0], one, two, three]


def add2(a, b):
    return (a.astype(F32) + b.astype(F32)).astype(BF)


def tie(*arrays):
    return lax.optimization_barrier(arrays)


def fold(a, axis):
    got = send([a[s] for s in range(a.shape[0])], axis)
    return sum(v.astype(F32) for v in got)


def local(
    tokens, patch_counts, attn_routes, mlp_routes, gain1, bias1, gain2, bias2, wkv, rattn, rmlp,
    wq, wo, wup, wdown, cotangent,
):
    tokens = tokens.reshape(MB, SQ, D)
    cot = cotangent.reshape(MB, SQ, D)
    index = [lax.axis_index(a) for a in ("x", "c", "z", "y")]
    sc = jnp.stack(index + [patch_counts[0, 0], patch_counts[1, 0], 0, 0]).astype(jnp.int32)

    vecs = jnp.concatenate([gain1, bias1, gain2, bias2]).reshape(1, 12)
    shared, own, mlp_shard = pack(wkv, rattn, rmlp, vecs, wq, wo, wup, wdown)
    routes = jnp.concatenate([attn_routes, mlp_routes], -1).reshape(MB, SQ, 8)
    routes = jnp.moveaxis(routes, 1, 2).astype(BF)
    packed = jnp.concatenate([tokens, jnp.pad(routes, ((0, 0), (0, 8), (0, D - SQ)))], 1)
    kv12 = jnp.concatenate([v[0:3] for v in fetch(shared, "x")], 0)
    shard = jnp.concatenate([own[:, 0:12], kv12[:, :768].reshape(3, 4, 768)], 1).reshape(48, 768)
    shard = jnp.concatenate([shard, jnp.pad(kv12[:, 768:], ((0, 36), (0, 0)))], 1)
    zs = jnp.stack(fetch(shard, "z"))
    toks = fetch(packed, "x")
    a0 = jnp.stack(fetch(zs, "y")).reshape(16, 48, 896)
    a0, toks, mlp_shard = tie(a0, toks, mlp_shard)
    wmlp = lax.all_gather(mlp_shard, TOKS, axis=0).reshape(32, EXP, 112, D)
    fq, fo, fkv, fkvt, sm, vec = prep(sc, a0, shift(a0, "c", 1))

    gs = fetch(cot, "x")
    parts, saved = attend(sc, toks, (fq, fo, fkv, sm, vec))
    parts, gs = tie(parts, gs)
    mixed, mlp_in = mix(tokens, send(parts, "x"), vec)
    xs = fetch(mlp_in, "x")
    outp, gradp, rm, kept = experts(sc, xs, gs, toks, sm, wmlp)
    gradp = send(gradp, "x")
    dmlp = expert_grads(kept)
    gradp, dmlp = tie(gradp, dmlp)
    dmlp = lax.psum_scatter(dmlp, TOKS, scatter_dimension=0, tiled=True)
    gmix, gmixb, gv = turn(mixed, cot, gradp, vec)
    gms = fetch(gmixb, "x")
    back, (ta, ta1) = attend_back(sc, gms, toks, saved, fq, fo, fkvt, sm, vec, gv, rm)
    ta1 = shift(ta1, "c", 1)
    ta1, back, outp = tie(ta1, back, outp)
    ta = lax.all_to_all(add2(ta, ta1), ("z", "y"), 0, 0, tiled=True)
    ta = jnp.sum(ta.astype(F32), 0)
    back = send(back, "x")
    outp, back = tie(outp, back)
    tokens_grad = finish(gmix, tokens, back, vec)
    result = mixed
    for o in send(outp, "x"):
        result = result + o.astype(F32)
    result = result.astype(BF)
    t3 = ta.reshape(3, 16, 896)
    kv = jnp.concatenate([t3[:, 12:16, :768].reshape(12, 768), ta[0:12, 768:]], 1)
    small = fold(kv.astype(BF).reshape(4, 3, 896), "x")

    mlp = dmlp.astype(F32)
    mlp = mlp.reshape(EXP, 112, D)
    dup = mlp[:, 0:64].reshape(EXP, 4, 16, D)[:, :, 0:12]
    dup = jnp.moveaxis(dup, 1, 2).reshape(EXP, 12, FF)
    ddown = mlp[:, 64:112]
    dq, do = t3[:, :12, :D], t3[:, :12, D:768]
    shape = (MB, 1, SQ, D)
    return (
        result.reshape(shape),
        tokens_grad.reshape(shape),
        small[:, 792],
        small[:, 793],
        small[:, 794],
        small[:, 795],
        small[:, 0:768],
        small[:, 768:780],
        small[:, 780:792],
        dq,
        do,
        dup,
        ddown,
    )


def solution(mesh):
    fine = Mesh(mesh.devices.reshape(4, 4, 2, 4), ("z", "y", "c", "x"))
    every = TOKS + ("x",)
    act = P(None, TOKS, "x", None)
    row, mat, own = P(every), P(every, None), P("x", TOKS, None)
    return jax.shard_map(
        local,
        mesh=fine,
        in_specs=(
            act, P(None, TOKS), act, act, row, row, row, row, mat, mat, mat, own, own, own, own, act,
        ),
        out_specs=(act, act, row, row, row, row, mat, mat, mat, own, own, own, own),
        check_vma=False,
    )
```

```python
import jax
import jax.numpy as jnp
from jax import lax
from jax.experimental import pallas as pl
from jax.experimental.pallas import tpu as pltpu
from jax.sharding import Mesh, PartitionSpec as P

BF = jnp.bfloat16
F32 = jnp.float32
EPSILON = 1e-06
MASKED = -1e30
MB, NX, SQ, SLOTS, D = 2, 4, 144, 576, 384
EXP, CAP, HEADS, FF = 3, 256, 6, 1536
PACK = 160
TOKS = ("z", "y", "c")
VMEM = 62 * 1024 * 1024


def params(n, mib=60):
    return pltpu.CompilerParams(
        dimension_semantics=("arbitrary",) * n, vmem_limit_bytes=mib * 1024 * 1024
    )


def cost(us):
    return pl.CostEstimate(flops=int(us * 1e9), bytes_accessed=0, transcendentals=0)


def dot(a, b):
    return jnp.dot(a, b, preferred_element_type=F32)


def dot_nt(a, b):
    return lax.dot_general(a, b, (((1,), (1,)), ((), ())), preferred_element_type=F32)


def dot_tn(a, b):
    return lax.dot_general(a, b, (((0,), (0,)), ((), ())), preferred_element_type=F32)


def iota(shape, dim):
    return lax.broadcasted_iota(jnp.int32, shape, dim)


def hot(cond):
    return jnp.where(cond, 1.0, 0.0).astype(BF)


def eye(n):
    return hot(iota((n, n), 0) == iota((n, n), 1))


def flip(a):
    return dot_nt(eye(a.shape[1]), a)


def tok_of(place, sc, plain=False):
    c = (sc[1] + (place >> 4)) & 1
    if plain:
        return (place & 15) * 2 + c
    z = (sc[2] + (place & 3)) & 3
    y = (sc[3] + ((place >> 2) & 3)) & 3
    return z * 8 + y * 2 + c


def third(v):
    return (v * 11) >> 5


def owned_feature(k, sc, plain=False):
    r = k & 15
    return jnp.where(r < 12, tok_of(k >> 4, sc, plain) * 12 + r, -1)


def shared_feature(place, idx, valid, sc, plain=False):
    s = third(idx)
    feature = tok_of(place, sc, plain) * 12 + ((sc[0] + s) & 3) * 3 + idx - 3 * s
    return jnp.where(valid, feature, -1)


def canonical_feature(col):
    r = col & 15
    return jnp.where(r < 12, (col >> 4) * 12 + r, -1)


def native_lane(sc):
    j = iota((1, 128), 1)
    n = j + 3 * sc[0]
    n = jnp.where(n >= 12, n - 12, n)
    return jnp.where(j < 12, n, -1)


def router_turn(sc, offset):
    n = native_lane(sc)
    return hot((iota((128, 128), 0) == n + offset) & (n >= 0))


def norm_parts(x):
    mu = jnp.mean(x, -1, keepdims=True)
    c = x - mu
    var = jnp.mean(c * c, -1, keepdims=True)
    inv = lax.rsqrt(var + EPSILON)
    return c * inv, inv


def norm_back(grad, normed, inv, gain):
    u = grad * gain
    a = jnp.mean(u, -1, keepdims=True)
    b = jnp.mean(u * normed, -1, keepdims=True)
    return (u - a - normed * b) * inv


def soft_gates(posc, x, router):
    inside = posc >= 0.0
    logits = jnp.where(inside, dot(x, router), MASKED)
    top = jnp.max(logits, -1, keepdims=True)
    ex = jnp.where(inside, jnp.exp(logits - top), 0.0)
    return ex / jnp.sum(ex, -1, keepdims=True)


def gate_lanes(gates):
    hi = gates.astype(BF).astype(F32)
    lo = pltpu.roll(gates - hi, 64, 1)
    return jnp.where(iota(gates.shape, 1) < 64, hi, lo).astype(BF)


def pick(ext, e):
    lane = iota(ext.shape, 1)
    return jnp.sum(jnp.where((lane == e) | (lane == 64 + e), ext, 0.0), -1, keepdims=True)


def split_lanes(col, e):
    hi = col.astype(BF).astype(F32)
    lane = iota((col.shape[0], 128), 1)
    both = jnp.where(lane == e, hi, 0.0) + jnp.where(lane == 64 + e, col - hi, 0.0)
    return both.astype(BF)


def gather_matrix(row):
    return hot(row == iota((CAP, SLOTS), 0).astype(F32))


def scatter_matrix(posc, e):
    col = jnp.sum(jnp.where(iota(posc.shape, 1) == e, posc, 0.0), -1, keepdims=True)
    return hot(col == iota((SLOTS, CAP), 1).astype(F32))


def router_grad(gates, lanes):
    t = lanes + pltpu.roll(lanes, 64, 1)
    inner = jnp.sum(gates * t, -1, keepdims=True)
    return (gates * (t - inner)).astype(BF)


def smem():
    return pl.BlockSpec(memory_space=pltpu.SMEM)


def full(shape):
    return pl.BlockSpec(shape, lambda *_: (0,) * len(shape))


def sds(shape, dtype):
    return jax.ShapeDtypeStruct(shape, dtype)


def pack_kernel(
    wkv, rattn, rmlp, g1, b1, g2, b2, wq, wo, wup, wdown, ra, rm, shared, own, mlp
):
    shared[...] = jnp.zeros_like(shared)
    own[...] = jnp.zeros_like(own)
    mlp[...] = jnp.zeros_like(mlp)
    shared[0:3, 0:768] = wkv[...]
    shared[0:3, 768:780] = rattn[...]
    shared[0:3, 780:792] = rmlp[...]
    lane, row = iota((3, 3), 1), iota((3, 3), 0)
    cols = []
    for v in (g1, b1, g2, b2):
        line = v[...].astype(F32).reshape(1, 3)
        cols.append(jnp.sum(jnp.where(lane == row, line, 0.0), -1, keepdims=True))
    shared[0:3, 792:796] = jnp.concatenate(cols, 1).astype(BF)
    routes = jnp.zeros((16, SQ), F32)
    for m in range(MB):
        for i, r in enumerate((ra, rm)):
            put = hot(iota((16, 4), 0) == iota((16, 4), 1) + 8 * i + 4 * m)
            routes = routes + dot(put, r[m].astype(F32).astype(BF))
    shared[:, 1024 : 1024 + SQ] = routes.astype(BF)
    for e in range(EXP):
        own[e, 0:12, 0:D] = wq[e]
        own[e, 0:12, D : 2 * D] = wo[e]
        for g in range(4):
            mlp[e, 16 * g : 16 * g + 12, :] = wup[e, :, D * g : D * g + D]
        mlp[e, 64:112, :] = wdown[e]


def pack(*args):
    shapes = [(16, 1280), (EXP, 16, 768), (EXP, 112, D)]
    return pl.pallas_call(
        pack_kernel,
        grid=(1,),
        in_specs=[full(v.shape) for v in args],
        out_specs=[full(v) for v in shapes],
        out_shape=[sds(v, BF) for v in shapes],
        compiler_params=params(1, 62),
        cost_estimate=cost(2),
        name="pack",
    )(*args)


def plan_kernel(sc, r0, r1, r2, r3, posr, posc):
    unit = hot(iota((SQ, 256), 0) == iota((SQ, 256), 1))
    rcol = jnp.concatenate([dot_nt(unit, r[...]) for r in (r0, r1, r2, r3)], 0)
    nat = native_lane(sc).astype(F32)
    lower = hot(iota((SLOTS, SLOTS), 1) < iota((SLOTS, SLOTS), 0))
    unit = hot(iota((16, 128), 0) == iota((16, 128), 1))
    for i in range(2 * MB):
        member = jnp.zeros((SLOTS, 128), F32)
        for k in range(4 * i, 4 * i + 4):
            member = member + jnp.where(rcol[:, k : k + 1] == nat, 1.0, 0.0)
        mb = member.astype(BF)
        mt = dot_nt(unit, mb)
        posc[i // MB, i % MB] = jnp.where(member > 0.5, dot(lower, mb), -1.0)
        posr[i // MB, i % MB] = jnp.where(mt > 0.5, dot_nt(mt.astype(BF), lower), -1.0)


def plan(sc, pieces):
    return pl.pallas_call(
        plan_kernel,
        grid=(1,),
        in_specs=[smem()] + [pl.BlockSpec((16, 256), lambda i: (0, 4))] * 4,
        out_specs=[full((2, MB, 16, SLOTS)), full((2, MB, SLOTS, 128))],
        out_shape=[sds((2, MB, 16, SLOTS), F32), sds((2, MB, SLOTS, 128), F32)],
        compiler_params=params(1, 62),
        cost_estimate=cost(4),
        name="plan",
    )(sc, *pieces)


def prepare(sc, pieces, wq, wo, wkv, wkvt, sm, vec):
    def gathered(rows, lanes):
        return jnp.concatenate([p[:, rows, lanes].reshape(-1, lanes.stop - lanes.start) for p in pieces], 0)

    take = hot(iota((D, 512), 0) == owned_feature(iota((1, 512), 1), sc))
    for e in range(EXP):
        nat = dot(take, gathered(slice(16 * e, 16 * e + 16), slice(0, 768))).astype(BF)
        wq[e] = nat[:, :D]
        wo[e] = nat[:, D:]
    k = iota((1, 1536), 1)
    place = (k * 1366) >> 16
    r48 = k - place * 48
    r16 = r48 & 15
    kv_feature = shared_feature(place, (r48 >> 4) * 4 + r16 - 12, r16 >= 12, sc)
    kv = dot(hot(iota((D, 1536), 0) == kv_feature), gathered(slice(0, 48), slice(0, 768))).astype(BF)
    wkv[...] = kv
    wkvt[...] = kv.T
    k = iota((1, 512), 1)
    sm_feature = shared_feature(k >> 4, k & 15, (k & 15) < 12, sc)
    side = gathered(slice(0, 16), slice(768, 896))
    small = dot(hot(iota((D, 512), 0) == sm_feature), side).astype(BF)
    sm[...] = small
    vec[...] = dot_nt(hot(iota((8, 128), 1) == iota((8, 128), 0) + 24), small)


ROWS = EXP * CAP


def gather_all(posr):
    return jnp.concatenate([gather_matrix(posr[e : e + 1, :]) for e in range(EXP)], 0)


def scatter_all(posc):
    return jnp.concatenate([scatter_matrix(posc, e) for e in range(EXP)], 1)


def by_expert(f):
    return jnp.concatenate([f(e, slice(CAP * e, CAP * e + CAP)) for e in range(EXP)], 0)


def own_half(rows, side):
    lane = iota((rows, 128), 1)
    return lane < 64 if side == 0 else lane >= 64


def spare(side):
    return 64 if side == 0 else 0


def with_ones(v, side):
    lane, at = iota(v.shape, 1), spare(side)
    ones = jnp.where((lane == at) | (lane == at + 1), 1.0, 0.0)
    return jnp.where(own_half(v.shape[0], side), v.astype(F32), ones).astype(BF)


def attend_kernel(
    sc, t0, t1, t2, t3, pr, pc, w0, w1, w2, w3, w4, w5, w6, w7,
    o0, o1, o2, o3, xo, kvo, gateo, rowso, qo, atto, bro, grow, rin,
    wq, wo, wkv, wkvt, sm, vec, exo, exb, sem,
):
    m = pl.program_id(0)

    @pl.when(m == 0)
    def _():
        prepare(sc, (w0, w1, w2, w3, w4, w5, w6, w7), wq, wo, wkv, wkvt, sm, vec)

    def out_copy(i, h):
        return pltpu.make_async_copy(exb.at[h], exo.at[i, h], sem.at[h])

    @pl.when(m > 0)
    def _():
        for h in range(HEADS):
            out_copy(m - 1, h).wait()

    toks = (t0, t1, t2, t3)
    x = jnp.concatenate([t[0].astype(F32) for t in toks], 0)
    n, _ = norm_parts(x)
    a = (n * vec[0:1, :] + vec[1:2, :]).astype(BF)
    xo[0] = a
    router = dot(sm[...], router_turn(sc, 0)).astype(BF)
    posr, posc = pr[0, 0], pc[0, 0]
    gates = soft_gates(posc, a, router)
    gateo[0] = gates
    kv = dot(a, wkv[...]).astype(BF)
    kvo[0] = kv

    ext = dot(gather_all(posr), jnp.concatenate([a, gate_lanes(gates)], 1))
    rows = ext[:, 0:D].astype(BF)
    gate = by_expert(lambda e, r: pick(ext[r, D:512], e))
    rowso[0] = rows
    grow[0] = jnp.broadcast_to(gate, (ROWS, 128))
    q = by_expert(lambda e, r: dot(rows[r], wq[e])).astype(BF)
    q = q * jnp.asarray(0.125, BF)
    qo[0] = q
    slot = iota((SLOTS, 1), 0) + SQ * sc[0]
    slot = jnp.where(slot >= SLOTS, slot - SLOTS, slot)
    bias = jnp.where(slot < sc[4 + m], 0.0, MASKED)
    lane = iota((ROWS, 128), 1)
    inv_lanes = jnp.zeros((ROWS, 128), F32)
    for hp in range(3):
        span = slice(128 * hp, 128 * hp + 128)
        halves = []
        for side in range(2):
            h = 2 * hp + side
            at = spare(side)
            ka = jnp.where(own_half(SLOTS, side), kv[:, span].astype(F32), jnp.where(iota((SLOTS, 128), 1) == at, bias, 0.0)).astype(BF)
            one = jnp.where(lane == at, 1.0, 0.0)
            qa = jnp.where(own_half(ROWS, side), q[:, span].astype(F32), one).astype(BF)
            va = with_ones(kv[:, D + 128 * hp : D + 128 * hp + 128], side)
            s = dot_nt(qa, ka)
            ex = jnp.exp(s - jnp.max(s, -1, keepdims=True)).astype(BF)
            exb[h] = ex
            out_copy(m, h).start()
            pv = dot(ex, va)
            inv = 1.0 / pv[:, at : at + 1]
            inv_lanes = jnp.where(lane == h, inv, inv_lanes)
            halves.append(pv * inv)
        atto[0, :, span] = jnp.where(lane < 64, halves[0], halves[1]).astype(BF)
    rin[0] = inv_lanes
    br = by_expert(lambda e, r: dot(atto[0, r, :], wo[e])).astype(BF)
    bro[0] = br
    acc = dot(scatter_all(posc), (gate * br.astype(F32)).astype(BF))
    for s, o in enumerate((o0, o1, o2, o3)):
        o[0] = acc[SQ * s : SQ * s + SQ, :].astype(BF)

    @pl.when(m == MB - 1)
    def _():
        for h in range(HEADS):
            out_copy(m, h).wait()


def per_m(*shape):
    return pl.BlockSpec((1,) + shape, lambda m: (m,) + (0,) * len(shape))


def attend(sc, toks, posr, posc, pieces):
    saved = [
        (SLOTS, D, BF),
        (SLOTS, 768, BF),
        (SLOTS, 128, F32),
        (ROWS, D, BF),
        (ROWS, D, BF),
        (ROWS, D, BF),
        (ROWS, D, BF),
        (ROWS, 128, F32),
        (ROWS, 128, F32),
    ]
    outs = [(SQ, D, BF)] * 4 + saved
    kept = (MB, HEADS, ROWS, SLOTS)
    shared = [
        ((EXP, D, D), BF), ((EXP, D, D), BF), ((D, 768), BF), ((768, D), BF), ((D, 128), BF),
        ((8, D), F32),
    ]
    out = pl.pallas_call(
        attend_kernel,
        grid=(MB,),
        in_specs=[smem()]
        + [per_m(SQ, D)] * 4
        + [
            pl.BlockSpec((1, 1, 16, SLOTS), lambda m: (0, m, 0, 0)),
            pl.BlockSpec((1, 1, SLOTS, 128), lambda m: (0, m, 0, 0)),
        ]
        + [full((4, 48, 896))] * 8,
        out_specs=[per_m(*o[:-1]) for o in outs]
        + [full(v[0]) for v in shared]
        + [pl.BlockSpec(memory_space=pl.ANY)],
        out_shape=[sds((MB,) + o[:-1], o[-1]) for o in outs]
        + [sds(*v) for v in shared]
        + [sds(kept, BF)],
        scratch_shapes=[pltpu.VMEM(kept[1:], BF), pltpu.SemaphoreType.DMA((HEADS,))],
        compiler_params=params(1, 62),
        cost_estimate=cost(24),
        name="attend",
    )(sc, *toks, posr, posc, *pieces)
    n = len(outs)
    return out[:4], out[4:n] + out[-1:], out[n:-1]


def mix_kernel(t, p0, p1, p2, p3, vec, mixed, mlp_in):
    for m in range(MB):
        x = t[m].astype(F32)
        for p in (p0, p1, p2, p3):
            x = x + p[m].astype(F32)
        mixed[m] = x
        n, _ = norm_parts(x)
        mlp_in[m] = (n * vec[2:3, :] + vec[3:4, :]).astype(BF)


def mix(tokens, parts, vec):
    shape = (MB, SQ, D)
    return pl.pallas_call(
        mix_kernel,
        grid=(1,),
        in_specs=[full(shape)] * 5 + [full((8, D))],
        out_specs=[full(shape)] * 2,
        out_shape=[sds(shape, F32), sds(shape, BF)],
        compiler_params=params(1, 8),
        cost_estimate=cost(2),
        name="mix",
    )(tokens, *parts, vec)


def gelu_both(v):
    phi = 0.5 + 0.5 * lax.erf(v * 0.7071067811865476)
    density = jnp.exp(-0.5 * (v * v)) * 0.3989422804014327
    return v * phi, phi + v * density


FC = 768


def experts_kernel(
    sc, x0, x1, x2, x3, g0, g1, g2, g3, posr, posc, sm, w_ref,
    oo0, oo1, oo2, oo3, og0, og1, og2, og3, rmlp, keep, give, down,
    xe, gin, gates, acco, accg, hids, gps, dw,
):
    e = pl.program_id(0)

    @pl.when(e == 0)
    def _():
        turn = dot(sm[...], router_turn(sc, 12)).astype(BF)
        pad = hot(iota((D, 512), 0) == canonical_feature(iota((1, 512), 1)))
        for m in range(MB):
            a = jnp.concatenate([x[m] for x in (x0, x1, x2, x3)], 0)
            gt = soft_gates(posc[0, m], a, turn)
            gates[m] = gt
            xe[m, :, 0:512] = dot(a, pad).astype(BF)
            xe[m, :, 512:640] = gate_lanes(gt)
            gin[m] = jnp.concatenate([g[m] for g in (g0, g1, g2, g3)], 0)
        acco[...] = jnp.zeros_like(acco)
        accg[...] = jnp.zeros_like(accg)

    exts, grs = [], []
    for m in range(MB):
        g = gather_matrix(posr[0, m, pl.ds(e, 1), :])
        exts.append(dot(g, xe[m]))
        grs.append(dot(g, gin[m]))
    ext = jnp.concatenate(exts, 0)
    gr = jnp.concatenate(grs, 0)
    rows = ext[:, 0:512].astype(BF)
    gate = pick(ext[:, 512:640], e)
    gb = (gate * gr).astype(BF)
    branch = jnp.zeros((512, D), F32)
    back = jnp.zeros((512, 512), F32)
    for c in range(FF // FC):
        span = slice(c * FC, c * FC + FC)
        w = jnp.concatenate(
            [w_ref[:, 0, 16 * g : 16 * g + 16, :].reshape(512, D) for g in (2 * c, 2 * c + 1)], 1
        )
        wd = w_ref[16 * c : 16 * c + 16, 0, 64:112, :].reshape(FC, D)
        act, slope = gelu_both(dot(rows, w))
        hid = act.astype(BF)
        gp = (dot_nt(gb, wd) * slope).astype(BF)
        hids[:, span] = hid
        gps[:, span] = gp
        branch = branch + dot(hid, wd)
        back = back + dot_nt(gp, w)
    br = branch.astype(BF).astype(F32)
    t = jnp.sum(gr * br, -1, keepdims=True)
    scaled = (gate * br).astype(BF)
    lanes = split_lanes(t, e)
    backb = back.astype(BF)
    for m in range(MB):
        r = slice(CAP * m, CAP * m + CAP)
        sca = scatter_matrix(posc[0, m], e)
        acco[m] += dot(sca, jnp.concatenate([scaled[r], lanes[r]], 1))
        accg[m] += dot(sca, backb[r])
    dw[...] = dot_tn(rows, gps[...]).astype(BF).reshape(32, 16, FF)
    down[:, 0] = dot_tn(hids[...], gb).astype(BF).reshape(32, 48, D)
    for p in range(16):
        keep[p, 0] = dw[pl.ds(2 * p + sc[1], 1)][0]
        give[p, 0] = dw[pl.ds(2 * p + 1 - sc[1], 1)][0]

    @pl.when(e == EXP - 1)
    def _():
        turn = dot(sm[...], router_turn(sc, 12)).astype(BF)
        pad = hot(iota((D, 512), 0) == canonical_feature(iota((1, 512), 1)))
        total = jnp.zeros((D, 128), F32)
        for m in range(MB):
            dl = router_grad(gates[m], acco[m, :, D:512])
            a = jnp.concatenate([x[m] for x in (x0, x1, x2, x3)], 0)
            total = total + dot_tn(a, dl)
            part = dot_nt(accg[m].astype(BF), pad) + dot_nt(dl, turn)
            for s, (o, og) in enumerate(zip((oo0, oo1, oo2, oo3), (og0, og1, og2, og3))):
                r = slice(SQ * s, SQ * s + SQ)
                o[m] = acco[m, r, 0:D].astype(BF)
                og[m] = part[r].astype(BF)
        rmlp[...] = total


def experts(sc, xs, gs, posr, posc, sm, wmlp):
    piece = (full((MB, SQ, D)), sds((MB, SQ, D), BF))
    by_e = pl.BlockSpec((32, 1, 112, D), lambda e: (0, e, 0, 0))
    half = pl.BlockSpec((16, 1, 16, FF), lambda e: (0, e, 0, 0))
    outs = [piece] * 8 + [
        (full((D, 128)), sds((D, 128), F32)),
        (half, sds((16, EXP, 16, FF), BF)),
        (half, sds((16, EXP, 16, FF), BF)),
        (pl.BlockSpec((32, 1, 48, D), lambda e: (0, e, 0, 0)), sds((32, EXP, 48, D), BF)),
    ]
    got = pl.pallas_call(
        experts_kernel,
        grid=(EXP,),
        in_specs=[smem()]
        + [full((MB, SQ, D))] * 8
        + [
            pl.BlockSpec((1, MB, 16, SLOTS), lambda e: (1, 0, 0, 0)),
            pl.BlockSpec((1, MB, SLOTS, 128), lambda e: (1, 0, 0, 0)),
            full((D, 128)),
            by_e,
        ],
        out_specs=[o[0] for o in outs],
        out_shape=[o[1] for o in outs],
        scratch_shapes=[
            pltpu.VMEM((MB, SLOTS, 640), BF),
            pltpu.VMEM((MB, SLOTS, D), BF),
            pltpu.VMEM((MB, SLOTS, 128), F32),
            pltpu.VMEM((MB, SLOTS, 512), F32),
            pltpu.VMEM((MB, SLOTS, 512), F32),
            pltpu.VMEM((512, FF), BF),
            pltpu.VMEM((512, FF), BF),
            pltpu.VMEM((32, 16, FF), BF),
        ],
        compiler_params=params(1, 62),
        cost_estimate=cost(30),
        name="experts",
    )(sc, *xs, *gs, posr, posc, sm, wmlp)
    return got[:4], got[4:8], got[8], got[9:]


def turn_kernel(mixed, cot, p0, p1, p2, p3, vec, gmix, gmixb, gv):
    rows = [jnp.zeros((1, D), F32)] * 2
    for m in range(MB):
        n, inv = norm_parts(mixed[m])
        grad = jnp.zeros((SQ, D), F32)
        for p in (p0, p1, p2, p3):
            grad = grad + p[m].astype(F32)
        gm = cot[m].astype(F32) + norm_back(grad, n, inv, vec[2:3, :])
        gmix[m] = gm
        gmixb[m] = gm.astype(BF)
        rows[0] = rows[0] + jnp.sum(grad * n, 0, keepdims=True)
        rows[1] = rows[1] + jnp.sum(grad, 0, keepdims=True)
    gv[...] = jnp.concatenate(rows + [jnp.zeros((6, D), F32)], 0)


def turn(mixed, cot, parts, vec):
    shape = (MB, SQ, D)
    return pl.pallas_call(
        turn_kernel,
        grid=(1,),
        in_specs=[full(shape)] * 6 + [full((8, D))],
        out_specs=[full(shape), full(shape), full((8, D))],
        out_shape=[sds(shape, F32), sds(shape, BF), sds((8, D), F32)],
        compiler_params=params(1, 8),
        cost_estimate=cost(3),
        name="turn",
    )(mixed, cot, *parts, vec)


def attend_back_kernel(
    sc, g0, g1, g2, g3, t0, t1, t2, t3, posr, posc, x, kv, gates, rows, q, att, br, grow, rin, exi,
    wq, wo, wkvt, sm, vec, gv, rmlp,
    o0, o1, o2, o3, ta0, ta1,
    dkvt, dwq, dwo, dwkvt, dsm, dvec, exb, sem,
):
    m = pl.program_id(0)

    def in_copy(i, h):
        return pltpu.make_async_copy(exi.at[i, h], exb.at[i, h], sem.at[i, h])

    @pl.when(m == 0)
    def _():
        for h in range(HEADS):
            in_copy(0, h).start()
        dwq[...] = jnp.zeros_like(dwq)
        dwo[...] = jnp.zeros_like(dwo)
        dwkvt[...] = jnp.zeros_like(dwkvt)
        dsm[...] = jnp.zeros_like(dsm)
        dvec[...] = jnp.zeros_like(dvec)

    gin = jnp.concatenate([g[0] for g in (g0, g1, g2, g3)], 0)
    gr = dot(gather_all(posr[0, 0]), gin)
    gb = (grow[0][:, 0:1] * gr).astype(BF)
    t = jnp.sum(gr * br[0].astype(F32), -1, keepdims=True)
    ga = by_expert(lambda e, r: dot_nt(gb[r], wo[e])).astype(BF)
    for e in range(EXP):
        r = slice(CAP * e, CAP * e + CAP)
        dwo[:, D * e : D * e + D] += dot_tn(att[0, r, :], gb[r])
    lane = iota((ROWS, 128), 1)
    low = lane < 64
    dqs = []
    for h in range(HEADS):
        in_copy(m, h).wait()

    @pl.when(m == 0)
    def _():
        for h in range(HEADS):
            in_copy(1, h).start()

    for hp in range(3):
        span = slice(128 * hp, 128 * hp + 128)
        inv = jnp.where(low, rin[0, :, 2 * hp : 2 * hp + 1], rin[0, :, 2 * hp + 1 : 2 * hp + 2])
        gap = ga[:, span].astype(F32) * inv
        inner = gap * att[0, :, span].astype(F32)
        gapt = flip(gap.astype(BF)).astype(BF)
        qt = flip(q[0, :, span]).astype(BF)
        outs = []
        for side in range(2):
            h = 2 * hp + side
            at = spare(side)
            own = own_half(ROWS, side)
            ri = jnp.sum(jnp.where(own, inner, 0.0), -1, keepdims=True)
            hi = ri.astype(BF).astype(F32)
            rest = jnp.where(lane == at, -hi, jnp.where(lane == at + 1, hi - ri, 0.0))
            gaa = jnp.where(own, gap, rest).astype(BF)
            va = with_ones(kv[0, :, D + 128 * hp : D + 128 * hp + 128], side)
            p = exb[m, h]
            ds = (p.astype(F32) * dot_nt(gaa, va)).astype(BF)
            outs.append(dot(ds, kv[0, :, span]))
            hs = slice(64 * side, 64 * side + 64)
            dkvt[64 * h : 64 * h + 64, :] = dot(qt[hs, :], ds)
            dkvt[D + 64 * h : D + 64 * h + 64, :] = dot(gapt[hs, :], p)
        dqs.append((jnp.where(low, outs[0], outs[1]) * 0.125).astype(BF))
    dq = jnp.concatenate(dqs, 1)
    for e in range(EXP):
        r = slice(CAP * e, CAP * e + CAP)
        dwq[:, D * e : D * e + D] += dot_tn(rows[0, r, :], dq[r])
    back = by_expert(lambda e, r: dot_nt(dq[r], wq[e])).astype(BF)
    lanes = by_expert(lambda e, r: split_lanes(t[r], e))
    acc = dot(scatter_all(posc[0, 0]), jnp.concatenate([back, lanes], 1))

    dl = router_grad(gates[0], acc[:, D:512])
    router = dot(sm[...], router_turn(sc, 0)).astype(BF)
    dkvb = dkvt[...].astype(BF)
    part = acc[:, 0:D] + dot_nt(dl, router) + dot_tn(dkvb, wkvt[...])
    tk = jnp.concatenate([r[0].astype(F32) for r in (t0, t1, t2, t3)], 0)
    n, _ = norm_parts(tk)
    dvec[0:1, :] += jnp.sum(part * n, 0, keepdims=True)
    dvec[1:2, :] += jnp.sum(part, 0, keepdims=True)
    dsm[...] += dot_tn(x[0], dl)
    dwkvt[...] += dot(dkvb, x[0])
    for s, o in enumerate((o0, o1, o2, o3)):
        o[0] = part[SQ * s : SQ * s + SQ].astype(BF)

    @pl.when(m == MB - 1)
    def _():
        small = dot_nt(dsm[...].astype(BF), router_turn(sc, 0))
        small = small + dot_nt(rmlp[...].astype(BF), router_turn(sc, 12))
        vecs = jnp.concatenate(
            [jnp.zeros((24, D), F32), dvec[0:2, :], gv[0:2, :], jnp.zeros((100, D), F32)], 0
        ).astype(BF)
        small = (small + dot_nt(eye(D), vecs)).astype(BF)
        k, d = iota((512, 1), 0), iota((512, D), 1)
        r = k & 15
        own = hot(owned_feature(k, sc, True) == d)
        kvb = flip(dwkvt[...].astype(BF)).astype(BF)
        for e in range(EXP):
            span = slice(D * e, D * e + D)
            shared = hot(shared_feature(k >> 4, 4 * e + r - 12, r >= 12, sc, True) == d)
            weights = jnp.concatenate([dwq[:, span], dwo[:, span]], 1).astype(BF)
            wide = dot(jnp.concatenate([own, shared], 1), jnp.concatenate([weights, kvb], 0))
            wide = wide.astype(BF)
            rows = slice(16 * e, 16 * e + 16)
            for i, t in enumerate((ta0, ta1)):
                t[:, rows, 0:768] = wide[256 * i : 256 * i + 256].reshape(16, 16, 768)
            if e == 0:
                side = dot(hot(shared_feature(k >> 4, r, r < 12, sc, True) == d), small).astype(BF)
            else:
                side = jnp.zeros((512, 128), BF)
            for i, t in enumerate((ta0, ta1)):
                t[:, rows, 768:896] = side[256 * i : 256 * i + 256].reshape(16, 16, 128)


def attend_back(sc, gs, toks, posr, posc, saved, wq, wo, wkvt, sm, vec, gv, rmlp):
    piece = [(per_m(SQ, D), sds((MB, SQ, D), BF))] * 4
    outs = piece + [
        (full((16, 48, 896)), sds((16, 48, 896), BF)),
        (full((16, 48, 896)), sds((16, 48, 896), BF)),
    ]
    got = pl.pallas_call(
        attend_back_kernel,
        grid=(MB,),
        in_specs=[smem()]
        + [per_m(SQ, D)] * 8
        + [
            pl.BlockSpec((1, 1, 16, SLOTS), lambda m: (0, m, 0, 0)),
            pl.BlockSpec((1, 1, SLOTS, 128), lambda m: (0, m, 0, 0)),
        ]
        + [per_m(*v.shape[1:]) for v in saved[:-1]]
        + [pl.BlockSpec(memory_space=pl.ANY)]
        + [
            full((EXP, D, D)), full((EXP, D, D)), full((768, D)), full((D, 128)), full((8, D)),
            full((8, D)), full((D, 128)),
        ],
        out_specs=[o[0] for o in outs],
        out_shape=[o[1] for o in outs],
        scratch_shapes=[
            pltpu.VMEM((768, SLOTS), F32),
            pltpu.VMEM((D, EXP * D), F32),
            pltpu.VMEM((D, EXP * D), F32),
            pltpu.VMEM((768, D), F32),
            pltpu.VMEM((D, 128), F32),
            pltpu.VMEM((8, D), F32),
            pltpu.VMEM((MB, HEADS, ROWS, SLOTS), BF),
            pltpu.SemaphoreType.DMA((MB, HEADS)),
        ],
        compiler_params=params(1, 62),
        cost_estimate=cost(120),
        name="attend_back",
    )(sc, *gs, *toks, posr, posc, *saved, wq, wo, wkvt, sm, vec, gv, rmlp)
    return got[:4], got[4:]


def finish_kernel(gmix, tokens, p0, p1, p2, p3, vec, out):
    for m in range(MB):
        n, inv = norm_parts(tokens[m].astype(F32))
        grad = jnp.zeros((SQ, D), F32)
        for p in (p0, p1, p2, p3):
            grad = grad + p[m].astype(F32)
        out[m] = (gmix[m] + norm_back(grad, n, inv, vec[0:1, :])).astype(BF)


def finish(gmix, tokens, parts, vec):
    shape = (MB, SQ, D)
    return pl.pallas_call(
        finish_kernel,
        grid=(1,),
        in_specs=[full(shape)] * 6 + [full((8, D))],
        out_specs=full(shape),
        out_shape=sds(shape, BF),
        compiler_params=params(1, 8),
        cost_estimate=cost(2),
        name="finish",
    )(gmix, tokens, *parts, vec)


def shift(a, axis, s):
    n = lax.axis_size(axis)
    return lax.ppermute(a, axis, [(i, (i + s) % n) for i in range(n)])


def fetch(a, axis):
    one, three, two = [shift(a, axis, 4 - s) for s in (1, 3, 2)]
    return [a, one, two, three]


def send(parts, axis):
    two, one, three = [shift(parts[s], axis, s) for s in (2, 1, 3)]
    return [parts[0], one, two, three]


def add2(a, b):
    return (a.astype(F32) + b.astype(F32)).astype(BF)


def tie(*arrays):
    return lax.optimization_barrier(arrays)


def fold(a, axis):
    got = send([a[s] for s in range(a.shape[0])], axis)
    return sum(v.astype(F32) for v in got)


def local(
    tokens, patch_counts, attn_routes, mlp_routes, gain1, bias1, gain2, bias2, wkv, rattn, rmlp,
    wq, wo, wup, wdown, cotangent,
):
    tokens = tokens.reshape(MB, SQ, D)
    cot = cotangent.reshape(MB, SQ, D)
    index = [lax.axis_index(a) for a in ("x", "c", "z", "y")]
    sc = jnp.stack(index + [patch_counts[0, 0], patch_counts[1, 0], 0, 0]).astype(jnp.int32)

    shared, own, mlp_shard = pack(
        wkv, rattn, rmlp, gain1, bias1, gain2, bias2, wq, wo, wup, wdown,
        *[jnp.moveaxis(r.reshape(MB, SQ, 4), 1, 2) for r in (attn_routes, mlp_routes)],
    )
    got = fetch(shared, "x")
    kv12 = jnp.concatenate([v[0:3, 0:896] for v in got], 0)
    shard = jnp.concatenate([own[:, 0:12], kv12[:, :768].reshape(3, 4, 768)], 1).reshape(48, 768)
    shard = jnp.concatenate([shard, jnp.pad(kv12[:, 768:], ((0, 36), (0, 0)))], 1)
    zs = jnp.stack(fetch(shard, "z"))
    zs, sc = tie(zs, sc)
    posr, posc = plan(sc, got)
    pieces = fetch(zs, "y")
    toks = fetch(tokens, "x")
    both = tie(*pieces, *toks)
    pieces, toks = list(both[:4]), list(both[4:])
    pieces = pieces + [shift(p, "c", 1) for p in pieces]
    *pieces, mlp_shard, posr, posc = tie(*pieces, mlp_shard, posr, posc)
    wmlp = lax.all_gather(mlp_shard, TOKS, axis=0).reshape(32, EXP, 112, D)

    parts, saved, (fq, fo, fkv, fkvt, sm, vec) = attend(sc, toks, posr, posc, pieces)
    parts, cot = tie(parts, cot)
    gs = fetch(cot, "x")
    mixed, mlp_in = mix(tokens, send(parts, "x"), vec)
    xs = fetch(mlp_in, "x")
    outp, gradp, rm, (keep, give, down) = experts(sc, xs, gs, posr, posc, sm, wmlp)
    down = lax.psum_scatter(down, TOKS, scatter_dimension=0, tiled=True)
    give = shift(give, "c", 1)
    gradp = send(gradp, "x")
    up = add2(keep, give)
    *gradp, up = tie(*gradp, up)
    up = lax.all_to_all(up, ("z", "y"), 0, 0, tiled=True)
    gmix, gmixb, gv = turn(mixed, cot, gradp, vec)
    gms = fetch(gmixb, "x")
    back, (ta, ta1) = attend_back(sc, gms, toks, posr, posc, saved, fq, fo, fkvt, sm, vec, gv, rm)
    ta1 = shift(ta1, "c", 1)
    ta1, back, outp = tie(ta1, back, outp)
    ta, up = tie(add2(ta, ta1), up)
    ta = lax.all_to_all(ta, ("z", "y"), 0, 0, tiled=True)
    ta = jnp.sum(ta.astype(F32), 0)
    back = send(back, "x")
    outp, back = tie(outp, back)
    dup = jnp.sum(up.astype(F32), 0)[:, 0:12]
    gmix, dup = tie(gmix, dup)
    tokens_grad = finish(gmix, tokens, back, vec)
    result = mixed
    for o in send(outp, "x"):
        result = result + o.astype(F32)
    result = result.astype(BF)
    t3 = ta.reshape(3, 16, 896)
    kv = jnp.concatenate([t3[:, 12:16, :768].reshape(12, 768), ta[0:12, 768:]], 1)
    small = fold(kv.astype(BF).reshape(4, 3, 896), "x")
    small, down = tie(small, down)

    ddown = down.astype(F32).reshape(EXP, 48, D)
    dq, do = t3[:, :12, :D], t3[:, :12, D:768]
    shape = (MB, 1, SQ, D)
    return (
        result.reshape(shape),
        tokens_grad.reshape(shape),
        small[:, 792],
        small[:, 793],
        small[:, 794],
        small[:, 795],
        small[:, 0:768],
        small[:, 768:780],
        small[:, 780:792],
        dq,
        do,
        dup,
        ddown,
    )


def solution(mesh):
    fine = Mesh(mesh.devices.reshape(4, 4, 2, 4), ("z", "y", "c", "x"))
    every = TOKS + ("x",)
    act = P(None, TOKS, "x", None)
    row, mat, own = P(every), P(every, None), P("x", TOKS, None)
    return jax.shard_map(
        local,
        mesh=fine,
        in_specs=(
            act, P(None, TOKS), act, act, row, row, row, row, mat, mat, mat, own, own, own, own, act,
        ),
        out_specs=(act, act, row, row, row, row, mat, mat, mat, own, own, own, own),
        check_vma=False,
    )
```

```python
import jax
import jax.numpy as jnp
from jax import lax
from jax.experimental import pallas as pl
from jax.experimental.pallas import tpu as pltpu
from jax.sharding import Mesh, PartitionSpec as P

BF = jnp.bfloat16
F32 = jnp.float32
EPSILON = 1e-06
MASKED = -1e30
MB, NX, SQ, SLOTS, D = 2, 4, 144, 576, 384
EXP, CAP, HEADS, FF = 3, 256, 6, 1536
PACK = 160
TOKS = ("z", "y", "c")
VMEM = 62 * 1024 * 1024


def params(n, mib=60):
    return pltpu.CompilerParams(
        dimension_semantics=("arbitrary",) * n, vmem_limit_bytes=mib * 1024 * 1024
    )


def cost(us):
    return pl.CostEstimate(flops=int(us * 1e9), bytes_accessed=0, transcendentals=0)


def dot(a, b):
    return jnp.dot(a, b, preferred_element_type=F32)


def dot_nt(a, b):
    return lax.dot_general(a, b, (((1,), (1,)), ((), ())), preferred_element_type=F32)


def dot_tn(a, b):
    return lax.dot_general(a, b, (((0,), (0,)), ((), ())), preferred_element_type=F32)


def iota(shape, dim):
    return lax.broadcasted_iota(jnp.int32, shape, dim)


def hot(cond):
    return jnp.where(cond, 1.0, 0.0).astype(BF)


def eye(n):
    return hot(iota((n, n), 0) == iota((n, n), 1))


def flip(a):
    return dot_nt(eye(a.shape[1]), a)


def tok_of(place, sc, plain=False):
    c = (sc[1] + (place >> 4)) & 1
    if plain:
        return (place & 15) * 2 + c
    z = (sc[2] + (place & 3)) & 3
    y = (sc[3] + ((place >> 2) & 3)) & 3
    return z * 8 + y * 2 + c


def third(v):
    return (v * 11) >> 5


def owned_feature(k, sc, plain=False):
    r = k & 15
    return jnp.where(r < 12, tok_of(k >> 4, sc, plain) * 12 + r, -1)


def shared_feature(place, idx, valid, sc, plain=False):
    s = third(idx)
    feature = tok_of(place, sc, plain) * 12 + ((sc[0] + s) & 3) * 3 + idx - 3 * s
    return jnp.where(valid, feature, -1)


def canonical_feature(col):
    r = col & 15
    return jnp.where(r < 12, (col >> 4) * 12 + r, -1)


def native_lane(sc):
    j = iota((1, 128), 1)
    n = j + 3 * sc[0]
    n = jnp.where(n >= 12, n - 12, n)
    return jnp.where(j < 12, n, -1)


def router_turn(sc, offset):
    n = native_lane(sc)
    return hot((iota((128, 128), 0) == n + offset) & (n >= 0))


def norm_parts(x):
    mu = jnp.mean(x, -1, keepdims=True)
    c = x - mu
    var = jnp.mean(c * c, -1, keepdims=True)
    inv = lax.rsqrt(var + EPSILON)
    return c * inv, inv


def norm_back(grad, normed, inv, gain):
    u = grad * gain
    a = jnp.mean(u, -1, keepdims=True)
    b = jnp.mean(u * normed, -1, keepdims=True)
    return (u - a - normed * b) * inv


def soft_gates(posc, x, router):
    inside = posc >= 0.0
    logits = jnp.where(inside, dot(x, router), MASKED)
    top = jnp.max(logits, -1, keepdims=True)
    ex = jnp.where(inside, jnp.exp(logits - top), 0.0)
    return ex / jnp.sum(ex, -1, keepdims=True)


def gate_lanes(gates):
    hi = gates.astype(BF).astype(F32)
    lo = pltpu.roll(gates - hi, 64, 1)
    return jnp.where(iota(gates.shape, 1) < 64, hi, lo).astype(BF)


def pick(ext, e):
    lane = iota(ext.shape, 1)
    return jnp.sum(jnp.where((lane == e) | (lane == 64 + e), ext, 0.0), -1, keepdims=True)


def split_lanes(col, e):
    hi = col.astype(BF).astype(F32)
    lane = iota((col.shape[0], 128), 1)
    both = jnp.where(lane == e, hi, 0.0) + jnp.where(lane == 64 + e, col - hi, 0.0)
    return both.astype(BF)


def gather_matrix(row):
    return hot(row == iota((CAP, SLOTS), 0).astype(F32))


def router_grad(gates, lanes):
    t = lanes + pltpu.roll(lanes, 64, 1)
    inner = jnp.sum(gates * t, -1, keepdims=True)
    return (gates * (t - inner)).astype(BF)


def smem():
    return pl.BlockSpec(memory_space=pltpu.SMEM)


def full(shape):
    return pl.BlockSpec(shape, lambda *_: (0,) * len(shape))


def sds(shape, dtype):
    return jax.ShapeDtypeStruct(shape, dtype)


def pack_kernel(
    wkv, rattn, rmlp, g1, b1, g2, b2, wq, wo, wup, wdown, ra, rm, shared, own, mlp
):
    shared[...] = jnp.zeros_like(shared)
    own[...] = jnp.zeros_like(own)
    mlp[...] = jnp.zeros_like(mlp)
    shared[0:3, 0:768] = wkv[...]
    shared[0:3, 768:780] = rattn[...]
    shared[0:3, 780:792] = rmlp[...]
    lane, row = iota((3, 3), 1), iota((3, 3), 0)
    cols = []
    for v in (g1, b1, g2, b2):
        line = v[...].astype(F32).reshape(1, 3)
        cols.append(jnp.sum(jnp.where(lane == row, line, 0.0), -1, keepdims=True))
    shared[0:3, 792:796] = jnp.concatenate(cols, 1).astype(BF)
    routes = jnp.zeros((16, SQ), F32)
    for m in range(MB):
        for i, r in enumerate((ra, rm)):
            put = hot(iota((16, 4), 0) == iota((16, 4), 1) + 8 * i + 4 * m)
            routes = routes + dot(put, r[m].astype(F32).astype(BF))
    shared[:, 1024 : 1024 + SQ] = routes.astype(BF)
    for e in range(EXP):
        own[e, 0:12, 0:D] = wq[e]
        own[e, 0:12, D : 2 * D] = wo[e]
        for g in range(4):
            mlp[e, 16 * g : 16 * g + 12, :] = wup[e, :, D * g : D * g + D]
        mlp[e, 64:112, :] = wdown[e]


def pack(*args):
    shapes = [(16, 1280), (EXP, 16, 768), (EXP, 112, D)]
    return pl.pallas_call(
        pack_kernel,
        grid=(1,),
        in_specs=[full(v.shape) for v in args],
        out_specs=[full(v) for v in shapes],
        out_shape=[sds(v, BF) for v in shapes],
        compiler_params=params(1, 62),
        cost_estimate=cost(2),
        name="pack",
    )(*args)


def plan_kernel(sc, r0, r1, r2, r3, posr, posc):
    unit = hot(iota((SQ, 256), 0) == iota((SQ, 256), 1))
    rcol = jnp.concatenate([dot_nt(unit, r[...]) for r in (r0, r1, r2, r3)], 0)
    nat = native_lane(sc).astype(F32)
    lower = hot(iota((SLOTS, SLOTS), 1) < iota((SLOTS, SLOTS), 0))
    unit = hot(iota((16, 128), 0) == iota((16, 128), 1))
    for i in range(2 * MB):
        member = jnp.zeros((SLOTS, 128), F32)
        for k in range(4 * i, 4 * i + 4):
            member = member + jnp.where(rcol[:, k : k + 1] == nat, 1.0, 0.0)
        mb = member.astype(BF)
        mt = dot_nt(unit, mb)
        posc[i // MB, i % MB] = jnp.where(member > 0.5, dot(lower, mb), -1.0)
        posr[i // MB, i % MB] = jnp.where(mt > 0.5, dot_nt(mt.astype(BF), lower), -1.0)


def plan(sc, pieces):
    return pl.pallas_call(
        plan_kernel,
        grid=(1,),
        in_specs=[smem()] + [pl.BlockSpec((16, 256), lambda i: (0, 4))] * 4,
        out_specs=[full((2, MB, 16, SLOTS)), full((2, MB, SLOTS, 128))],
        out_shape=[sds((2, MB, 16, SLOTS), F32), sds((2, MB, SLOTS, 128), F32)],
        compiler_params=params(1, 62),
        cost_estimate=cost(4),
        name="plan",
    )(sc, *pieces)


def prepare(sc, pieces, wq, wo, wkv, wkvt, sm, vec):
    def gathered(rows, lanes):
        return jnp.concatenate([p[:, rows, lanes].reshape(-1, lanes.stop - lanes.start) for p in pieces], 0)

    take = hot(iota((D, 512), 0) == owned_feature(iota((1, 512), 1), sc))
    for e in range(EXP):
        nat = dot(take, gathered(slice(16 * e, 16 * e + 16), slice(0, 768))).astype(BF)
        wq[e] = nat[:, :D]
        wo[e] = nat[:, D:]
    k = iota((1, 1536), 1)
    place = (k * 1366) >> 16
    r48 = k - place * 48
    r16 = r48 & 15
    kv_feature = shared_feature(place, (r48 >> 4) * 4 + r16 - 12, r16 >= 12, sc)
    kv = dot(hot(iota((D, 1536), 0) == kv_feature), gathered(slice(0, 48), slice(0, 768))).astype(BF)
    wkv[...] = kv
    wkvt[...] = kv.T
    k = iota((1, 512), 1)
    sm_feature = shared_feature(k >> 4, k & 15, (k & 15) < 12, sc)
    side = gathered(slice(0, 16), slice(768, 896))
    small = dot(hot(iota((D, 512), 0) == sm_feature), side).astype(BF)
    sm[...] = small
    vec[...] = dot_nt(hot(iota((8, 128), 1) == iota((8, 128), 0) + 24), small)


ROWS = EXP * CAP


def gather_all(posr):
    return jnp.concatenate([gather_matrix(posr[e : e + 1, :]) for e in range(EXP)], 0)


def by_expert(f):
    return jnp.concatenate([f(e, slice(CAP * e, CAP * e + CAP)) for e in range(EXP)], 0)


def own_half(rows, side):
    lane = iota((rows, 128), 1)
    return lane < 64 if side == 0 else lane >= 64


def spare(side):
    return 64 if side == 0 else 0


def keep_lanes(side):
    return hot(own_half(1, side))


def with_ones(v, side):
    lane, at = iota((1, 128), 1), spare(side)
    return v * keep_lanes(side) + hot((lane == at) | (lane == at + 1))


def attend_kernel(
    sc, t0, t1, t2, t3, pr, pc, w0, w1, w2, w3, w4, w5, w6, w7,
    o0, o1, o2, o3, gateo, kvo, rowso, qo, atto, bro, rin,
    wq, wo, wkvt, sm, vec, exo, exb, sem, wkv,
):
    m = pl.program_id(0)

    @pl.when(m == 0)
    def _():
        prepare(sc, (w0, w1, w2, w3, w4, w5, w6, w7), wq, wo, wkv, wkvt, sm, vec)

    def out_copy(i, h):
        return pltpu.make_async_copy(exb.at[h], exo.at[i, h], sem.at[h])

    @pl.when(m > 0)
    def _():
        for h in range(HEADS):
            out_copy(m - 1, h).wait()

    toks = (t0, t1, t2, t3)
    x = jnp.concatenate([t[0].astype(F32) for t in toks], 0)
    n, _ = norm_parts(x)
    a = (n * vec[0:1, :] + vec[1:2, :]).astype(BF)
    router = dot(sm[...], router_turn(sc, 0)).astype(BF)
    posr, posc = pr[0, 0], pc[0, 0]
    gates = soft_gates(posc, a, router)
    gateo[0] = gates
    kv = dot(a, wkv[...]).astype(BF)
    kvo[0] = kv

    route = gather_all(posr)
    ext = dot(route, jnp.concatenate([a, gate_lanes(gates)], 1))
    rows = ext[:, 0:D].astype(BF)
    gate = by_expert(lambda e, r: pick(ext[r, D:512], e))
    rowso[0] = rows
    q = by_expert(lambda e, r: dot(rows[r], wq[e])).astype(BF)
    q = q * jnp.asarray(0.125, BF)
    qo[0] = q
    slot = iota((SLOTS, 1), 0) + SQ * sc[0]
    slot = jnp.where(slot >= SLOTS, slot - SLOTS, slot)
    bias = jnp.where(slot < sc[4 + m], 0.0, MASKED)
    lane = iota((ROWS, 128), 1)
    biases = [
        jnp.where(iota((SLOTS, 128), 1) == spare(side), bias, 0.0).astype(BF) for side in range(2)
    ]
    inv_lanes = jnp.zeros((ROWS, 128), F32)
    for hp in range(3):
        span = slice(128 * hp, 128 * hp + 128)
        halves = []
        for side in range(2):
            h = 2 * hp + side
            at = spare(side)
            ka = kv[:, span] * keep_lanes(side) + biases[side]
            qa = q[:, span] * keep_lanes(side) + hot(iota((1, 128), 1) == at)
            va = with_ones(kv[:, D + 128 * hp : D + 128 * hp + 128], side)
            s = dot_nt(qa, ka)
            ex = jnp.exp(s - jnp.max(s, -1, keepdims=True)).astype(BF)
            exb[h] = ex
            out_copy(m, h).start()
            pv = dot(ex, va)
            inv = 1.0 / pv[:, at : at + 1]
            inv_lanes = jnp.where(lane == h, inv, inv_lanes)
            halves.append(pv * inv)
        atto[0, :, span] = jnp.where(lane < 64, halves[0], halves[1]).astype(BF)
    rin[0] = jnp.where(lane == 8, gate, inv_lanes)
    br = by_expert(lambda e, r: dot(atto[0, r, :], wo[e])).astype(BF)
    bro[0] = br
    acc = dot_tn(route, (gate * br.astype(F32)).astype(BF))
    for s, o in enumerate((o0, o1, o2, o3)):
        o[0] = acc[SQ * s : SQ * s + SQ, :].astype(BF)

    @pl.when(m == MB - 1)
    def _():
        for h in range(HEADS):
            out_copy(m, h).wait()


def per_m(*shape):
    return pl.BlockSpec((1,) + shape, lambda m: (m,) + (0,) * len(shape))


def attend(sc, toks, posr, posc, pieces):
    saved = [
        (SLOTS, 128, F32),
        (SLOTS, 768, BF),
        (ROWS, D, BF),
        (ROWS, D, BF),
        (ROWS, D, BF),
        (ROWS, D, BF),
        (ROWS, 128, F32),
    ]
    outs = [(SQ, D, BF)] * 4 + saved
    kept = (MB, HEADS, ROWS, SLOTS)
    shared = [
        ((EXP, D, D), BF), ((EXP, D, D), BF), ((768, D), BF), ((D, 128), BF),
        ((8, D), F32),
    ]
    out = pl.pallas_call(
        attend_kernel,
        grid=(MB,),
        in_specs=[smem()]
        + [per_m(SQ, D)] * 4
        + [
            pl.BlockSpec((1, 1, 16, SLOTS), lambda m: (0, m, 0, 0)),
            pl.BlockSpec((1, 1, SLOTS, 128), lambda m: (0, m, 0, 0)),
        ]
        + [full((4, 48, 896))] * 8,
        out_specs=[per_m(*o[:-1]) for o in outs]
        + [full(v[0]) for v in shared]
        + [pl.BlockSpec(memory_space=pl.ANY)],
        out_shape=[sds((MB,) + o[:-1], o[-1]) for o in outs]
        + [sds(*v) for v in shared]
        + [sds(kept, BF)],
        scratch_shapes=[
            pltpu.VMEM(kept[1:], BF),
            pltpu.SemaphoreType.DMA((HEADS,)),
            pltpu.VMEM((D, 768), BF),
        ],
        compiler_params=params(1, 62),
        cost_estimate=cost(24),
        name="attend",
    )(sc, *toks, posr, posc, *pieces)
    n = len(outs)
    return out[:4], out[4:n] + out[-1:], out[n:-1]


def mix_kernel(t, p0, p1, p2, p3, vec, mixed, mlp_in):
    for m in range(MB):
        x = t[m].astype(F32)
        for p in (p0, p1, p2, p3):
            x = x + p[m].astype(F32)
        mixed[m] = x
        n, _ = norm_parts(x)
        mlp_in[m] = (n * vec[2:3, :] + vec[3:4, :]).astype(BF)


def mix(tokens, parts, vec):
    shape = (MB, SQ, D)
    return pl.pallas_call(
        mix_kernel,
        grid=(1,),
        in_specs=[full(shape)] * 5 + [full((8, D))],
        out_specs=[full(shape)] * 2,
        out_shape=[sds(shape, F32), sds(shape, BF)],
        compiler_params=params(1, 8),
        cost_estimate=cost(2),
        name="mix",
    )(tokens, *parts, vec)


def gelu_both(v):
    phi = 0.5 + 0.5 * lax.erf(v * 0.7071067811865476)
    density = jnp.exp(-0.5 * (v * v)) * 0.3989422804014327
    return v * phi, phi + v * density


FC = 768


def experts_kernel(
    sc, x0, x1, x2, x3, g0, g1, g2, g3, posr, posc, sm, w_any,
    oo0, oo1, oo2, oo3, og0, og1, og2, og3, rmlp, keep, give, down,
    xe, gates, acc, hids, gps, dw, wbuf, sem,
):
    e = pl.program_id(0)

    def fetch_weights(i):
        return pltpu.make_async_copy(w_any.at[:, i], wbuf.at[i], sem.at[i])

    @pl.when(e == 0)
    def _():
        for i in range(EXP):
            fetch_weights(i).start()

    @pl.when(e == 0)
    def _():
        turn = dot(sm[...], router_turn(sc, 12)).astype(BF)
        pad = hot(iota((D, 512), 0) == canonical_feature(iota((1, 512), 1)))
        for m in range(MB):
            a = jnp.concatenate([x[m] for x in (x0, x1, x2, x3)], 0)
            gt = soft_gates(posc[0, m], a, turn)
            gates[m] = gt
            xe[m, :, 0:512] = dot(a, pad).astype(BF)
            xe[m, :, 512:640] = gate_lanes(gt)
            xe[m, :, 640:1024] = jnp.concatenate([g[m] for g in (g0, g1, g2, g3)], 0)
        acc[...] = jnp.zeros_like(acc)

    routes = [gather_matrix(posr[0, m, pl.ds(e, 1), :]) for m in range(MB)]
    ext = jnp.concatenate([dot(routes[m], xe[m]) for m in range(MB)], 0)
    gr = ext[:, 640:1024]
    rows = ext[:, 0:512].astype(BF)
    gate = pick(ext[:, 512:640], e)
    gb = (gate * gr).astype(BF)
    branch = jnp.zeros((512, D), F32)
    back = jnp.zeros((512, 512), F32)
    fetch_weights(e).wait()
    w_ref = wbuf.at[e]
    for c in range(FF // FC):
        span = slice(c * FC, c * FC + FC)
        w = jnp.concatenate(
            [w_ref[:, 16 * g : 16 * g + 16, :].reshape(512, D) for g in (2 * c, 2 * c + 1)], 1
        )
        wd = w_ref[16 * c : 16 * c + 16, 64:112, :].reshape(FC, D)
        act, slope = gelu_both(dot(rows, w))
        hid = act.astype(BF)
        gp = (dot_nt(gb, wd) * slope).astype(BF)
        hids[:, span] = hid
        gps[:, span] = gp
        branch = branch + dot(hid, wd)
        back = back + dot_nt(gp, w)
    br = branch.astype(BF).astype(F32)
    t = jnp.sum(gr * br, -1, keepdims=True)
    scaled = (gate * br).astype(BF)
    lanes = split_lanes(t, e)
    backb = back.astype(BF)
    for m in range(MB):
        r = slice(CAP * m, CAP * m + CAP)
        acc[m] += dot_tn(routes[m], jnp.concatenate([scaled[r], lanes[r], backb[r]], 1))
    dw[...] = dot_tn(rows, gps[...]).astype(BF).reshape(32, 16, FF)
    down[:, 0] = dot_tn(hids[...], gb).astype(BF).reshape(32, 48, D)
    for p in range(16):
        keep[p, 0] = dw[pl.ds(2 * p + sc[1], 1)][0]
        give[p, 0] = dw[pl.ds(2 * p + 1 - sc[1], 1)][0]

    @pl.when(e == EXP - 1)
    def _():
        turn = dot(sm[...], router_turn(sc, 12)).astype(BF)
        pad = hot(iota((D, 512), 0) == canonical_feature(iota((1, 512), 1)))
        total = jnp.zeros((D, 128), F32)
        for m in range(MB):
            dl = router_grad(gates[m], acc[m, :, D:512])
            a = jnp.concatenate([x[m] for x in (x0, x1, x2, x3)], 0)
            total = total + dot_tn(a, dl)
            part = dot_nt(acc[m, :, 512:1024].astype(BF), pad) + dot_nt(dl, turn)
            for s, (o, og) in enumerate(zip((oo0, oo1, oo2, oo3), (og0, og1, og2, og3))):
                r = slice(SQ * s, SQ * s + SQ)
                o[m] = acc[m, r, 0:D].astype(BF)
                og[m] = part[r].astype(BF)
        rmlp[...] = total


def experts(sc, xs, gs, posr, posc, sm, wmlp):
    piece = (full((MB, SQ, D)), sds((MB, SQ, D), BF))
    half = pl.BlockSpec((16, 1, 16, FF), lambda e: (0, e, 0, 0))
    outs = [piece] * 8 + [
        (full((D, 128)), sds((D, 128), F32)),
        (half, sds((16, EXP, 16, FF), BF)),
        (half, sds((16, EXP, 16, FF), BF)),
        (pl.BlockSpec((32, 1, 48, D), lambda e: (0, e, 0, 0)), sds((32, EXP, 48, D), BF)),
    ]
    got = pl.pallas_call(
        experts_kernel,
        grid=(EXP,),
        in_specs=[smem()]
        + [full((MB, SQ, D))] * 8
        + [
            pl.BlockSpec((1, MB, 16, SLOTS), lambda e: (1, 0, 0, 0)),
            pl.BlockSpec((1, MB, SLOTS, 128), lambda e: (1, 0, 0, 0)),
            full((D, 128)),
            pl.BlockSpec(memory_space=pl.ANY),
        ],
        out_specs=[o[0] for o in outs],
        out_shape=[o[1] for o in outs],
        scratch_shapes=[
            pltpu.VMEM((MB, SLOTS, 1024), BF),
            pltpu.VMEM((MB, SLOTS, 128), F32),
            pltpu.VMEM((MB, SLOTS, 1024), F32),
            pltpu.VMEM((512, FF), BF),
            pltpu.VMEM((512, FF), BF),
            pltpu.VMEM((32, 16, FF), BF),
            pltpu.VMEM((EXP, 32, 112, D), BF),
            pltpu.SemaphoreType.DMA((EXP,)),
        ],
        compiler_params=params(1, 62),
        cost_estimate=cost(30),
        name="experts",
    )(sc, *xs, *gs, posr, posc, sm, wmlp)
    return got[:4], got[4:8], got[8], got[9:]


def turn_kernel(mixed, cot, p0, p1, p2, p3, vec, gmix, gmixb, gv):
    rows = [jnp.zeros((1, D), F32)] * 2
    for m in range(MB):
        n, inv = norm_parts(mixed[m])
        grad = jnp.zeros((SQ, D), F32)
        for p in (p0, p1, p2, p3):
            grad = grad + p[m].astype(F32)
        gm = cot[m].astype(F32) + norm_back(grad, n, inv, vec[2:3, :])
        gmix[m] = gm
        gmixb[m] = gm.astype(BF)
        rows[0] = rows[0] + jnp.sum(grad * n, 0, keepdims=True)
        rows[1] = rows[1] + jnp.sum(grad, 0, keepdims=True)
    gv[...] = jnp.concatenate(rows + [jnp.zeros((6, D), F32)], 0)


def turn(mixed, cot, parts, vec):
    shape = (MB, SQ, D)
    return pl.pallas_call(
        turn_kernel,
        grid=(1,),
        in_specs=[full(shape)] * 6 + [full((8, D))],
        out_specs=[full(shape), full(shape), full((8, D))],
        out_shape=[sds(shape, F32), sds(shape, BF), sds((8, D), F32)],
        compiler_params=params(1, 8),
        cost_estimate=cost(3),
        name="turn",
    )(mixed, cot, *parts, vec)


def attend_back_kernel(
    sc, g0, g1, g2, g3, posr, gates, rin, wq, wo, wkvt, sm, vec, gv, rmlp,
    t0, t1, t2, t3, kv_, rows_, q_, att_, br_, exi,
    o0, o1, o2, o3, ta0, ta1,
    dkvt, dwq, dwo, dwkvt, dsm, dvec, exb, sem,
    tb0, tb1, tb2, tb3, kvb, rowsb, qb, attb, brb, late,
):
    m = pl.program_id(0)
    moved = (
        (br_, brb), (att_, attb), (q_, qb), (kv_, kvb), (rows_, rowsb),
        (t0, tb0), (t1, tb1), (t2, tb2), (t3, tb3),
    )

    def load(i, k):
        return pltpu.make_async_copy(moved[k][0].at[i], moved[k][1].at[i], late.at[i, k])

    def load_all(i):
        for k in range(4):
            load(i, k).start()
        for h in range(HEADS):
            in_copy(i, h).start()
        for k in range(4, 9):
            load(i, k).start()

    def in_copy(i, h):
        return pltpu.make_async_copy(exi.at[i, h], exb.at[i, h], sem.at[i, h])

    @pl.when(m == 0)
    def _():
        load_all(0)
        dwq[...] = jnp.zeros_like(dwq)
        dwo[...] = jnp.zeros_like(dwo)
        dwkvt[...] = jnp.zeros_like(dwkvt)
        dsm[...] = jnp.zeros_like(dsm)
        dvec[...] = jnp.zeros_like(dvec)

    gin = jnp.concatenate([g[0] for g in (g0, g1, g2, g3)], 0)
    route = gather_all(posr[0, 0])
    gr = dot(route, gin)
    gb = (rin[0, :, 8:9] * gr).astype(BF)
    for k in range(4):
        load(m, k).wait()
    t = jnp.sum(gr * brb[m].astype(F32), -1, keepdims=True)
    ga = by_expert(lambda e, r: dot_nt(gb[r], wo[e])).astype(BF)
    for e in range(EXP):
        r = slice(CAP * e, CAP * e + CAP)
        dwo[:, D * e : D * e + D] += dot_tn(attb[m, r, :], gb[r])
    lane = iota((ROWS, 128), 1)
    low = lane < 64
    dqs = []

    @pl.when(m == 0)
    def _():
        load_all(1)

    for hp in range(3):
        span = slice(128 * hp, 128 * hp + 128)
        inv = jnp.where(low, rin[0, :, 2 * hp : 2 * hp + 1], rin[0, :, 2 * hp + 1 : 2 * hp + 2])
        gap = ga[:, span].astype(F32) * inv
        inner = gap * attb[m, :, span].astype(F32)
        gapt = flip(gap.astype(BF)).astype(BF)
        qt = flip(qb[m, :, span]).astype(BF)
        outs = []
        for side in range(2):
            h = 2 * hp + side
            at = spare(side)
            own = own_half(ROWS, side)
            ri = jnp.sum(jnp.where(own, inner, 0.0), -1, keepdims=True)
            hi = ri.astype(BF).astype(F32)
            rest = jnp.where(lane == at, -hi, jnp.where(lane == at + 1, hi - ri, 0.0))
            gaa = jnp.where(own, gap, rest).astype(BF)
            va = with_ones(kvb[m, :, D + 128 * hp : D + 128 * hp + 128], side)
            in_copy(m, h).wait()
            p = exb[m, h]
            ds = p * dot_nt(gaa, va).astype(BF)
            outs.append(dot(ds, kvb[m, :, span]))
            hs = slice(64 * side, 64 * side + 64)
            dkvt[64 * h : 64 * h + 64, :] = dot(qt[hs, :], ds)
            dkvt[D + 64 * h : D + 64 * h + 64, :] = dot(gapt[hs, :], p)
        dqs.append((jnp.where(low, outs[0], outs[1]) * 0.125).astype(BF))
    dq = jnp.concatenate(dqs, 1)
    for k in range(4, 9):
        load(m, k).wait()
    for e in range(EXP):
        r = slice(CAP * e, CAP * e + CAP)
        dwq[:, D * e : D * e + D] += dot_tn(rowsb[m, r, :], dq[r])
    back = by_expert(lambda e, r: dot_nt(dq[r], wq[e])).astype(BF)
    lanes = by_expert(lambda e, r: split_lanes(t[r], e))
    acc = dot_tn(route, jnp.concatenate([back, lanes], 1))

    dl = router_grad(gates[0], acc[:, D:512])
    router = dot(sm[...], router_turn(sc, 0)).astype(BF)
    dkvb = dkvt[...].astype(BF)
    part = acc[:, 0:D] + dot_nt(dl, router) + dot_tn(dkvb, wkvt[...])
    tk = jnp.concatenate([r[m].astype(F32) for r in (tb0, tb1, tb2, tb3)], 0)
    n, _ = norm_parts(tk)
    x = (n * vec[0:1, :] + vec[1:2, :]).astype(BF)
    dvec[0:1, :] += jnp.sum(part * n, 0, keepdims=True)
    dvec[1:2, :] += jnp.sum(part, 0, keepdims=True)
    dsm[...] += dot_tn(x, dl)
    dwkvt[...] += dot(dkvb, x)
    for s, o in enumerate((o0, o1, o2, o3)):
        o[0] = part[SQ * s : SQ * s + SQ].astype(BF)

    @pl.when(m == MB - 1)
    def _():
        small = dot_nt(dsm[...].astype(BF), router_turn(sc, 0))
        small = small + dot_nt(rmlp[...].astype(BF), router_turn(sc, 12))
        vecs = jnp.concatenate(
            [jnp.zeros((24, D), F32), dvec[0:2, :], gv[0:2, :], jnp.zeros((100, D), F32)], 0
        ).astype(BF)
        small = (small + dot_nt(eye(D), vecs)).astype(BF)
        k, d = iota((512, 1), 0), iota((512, D), 1)
        r = k & 15
        own = hot(owned_feature(k, sc, True) == d)
        kvb = flip(dwkvt[...].astype(BF)).astype(BF)
        for e in range(EXP):
            span = slice(D * e, D * e + D)
            shared = hot(shared_feature(k >> 4, 4 * e + r - 12, r >= 12, sc, True) == d)
            weights = jnp.concatenate([dwq[:, span], dwo[:, span]], 1).astype(BF)
            wide = dot(jnp.concatenate([own, shared], 1), jnp.concatenate([weights, kvb], 0))
            wide = wide.astype(BF)
            rows = slice(16 * e, 16 * e + 16)
            for i, t in enumerate((ta0, ta1)):
                t[:, rows, 0:768] = wide[256 * i : 256 * i + 256].reshape(16, 16, 768)
            if e == 0:
                side = dot(hot(shared_feature(k >> 4, r, r < 12, sc, True) == d), small).astype(BF)
            else:
                side = jnp.zeros((512, 128), BF)
            for i, t in enumerate((ta0, ta1)):
                t[:, rows, 768:896] = side[256 * i : 256 * i + 256].reshape(16, 16, 128)


def attend_back(sc, gs, toks, posr, saved, wq, wo, wkvt, sm, vec, gv, rmlp):
    gates, kv, rows, q, att, br, rin, ex = saved
    late = [*toks, kv, rows, q, att, br, ex]
    piece = [(per_m(SQ, D), sds((MB, SQ, D), BF))] * 4
    outs = piece + [(full((16, 48, 896)), sds((16, 48, 896), BF))] * 2
    got = pl.pallas_call(
        attend_back_kernel,
        grid=(MB,),
        in_specs=[smem()]
        + [per_m(SQ, D)] * 4
        + [
            pl.BlockSpec((1, 1, 16, SLOTS), lambda m: (0, m, 0, 0)),
            per_m(SLOTS, 128), per_m(ROWS, 128),
            full((EXP, D, D)), full((EXP, D, D)), full((768, D)), full((D, 128)), full((8, D)),
            full((8, D)), full((D, 128)),
        ]
        + [pl.BlockSpec(memory_space=pl.ANY)] * len(late),
        out_specs=[o[0] for o in outs],
        out_shape=[o[1] for o in outs],
        scratch_shapes=[
            pltpu.VMEM((768, SLOTS), F32),
            pltpu.VMEM((D, EXP * D), F32),
            pltpu.VMEM((D, EXP * D), F32),
            pltpu.VMEM((768, D), F32),
            pltpu.VMEM((D, 128), F32),
            pltpu.VMEM((8, D), F32),
            pltpu.VMEM((MB, HEADS, ROWS, SLOTS), BF),
            pltpu.SemaphoreType.DMA((MB, HEADS)),
        ]
        + [pltpu.VMEM(v.shape, BF) for v in late[:-1]]
        + [pltpu.SemaphoreType.DMA((MB, 9))],
        compiler_params=params(1, 62),
        cost_estimate=cost(120),
        name="attend_back",
    )(sc, *gs, posr, gates, rin, wq, wo, wkvt, sm, vec, gv, rmlp, *late)
    return got[:4], got[4:]


def finish_kernel(gmix, tokens, p0, p1, p2, p3, vec, out):
    for m in range(MB):
        n, inv = norm_parts(tokens[m].astype(F32))
        grad = jnp.zeros((SQ, D), F32)
        for p in (p0, p1, p2, p3):
            grad = grad + p[m].astype(F32)
        out[m] = (gmix[m] + norm_back(grad, n, inv, vec[0:1, :])).astype(BF)


def finish(gmix, tokens, parts, vec):
    shape = (MB, SQ, D)
    return pl.pallas_call(
        finish_kernel,
        grid=(1,),
        in_specs=[full(shape)] * 6 + [full((8, D))],
        out_specs=full(shape),
        out_shape=sds(shape, BF),
        compiler_params=params(1, 8),
        cost_estimate=cost(2),
        name="finish",
    )(gmix, tokens, *parts, vec)


def shift(a, axis, s):
    n = lax.axis_size(axis)
    return lax.ppermute(a, axis, [(i, (i + s) % n) for i in range(n)])


def fetch(a, axis):
    one, three, two = [shift(a, axis, 4 - s) for s in (1, 3, 2)]
    return [a, one, two, three]


def send(parts, axis):
    two, one, three = [shift(parts[s], axis, s) for s in (2, 1, 3)]
    return [parts[0], one, two, three]


def add2(a, b):
    return (a.astype(F32) + b.astype(F32)).astype(BF)


def tie(*arrays):
    return lax.optimization_barrier(arrays)


def fold(a, axis):
    got = send([a[s] for s in range(a.shape[0])], axis)
    return sum(v.astype(F32) for v in got)


def local(
    tokens, patch_counts, attn_routes, mlp_routes, gain1, bias1, gain2, bias2, wkv, rattn, rmlp,
    wq, wo, wup, wdown, cotangent,
):
    tokens = tokens.reshape(MB, SQ, D)
    cot = cotangent.reshape(MB, SQ, D)
    index = [lax.axis_index(a) for a in ("x", "c", "z", "y")]
    sc = jnp.stack(index + [patch_counts[0, 0], patch_counts[1, 0], 0, 0]).astype(jnp.int32)

    shared, own, mlp_shard = pack(
        wkv, rattn, rmlp, gain1, bias1, gain2, bias2, wq, wo, wup, wdown,
        *[jnp.moveaxis(r.reshape(MB, SQ, 4), 1, 2) for r in (attn_routes, mlp_routes)],
    )
    got = fetch(shared, "x")
    kv12 = jnp.concatenate([v[0:3, 0:896] for v in got], 0)
    shard = jnp.concatenate([own[:, 0:12], kv12[:, :768].reshape(3, 4, 768)], 1).reshape(48, 768)
    shard = jnp.concatenate([shard, jnp.pad(kv12[:, 768:], ((0, 36), (0, 0)))], 1)
    zs = jnp.stack(fetch(shard, "z"))
    zs, sc = tie(zs, sc)
    posr, posc = plan(sc, got)
    pieces = fetch(zs, "y")
    toks = fetch(tokens, "x")
    both = tie(*pieces, *toks, posr, posc)
    pieces, toks, posr, posc = list(both[:4]), list(both[4:8]), both[8], both[9]
    pieces = pieces + [shift(p, "c", 1) for p in pieces]
    *pieces, mlp_shard = tie(*pieces, mlp_shard)
    wmlp = lax.all_gather(mlp_shard, TOKS, axis=0).reshape(32, EXP, 112, D)

    parts, saved, (fq, fo, fkvt, sm, vec) = attend(sc, toks, posr, posc, pieces)
    parts, cot = tie(parts, cot)
    gs = fetch(cot, "x")
    mixed, mlp_in = mix(tokens, send(parts, "x"), vec)
    xs = fetch(mlp_in, "x")
    outp, gradp, rm, (keep, give, down) = experts(sc, xs, gs, posr, posc, sm, wmlp)
    down = lax.psum_scatter(down, TOKS, scatter_dimension=0, tiled=True)
    give = shift(give, "c", 1)
    gradp = send(gradp, "x")
    up = add2(keep, give)
    *gradp, up = tie(*gradp, up)
    up = lax.all_to_all(up, ("z", "y"), 0, 0, tiled=True)
    gmix, gmixb, gv = turn(mixed, cot, gradp, vec)
    gms = fetch(gmixb, "x")
    back, (ta, ta1) = attend_back(sc, gms, toks, posr, saved, fq, fo, fkvt, sm, vec, gv, rm)
    ta1 = shift(ta1, "c", 1)
    ta1, back, outp = tie(ta1, back, outp)
    ta, up = tie(add2(ta, ta1), up)
    ta = lax.all_to_all(ta, ("z", "y"), 0, 0, tiled=True)
    back = send(back, "x")
    outp, back = tie(outp, back)
    outp = send(outp, "x")
    dup = jnp.sum(up.astype(F32), 0)[:, 0:12]
    tokens_grad = finish(gmix, tokens, back, vec)
    ta, dup, tokens_grad = tie(ta, dup, tokens_grad)
    ta = jnp.sum(ta.astype(F32), 0)
    ta, *outp = tie(ta, *outp)
    result = mixed
    for o in outp:
        result = result + o.astype(F32)
    result = result.astype(BF)
    t3 = ta.reshape(3, 16, 896)
    kv = jnp.concatenate([t3[:, 12:16, :768].reshape(12, 768), ta[0:12, 768:]], 1)
    small = fold(kv.astype(BF).reshape(4, 3, 896), "x")
    small, down = tie(small, down)

    ddown = down.astype(F32).reshape(EXP, 48, D)
    dq, do = t3[:, :12, :D], t3[:, :12, D:768]
    shape = (MB, 1, SQ, D)
    return (
        result.reshape(shape),
        tokens_grad.reshape(shape),
        small[:, 792],
        small[:, 793],
        small[:, 794],
        small[:, 795],
        small[:, 0:768],
        small[:, 768:780],
        small[:, 780:792],
        dq,
        do,
        dup,
        ddown,
    )


def solution(mesh):
    fine = Mesh(mesh.devices.reshape(4, 4, 2, 4), ("z", "y", "c", "x"))
    every = TOKS + ("x",)
    act = P(None, TOKS, "x", None)
    row, mat, own = P(every), P(every, None), P("x", TOKS, None)
    return jax.shard_map(
        local,
        mesh=fine,
        in_specs=(
            act, P(None, TOKS), act, act, row, row, row, row, mat, mat, mat, own, own, own, own, act,
        ),
        out_specs=(act, act, row, row, row, row, mat, mat, mat, own, own, own, own),
        check_vma=False,
    )
```

```python
import jax
import jax.numpy as jnp
from jax import lax
from jax.experimental import pallas as pl
from jax.experimental.pallas import tpu as pltpu
from jax.sharding import Mesh, PartitionSpec as P

BF = jnp.bfloat16
F32 = jnp.float32
EPSILON = 1e-06
MASKED = -1e30
MB, NX, SQ, SLOTS, D = 2, 4, 144, 576, 384
EXP, CAP, HEADS, FF = 3, 256, 6, 1536
PACK = 160
TOKS = ("z", "y", "c")
VMEM = 62 * 1024 * 1024


def params(n, mib=60):
    return pltpu.CompilerParams(
        dimension_semantics=("arbitrary",) * n, vmem_limit_bytes=mib * 1024 * 1024
    )


def cost(us):
    return pl.CostEstimate(flops=int(us * 1e9), bytes_accessed=0, transcendentals=0)


def dot(a, b):
    return jnp.dot(a, b, preferred_element_type=F32)


def dot_nt(a, b):
    return lax.dot_general(a, b, (((1,), (1,)), ((), ())), preferred_element_type=F32)


def dot_tn(a, b):
    return lax.dot_general(a, b, (((0,), (0,)), ((), ())), preferred_element_type=F32)


def iota(shape, dim):
    return lax.broadcasted_iota(jnp.int32, shape, dim)


def hot(cond):
    return jnp.where(cond, 1.0, 0.0).astype(BF)


def eye(n):
    return hot(iota((n, n), 0) == iota((n, n), 1))


def flip(a):
    return dot_nt(eye(a.shape[1]), a)


def tok_of(place, sc, plain=False):
    c = (sc[1] + (place >> 4)) & 1
    if plain:
        return (place & 15) * 2 + c
    z = (sc[2] + (place & 3)) & 3
    y = (sc[3] + ((place >> 2) & 3)) & 3
    return z * 8 + y * 2 + c


def third(v):
    return (v * 11) >> 5


def owned_feature(k, sc, plain=False):
    r = k & 15
    return jnp.where(r < 12, tok_of(k >> 4, sc, plain) * 12 + r, -1)


def shared_feature(place, idx, valid, sc, plain=False):
    s = third(idx)
    feature = tok_of(place, sc, plain) * 12 + ((sc[0] + s) & 3) * 3 + idx - 3 * s
    return jnp.where(valid, feature, -1)


def canonical_feature(col):
    r = col & 15
    return jnp.where(r < 12, (col >> 4) * 12 + r, -1)


def native_lane(sc):
    j = iota((1, 128), 1)
    n = j + 3 * sc[0]
    n = jnp.where(n >= 12, n - 12, n)
    return jnp.where(j < 12, n, -1)


def router_turn(sc, offset):
    n = native_lane(sc)
    return hot((iota((128, 128), 0) == n + offset) & (n >= 0))


def norm_parts(x):
    mu = jnp.mean(x, -1, keepdims=True)
    c = x - mu
    var = jnp.mean(c * c, -1, keepdims=True)
    inv = lax.rsqrt(var + EPSILON)
    return c * inv, inv


def norm_back(grad, normed, inv, gain):
    u = grad * gain
    a = jnp.mean(u, -1, keepdims=True)
    b = jnp.mean(u * normed, -1, keepdims=True)
    return (u - a - normed * b) * inv


def soft_gates(posc, x, router):
    inside = posc >= 0.0
    logits = jnp.where(inside, dot(x, router), MASKED)
    top = jnp.max(logits, -1, keepdims=True)
    ex = jnp.where(inside, jnp.exp(logits - top), 0.0)
    return ex / jnp.sum(ex, -1, keepdims=True)


def gate_lanes(gates):
    hi = gates.astype(BF).astype(F32)
    lo = pltpu.roll(gates - hi, 64, 1)
    return jnp.where(iota(gates.shape, 1) < 64, hi, lo).astype(BF)


def pick(ext, e):
    lane = iota(ext.shape, 1)
    return jnp.sum(jnp.where((lane == e) | (lane == 64 + e), ext, 0.0), -1, keepdims=True)


def split_lanes(col, e):
    hi = col.astype(BF).astype(F32)
    lane = iota((col.shape[0], 128), 1)
    both = jnp.where(lane == e, hi, 0.0) + jnp.where(lane == 64 + e, col - hi, 0.0)
    return both.astype(BF)


def gather_matrix(row):
    return hot(row == iota((CAP, SLOTS), 0).astype(F32))


def router_grad(gates, lanes):
    t = lanes + pltpu.roll(lanes, 64, 1)
    inner = jnp.sum(gates * t, -1, keepdims=True)
    return (gates * (t - inner)).astype(BF)


def smem():
    return pl.BlockSpec(memory_space=pltpu.SMEM)


def full(shape):
    return pl.BlockSpec(shape, lambda *_: (0,) * len(shape))


def sds(shape, dtype):
    return jax.ShapeDtypeStruct(shape, dtype)


def pack_kernel(
    wkv, rattn, rmlp, g1, b1, g2, b2, wq, wo, wup, wdown, ra, rm, tokens, cot,
    shared, own, mlp, joined,
):
    joined[:, 0:SQ, :] = tokens[...]
    joined[:, SQ : 2 * SQ, :] = cot[...]
    shared[...] = jnp.zeros_like(shared)
    own[...] = jnp.zeros_like(own)
    mlp[...] = jnp.zeros_like(mlp)
    shared[0:3, 0:768] = wkv[...]
    shared[0:3, 768:780] = rattn[...]
    shared[0:3, 780:792] = rmlp[...]
    lane, row = iota((3, 3), 1), iota((3, 3), 0)
    cols = []
    for v in (g1, b1, g2, b2):
        line = v[...].astype(F32).reshape(1, 3)
        cols.append(jnp.sum(jnp.where(lane == row, line, 0.0), -1, keepdims=True))
    shared[0:3, 792:796] = jnp.concatenate(cols, 1).astype(BF)
    routes = jnp.zeros((16, SQ), F32)
    for m in range(MB):
        for i, r in enumerate((ra, rm)):
            put = hot(iota((16, 4), 0) == iota((16, 4), 1) + 8 * i + 4 * m)
            routes = routes + dot(put, r[m].astype(F32).astype(BF))
    shared[:, 1024 : 1024 + SQ] = routes.astype(BF)
    for e in range(EXP):
        own[e, 0:12, 0:D] = wq[e]
        own[e, 0:12, D : 2 * D] = wo[e]
        for g in range(4):
            mlp[e, 16 * g : 16 * g + 12, :] = wup[e, :, D * g : D * g + D]
        mlp[e, 64:112, :] = wdown[e]


def pack(*args):
    shapes = [(16, 1280), (EXP, 16, 768), (EXP, 112, D), (MB, 2 * SQ, D)]
    return pl.pallas_call(
        pack_kernel,
        grid=(1,),
        in_specs=[full(v.shape) for v in args],
        out_specs=[full(v) for v in shapes],
        out_shape=[sds(v, BF) for v in shapes],
        compiler_params=params(1, 62),
        cost_estimate=cost(2),
        name="pack",
    )(*args)


def plan_kernel(sc, r0, r1, r2, r3, posr, posc):
    unit = hot(iota((SQ, 256), 0) == iota((SQ, 256), 1))
    rcol = jnp.concatenate([dot_nt(unit, r[...]) for r in (r0, r1, r2, r3)], 0)
    nat = native_lane(sc).astype(F32)
    lower = hot(iota((SLOTS, SLOTS), 1) < iota((SLOTS, SLOTS), 0))
    unit = hot(iota((16, 128), 0) == iota((16, 128), 1))
    for i in range(2 * MB):
        member = jnp.zeros((SLOTS, 128), F32)
        for k in range(4 * i, 4 * i + 4):
            member = member + jnp.where(rcol[:, k : k + 1] == nat, 1.0, 0.0)
        mb = member.astype(BF)
        mt = dot_nt(unit, mb)
        posc[i // MB, i % MB] = jnp.where(member > 0.5, dot(lower, mb), -1.0)
        posr[i // MB, i % MB] = jnp.where(mt > 0.5, dot_nt(mt.astype(BF), lower), -1.0)


def plan(sc, pieces):
    return pl.pallas_call(
        plan_kernel,
        grid=(1,),
        in_specs=[smem()] + [pl.BlockSpec((16, 256), lambda i: (0, 4))] * 4,
        out_specs=[full((2, MB, 16, SLOTS)), full((2, MB, SLOTS, 128))],
        out_shape=[sds((2, MB, 16, SLOTS), F32), sds((2, MB, SLOTS, 128), F32)],
        compiler_params=params(1, 62),
        cost_estimate=cost(4),
        name="plan",
    )(sc, *pieces)


def prepare(sc, pieces, wq, wo, wkv, wkvt, sm, vec):
    def gathered(rows, lanes):
        return jnp.concatenate([p[:, rows, lanes].reshape(-1, lanes.stop - lanes.start) for p in pieces], 0)

    take = hot(iota((D, 512), 0) == owned_feature(iota((1, 512), 1), sc))
    for e in range(EXP):
        nat = dot(take, gathered(slice(16 * e, 16 * e + 16), slice(0, 768))).astype(BF)
        wq[e] = nat[:, :D]
        wo[e] = nat[:, D:]
    k = iota((1, 1536), 1)
    place = (k * 1366) >> 16
    r48 = k - place * 48
    r16 = r48 & 15
    kv_feature = shared_feature(place, (r48 >> 4) * 4 + r16 - 12, r16 >= 12, sc)
    kv = dot(hot(iota((D, 1536), 0) == kv_feature), gathered(slice(0, 48), slice(0, 768))).astype(BF)
    wkv[...] = kv
    wkvt[...] = kv.T
    k = iota((1, 512), 1)
    sm_feature = shared_feature(k >> 4, k & 15, (k & 15) < 12, sc)
    side = gathered(slice(0, 16), slice(768, 896))
    small = dot(hot(iota((D, 512), 0) == sm_feature), side).astype(BF)
    sm[...] = small
    vec[...] = dot_nt(hot(iota((8, 128), 1) == iota((8, 128), 0) + 24), small)


ROWS = EXP * CAP


def gather_all(posr):
    return jnp.concatenate([gather_matrix(posr[e : e + 1, :]) for e in range(EXP)], 0)


def turned(ref, s, sc):
    return ref[pl.ds((sc[0] + s) & 3, 1)][0]


def by_expert(f):
    return jnp.concatenate([f(e, slice(CAP * e, CAP * e + CAP)) for e in range(EXP)], 0)


def own_half(rows, side):
    lane = iota((rows, 128), 1)
    return lane < 64 if side == 0 else lane >= 64


def spare(side):
    return 64 if side == 0 else 0


def keep_lanes(side):
    return hot(own_half(1, side))


def with_ones(v, side):
    lane, at = iota((1, 128), 1), spare(side)
    return v * keep_lanes(side) + hot((lane == at) | (lane == at + 1))


def attend_kernel(
    sc, tall, pr, pc, w0, w1, w2, w3, w4, w5, w6, w7,
    o0, o1, o2, o3, gateo, kvo, rowso, qo, atto, bro, rin,
    wq, wo, wkvt, sm, vec, exo, exb, sem, wkv,
):
    m = pl.program_id(0)

    @pl.when(m == 0)
    def _():
        prepare(sc, (w0, w1, w2, w3, w4, w5, w6, w7), wq, wo, wkv, wkvt, sm, vec)

    def out_copy(i, h):
        return pltpu.make_async_copy(exb.at[h], exo.at[i, h], sem.at[h])

    @pl.when(m > 0)
    def _():
        for h in range(HEADS):
            out_copy(m - 1, h).wait()

    x = jnp.concatenate([turned(tall, s, sc)[0].astype(F32) for s in range(4)], 0)
    n, _ = norm_parts(x)
    a = (n * vec[0:1, :] + vec[1:2, :]).astype(BF)
    router = dot(sm[...], router_turn(sc, 0)).astype(BF)
    posr, posc = pr[0, 0], pc[0, 0]
    gates = soft_gates(posc, a, router)
    gateo[0] = gates
    kv = dot(a, wkv[...]).astype(BF)
    kvo[0] = kv

    route = gather_all(posr)
    ext = dot(route, jnp.concatenate([a, gate_lanes(gates)], 1))
    rows = ext[:, 0:D].astype(BF)
    gate = by_expert(lambda e, r: pick(ext[r, D:512], e))
    rowso[0] = rows
    q = by_expert(lambda e, r: dot(rows[r], wq[e])).astype(BF)
    q = q * jnp.asarray(0.125, BF)
    qo[0] = q
    slot = iota((SLOTS, 1), 0) + SQ * sc[0]
    slot = jnp.where(slot >= SLOTS, slot - SLOTS, slot)
    bias = jnp.where(slot < sc[4 + m], 0.0, MASKED)
    lane = iota((ROWS, 128), 1)
    biases = [
        jnp.where(iota((SLOTS, 128), 1) == spare(side), bias, 0.0).astype(BF) for side in range(2)
    ]
    inv_lanes = jnp.zeros((ROWS, 128), F32)
    for hp in range(3):
        span = slice(128 * hp, 128 * hp + 128)
        halves = []
        for side in range(2):
            h = 2 * hp + side
            at = spare(side)
            ka = kv[:, span] * keep_lanes(side) + biases[side]
            qa = q[:, span] * keep_lanes(side) + hot(iota((1, 128), 1) == at)
            va = with_ones(kv[:, D + 128 * hp : D + 128 * hp + 128], side)
            s = dot_nt(qa, ka)
            ex = jnp.exp(s - jnp.max(s, -1, keepdims=True)).astype(BF)
            exb[h] = ex
            out_copy(m, h).start()
            pv = dot(ex, va)
            inv = 1.0 / pv[:, at : at + 1]
            inv_lanes = jnp.where(lane == h, inv, inv_lanes)
            halves.append(pv * inv)
        atto[0, :, span] = jnp.where(lane < 64, halves[0], halves[1]).astype(BF)
    rin[0] = jnp.where(lane == 8, gate, inv_lanes)
    br = by_expert(lambda e, r: dot(atto[0, r, :], wo[e])).astype(BF)
    bro[0] = br
    acc = dot_tn(route, (gate * br.astype(F32)).astype(BF))
    for s, o in enumerate((o0, o1, o2, o3)):
        o[0] = acc[SQ * s : SQ * s + SQ, :].astype(BF)

    @pl.when(m == MB - 1)
    def _():
        for h in range(HEADS):
            out_copy(m, h).wait()


def per_m(*shape):
    return pl.BlockSpec((1,) + shape, lambda m: (m,) + (0,) * len(shape))


def attend(sc, tall, posr, posc, pieces):
    saved = [
        (SLOTS, 128, F32),
        (SLOTS, 768, BF),
        (ROWS, D, BF),
        (ROWS, D, BF),
        (ROWS, D, BF),
        (ROWS, D, BF),
        (ROWS, 128, F32),
    ]
    outs = [(SQ, D, BF)] * 4 + saved
    kept = (MB, HEADS, ROWS, SLOTS)
    shared = [
        ((EXP, D, D), BF), ((EXP, D, D), BF), ((768, D), BF), ((D, 128), BF),
        ((8, D), F32),
    ]
    out = pl.pallas_call(
        attend_kernel,
        grid=(MB,),
        in_specs=[smem()]
        + [
            pl.BlockSpec((4, 1, SQ, D), lambda m: (0, m, 0, 0)),
            pl.BlockSpec((1, 1, 16, SLOTS), lambda m: (0, m, 0, 0)),
            pl.BlockSpec((1, 1, SLOTS, 128), lambda m: (0, m, 0, 0)),
        ]
        + [full((4, 48, 896))] * 8,
        out_specs=[per_m(*o[:-1]) for o in outs]
        + [full(v[0]) for v in shared]
        + [pl.BlockSpec(memory_space=pl.ANY)],
        out_shape=[sds((MB,) + o[:-1], o[-1]) for o in outs]
        + [sds(*v) for v in shared]
        + [sds(kept, BF)],
        scratch_shapes=[
            pltpu.VMEM(kept[1:], BF),
            pltpu.SemaphoreType.DMA((HEADS,)),
            pltpu.VMEM((D, 768), BF),
        ],
        compiler_params=params(1, 62),
        cost_estimate=cost(24),
        name="attend",
    )(sc, tall, posr, posc, *pieces)
    n = len(outs)
    return out[:4], out[4:n] + out[-1:], out[n:-1]


def mix_kernel(t, p0, p1, p2, p3, vec, mixed, mlp_in):
    for m in range(MB):
        x = t[m].astype(F32)
        for p in (p0, p1, p2, p3):
            x = x + p[m].astype(F32)
        mixed[m] = x
        n, _ = norm_parts(x)
        mlp_in[m] = (n * vec[2:3, :] + vec[3:4, :]).astype(BF)


def mix(tokens, parts, vec):
    shape = (MB, SQ, D)
    return pl.pallas_call(
        mix_kernel,
        grid=(1,),
        in_specs=[full(shape)] * 5 + [full((8, D))],
        out_specs=[full(shape)] * 2,
        out_shape=[sds(shape, F32), sds(shape, BF)],
        compiler_params=params(1, 8),
        cost_estimate=cost(2),
        name="mix",
    )(tokens, *parts, vec)


def gelu_both(v):
    phi = 0.5 + 0.5 * lax.erf(v * 0.7071067811865476)
    density = jnp.exp(-0.5 * (v * v)) * 0.3989422804014327
    return v * phi, phi + v * density


FC = 768


def experts_kernel(
    sc, x0, x1, x2, x3, tall, posr, posc, sm, w_any,
    oo0, oo1, oo2, oo3, og0, og1, og2, og3, rmlp, keep, give, down,
    xe, gates, acc, hids, gps, dw, wbuf, sem,
):
    e = pl.program_id(0)

    def fetch_weights(i):
        return pltpu.make_async_copy(w_any.at[:, i], wbuf.at[i], sem.at[i])

    @pl.when(e == 0)
    def _():
        for i in range(EXP):
            fetch_weights(i).start()

    @pl.when(e == 0)
    def _():
        turn = dot(sm[...], router_turn(sc, 12)).astype(BF)
        pad = hot(iota((D, 512), 0) == canonical_feature(iota((1, 512), 1)))
        for m in range(MB):
            a = jnp.concatenate([x[m] for x in (x0, x1, x2, x3)], 0)
            gt = soft_gates(posc[0, m], a, turn)
            gates[m] = gt
            xe[m, :, 0:512] = dot(a, pad).astype(BF)
            xe[m, :, 512:640] = gate_lanes(gt)
            xe[m, :, 640:1024] = jnp.concatenate(
                [turned(tall, s, sc)[m] for s in range(4)], 0
            )
        acc[...] = jnp.zeros_like(acc)

    routes = [gather_matrix(posr[0, m, pl.ds(e, 1), :]) for m in range(MB)]
    ext = jnp.concatenate([dot(routes[m], xe[m]) for m in range(MB)], 0)
    gr = ext[:, 640:1024]
    rows = ext[:, 0:512].astype(BF)
    gate = pick(ext[:, 512:640], e)
    gb = (gate * gr).astype(BF)
    branch = jnp.zeros((512, D), F32)
    back = jnp.zeros((512, 512), F32)
    fetch_weights(e).wait()
    w_ref = wbuf.at[e]
    for c in range(FF // FC):
        span = slice(c * FC, c * FC + FC)
        w = jnp.concatenate(
            [w_ref[:, 16 * g : 16 * g + 16, :].reshape(512, D) for g in (2 * c, 2 * c + 1)], 1
        )
        wd = w_ref[16 * c : 16 * c + 16, 64:112, :].reshape(FC, D)
        act, slope = gelu_both(dot(rows, w))
        hid = act.astype(BF)
        gp = (dot_nt(gb, wd) * slope).astype(BF)
        hids[:, span] = hid
        gps[:, span] = gp
        branch = branch + dot(hid, wd)
        back = back + dot_nt(gp, w)
    br = branch.astype(BF).astype(F32)
    t = jnp.sum(gr * br, -1, keepdims=True)
    scaled = (gate * br).astype(BF)
    lanes = split_lanes(t, e)
    backb = back.astype(BF)
    for m in range(MB):
        r = slice(CAP * m, CAP * m + CAP)
        acc[m] += dot_tn(routes[m], jnp.concatenate([scaled[r], lanes[r], backb[r]], 1))
    dw[...] = dot_tn(rows, gps[...]).astype(BF).reshape(32, 16, FF)
    down[:, 0] = dot_tn(hids[...], gb).astype(BF).reshape(32, 48, D)
    for p in range(16):
        keep[p, 0] = dw[pl.ds(2 * p + sc[1], 1)][0]
        give[p, 0] = dw[pl.ds(2 * p + 1 - sc[1], 1)][0]

    @pl.when(e == EXP - 1)
    def _():
        turn = dot(sm[...], router_turn(sc, 12)).astype(BF)
        pad = hot(iota((D, 512), 0) == canonical_feature(iota((1, 512), 1)))
        total = jnp.zeros((D, 128), F32)
        for m in range(MB):
            dl = router_grad(gates[m], acc[m, :, D:512])
            a = jnp.concatenate([x[m] for x in (x0, x1, x2, x3)], 0)
            total = total + dot_tn(a, dl)
            part = dot_nt(acc[m, :, 512:1024].astype(BF), pad) + dot_nt(dl, turn)
            for s, (o, og) in enumerate(zip((oo0, oo1, oo2, oo3), (og0, og1, og2, og3))):
                r = slice(SQ * s, SQ * s + SQ)
                o[m] = acc[m, r, 0:D].astype(BF)
                og[m] = part[r].astype(BF)
        rmlp[...] = total


def experts(sc, xs, tall, posr, posc, sm, wmlp):
    piece = (full((MB, SQ, D)), sds((MB, SQ, D), BF))
    half = pl.BlockSpec((16, 1, 16, FF), lambda e: (0, e, 0, 0))
    outs = [piece] * 8 + [
        (full((D, 128)), sds((D, 128), F32)),
        (half, sds((16, EXP, 16, FF), BF)),
        (half, sds((16, EXP, 16, FF), BF)),
        (pl.BlockSpec((32, 1, 48, D), lambda e: (0, e, 0, 0)), sds((32, EXP, 48, D), BF)),
    ]
    got = pl.pallas_call(
        experts_kernel,
        grid=(EXP,),
        in_specs=[smem()]
        + [full((MB, SQ, D))] * 4
        + [
            pl.BlockSpec((4, MB, SQ, D), lambda e: (0, 0, 1, 0)),
            pl.BlockSpec((1, MB, 16, SLOTS), lambda e: (1, 0, 0, 0)),
            pl.BlockSpec((1, MB, SLOTS, 128), lambda e: (1, 0, 0, 0)),
            full((D, 128)),
            pl.BlockSpec(memory_space=pl.ANY),
        ],
        out_specs=[o[0] for o in outs],
        out_shape=[o[1] for o in outs],
        scratch_shapes=[
            pltpu.VMEM((MB, SLOTS, 1024), BF),
            pltpu.VMEM((MB, SLOTS, 128), F32),
            pltpu.VMEM((MB, SLOTS, 1024), F32),
            pltpu.VMEM((512, FF), BF),
            pltpu.VMEM((512, FF), BF),
            pltpu.VMEM((32, 16, FF), BF),
            pltpu.VMEM((EXP, 32, 112, D), BF),
            pltpu.SemaphoreType.DMA((EXP,)),
        ],
        compiler_params=params(1, 62),
        cost_estimate=cost(30),
        name="experts",
    )(sc, *xs, tall, posr, posc, sm, wmlp)
    return got[:4], got[4:8], got[8], got[9:]


def turn_kernel(mixed, cot, p0, p1, p2, p3, vec, gmix, gmixb, gv):
    rows = [jnp.zeros((1, D), F32)] * 2
    for m in range(MB):
        n, inv = norm_parts(mixed[m])
        grad = jnp.zeros((SQ, D), F32)
        for p in (p0, p1, p2, p3):
            grad = grad + p[m].astype(F32)
        gm = cot[m].astype(F32) + norm_back(grad, n, inv, vec[2:3, :])
        gmix[m] = gm
        gmixb[m] = gm.astype(BF)
        rows[0] = rows[0] + jnp.sum(grad * n, 0, keepdims=True)
        rows[1] = rows[1] + jnp.sum(grad, 0, keepdims=True)
    gv[...] = jnp.concatenate(rows + [jnp.zeros((6, D), F32)], 0)


def turn(mixed, cot, parts, vec):
    shape = (MB, SQ, D)
    return pl.pallas_call(
        turn_kernel,
        grid=(1,),
        in_specs=[full(shape)] * 6 + [full((8, D))],
        out_specs=[full(shape), full(shape), full((8, D))],
        out_shape=[sds(shape, F32), sds(shape, BF), sds((8, D), F32)],
        compiler_params=params(1, 8),
        cost_estimate=cost(3),
        name="turn",
    )(mixed, cot, *parts, vec)


def attend_back_kernel(
    sc, g0, g1, g2, g3, posr, gates, rin, wq, wo, wkvt, sm, vec, gv, rmlp,
    tall, kv_, rows_, q_, att_, br_, exi,
    o0, o1, o2, o3, ta0, ta1,
    dkvt, dwq, dwo, dwkvt, dsm, dvec, exb, sem,
    tb0, tb1, tb2, tb3, kvb, rowsb, qb, attb, brb, late,
):
    m = pl.program_id(0)
    moved = (
        (br_, brb), (att_, attb), (q_, qb), (kv_, kvb), (rows_, rowsb),
    )
    tb = (tb0, tb1, tb2, tb3)

    def load(i, k):
        if k < 5:
            src, dst = moved[k][0].at[i], moved[k][1].at[i]
        else:
            src, dst = tall.at[(sc[0] + k - 5) & 3, i, pl.ds(0, SQ)], tb[k - 5].at[i]
        return pltpu.make_async_copy(src, dst, late.at[i, k])

    def load_all(i):
        for k in range(4):
            load(i, k).start()
        for h in range(HEADS):
            in_copy(i, h).start()
        for k in range(4, 9):
            load(i, k).start()

    def in_copy(i, h):
        return pltpu.make_async_copy(exi.at[i, h], exb.at[i, h], sem.at[i, h])

    @pl.when(m == 0)
    def _():
        load_all(0)
        dwq[...] = jnp.zeros_like(dwq)
        dwo[...] = jnp.zeros_like(dwo)
        dwkvt[...] = jnp.zeros_like(dwkvt)
        dsm[...] = jnp.zeros_like(dsm)
        dvec[...] = jnp.zeros_like(dvec)

    gin = jnp.concatenate([g[0] for g in (g0, g1, g2, g3)], 0)
    route = gather_all(posr[0, 0])
    gr = dot(route, gin)
    gb = (rin[0, :, 8:9] * gr).astype(BF)
    for k in range(4):
        load(m, k).wait()
    t = jnp.sum(gr * brb[m].astype(F32), -1, keepdims=True)
    ga = by_expert(lambda e, r: dot_nt(gb[r], wo[e])).astype(BF)
    for e in range(EXP):
        r = slice(CAP * e, CAP * e + CAP)
        dwo[:, D * e : D * e + D] += dot_tn(attb[m, r, :], gb[r])
    lane = iota((ROWS, 128), 1)
    low = lane < 64
    dqs = []

    @pl.when(m == 0)
    def _():
        load_all(1)

    for hp in range(3):
        span = slice(128 * hp, 128 * hp + 128)
        inv = jnp.where(low, rin[0, :, 2 * hp : 2 * hp + 1], rin[0, :, 2 * hp + 1 : 2 * hp + 2])
        gap = ga[:, span].astype(F32) * inv
        inner = gap * attb[m, :, span].astype(F32)
        gapt = flip(gap.astype(BF)).astype(BF)
        qt = flip(qb[m, :, span]).astype(BF)
        outs = []
        for side in range(2):
            h = 2 * hp + side
            at = spare(side)
            own = own_half(ROWS, side)
            ri = jnp.sum(jnp.where(own, inner, 0.0), -1, keepdims=True)
            hi = ri.astype(BF).astype(F32)
            rest = jnp.where(lane == at, -hi, jnp.where(lane == at + 1, hi - ri, 0.0))
            gaa = jnp.where(own, gap, rest).astype(BF)
            va = with_ones(kvb[m, :, D + 128 * hp : D + 128 * hp + 128], side)
            in_copy(m, h).wait()
            p = exb[m, h]
            ds = p * dot_nt(gaa, va).astype(BF)
            outs.append(dot(ds, kvb[m, :, span]))
            hs = slice(64 * side, 64 * side + 64)
            dkvt[64 * h : 64 * h + 64, :] = dot(qt[hs, :], ds)
            dkvt[D + 64 * h : D + 64 * h + 64, :] = dot(gapt[hs, :], p)
        dqs.append((jnp.where(low, outs[0], outs[1]) * 0.125).astype(BF))
    dq = jnp.concatenate(dqs, 1)
    for k in range(4, 9):
        load(m, k).wait()
    for e in range(EXP):
        r = slice(CAP * e, CAP * e + CAP)
        dwq[:, D * e : D * e + D] += dot_tn(rowsb[m, r, :], dq[r])
    back = by_expert(lambda e, r: dot_nt(dq[r], wq[e])).astype(BF)
    lanes = by_expert(lambda e, r: split_lanes(t[r], e))
    acc = dot_tn(route, jnp.concatenate([back, lanes], 1))

    dl = router_grad(gates[0], acc[:, D:512])
    router = dot(sm[...], router_turn(sc, 0)).astype(BF)
    dkvb = dkvt[...].astype(BF)
    part = acc[:, 0:D] + dot_nt(dl, router) + dot_tn(dkvb, wkvt[...])
    tk = jnp.concatenate([r[m].astype(F32) for r in (tb0, tb1, tb2, tb3)], 0)
    n, _ = norm_parts(tk)
    x = (n * vec[0:1, :] + vec[1:2, :]).astype(BF)
    dvec[0:1, :] += jnp.sum(part * n, 0, keepdims=True)
    dvec[1:2, :] += jnp.sum(part, 0, keepdims=True)
    dsm[...] += dot_tn(x, dl)
    dwkvt[...] += dot(dkvb, x)
    for s, o in enumerate((o0, o1, o2, o3)):
        o[0] = part[SQ * s : SQ * s + SQ].astype(BF)

    @pl.when(m == MB - 1)
    def _():
        small = dot_nt(dsm[...].astype(BF), router_turn(sc, 0))
        small = small + dot_nt(rmlp[...].astype(BF), router_turn(sc, 12))
        vecs = jnp.concatenate(
            [jnp.zeros((24, D), F32), dvec[0:2, :], gv[0:2, :], jnp.zeros((100, D), F32)], 0
        ).astype(BF)
        small = (small + dot_nt(eye(D), vecs)).astype(BF)
        k, d = iota((512, 1), 0), iota((512, D), 1)
        r = k & 15
        own = hot(owned_feature(k, sc, True) == d)
        kvb = flip(dwkvt[...].astype(BF)).astype(BF)
        for e in range(EXP):
            span = slice(D * e, D * e + D)
            shared = hot(shared_feature(k >> 4, 4 * e + r - 12, r >= 12, sc, True) == d)
            weights = jnp.concatenate([dwq[:, span], dwo[:, span]], 1).astype(BF)
            wide = dot(jnp.concatenate([own, shared], 1), jnp.concatenate([weights, kvb], 0))
            wide = wide.astype(BF)
            rows = slice(16 * e, 16 * e + 16)
            for i, t in enumerate((ta0, ta1)):
                t[:, rows, 0:768] = wide[256 * i : 256 * i + 256].reshape(16, 16, 768)
            if e == 0:
                side = dot(hot(shared_feature(k >> 4, r, r < 12, sc, True) == d), small).astype(BF)
            else:
                side = jnp.zeros((512, 128), BF)
            for i, t in enumerate((ta0, ta1)):
                t[:, rows, 768:896] = side[256 * i : 256 * i + 256].reshape(16, 16, 128)


def attend_back(sc, gs, tall, posr, saved, wq, wo, wkvt, sm, vec, gv, rmlp):
    gates, kv, rows, q, att, br, rin, ex = saved
    late = [tall, kv, rows, q, att, br, ex]
    piece = [(per_m(SQ, D), sds((MB, SQ, D), BF))] * 4
    outs = piece + [(full((16, 48, 896)), sds((16, 48, 896), BF))] * 2
    got = pl.pallas_call(
        attend_back_kernel,
        grid=(MB,),
        in_specs=[smem()]
        + [per_m(SQ, D)] * 4
        + [
            pl.BlockSpec((1, 1, 16, SLOTS), lambda m: (0, m, 0, 0)),
            per_m(SLOTS, 128), per_m(ROWS, 128),
            full((EXP, D, D)), full((EXP, D, D)), full((768, D)), full((D, 128)), full((8, D)),
            full((8, D)), full((D, 128)),
        ]
        + [pl.BlockSpec(memory_space=pl.ANY)] * len(late),
        out_specs=[o[0] for o in outs],
        out_shape=[o[1] for o in outs],
        scratch_shapes=[
            pltpu.VMEM((768, SLOTS), F32),
            pltpu.VMEM((D, EXP * D), F32),
            pltpu.VMEM((D, EXP * D), F32),
            pltpu.VMEM((768, D), F32),
            pltpu.VMEM((D, 128), F32),
            pltpu.VMEM((8, D), F32),
            pltpu.VMEM((MB, HEADS, ROWS, SLOTS), BF),
            pltpu.SemaphoreType.DMA((MB, HEADS)),
        ]
        + [pltpu.VMEM((MB, SQ, D), BF)] * 4
        + [pltpu.VMEM(v.shape, BF) for v in late[1:-1]]
        + [pltpu.SemaphoreType.DMA((MB, 9))],
        compiler_params=params(1, 62),
        cost_estimate=cost(120),
        name="attend_back",
    )(sc, *gs, posr, gates, rin, wq, wo, wkvt, sm, vec, gv, rmlp, *late)
    return got[:4], got[4:]


def finish_kernel(gmix, tokens, p0, p1, p2, p3, vec, out):
    for m in range(MB):
        n, inv = norm_parts(tokens[m].astype(F32))
        grad = jnp.zeros((SQ, D), F32)
        for p in (p0, p1, p2, p3):
            grad = grad + p[m].astype(F32)
        out[m] = (gmix[m] + norm_back(grad, n, inv, vec[0:1, :])).astype(BF)


def finish(gmix, tokens, parts, vec):
    shape = (MB, SQ, D)
    return pl.pallas_call(
        finish_kernel,
        grid=(1,),
        in_specs=[full(shape)] * 6 + [full((8, D))],
        out_specs=full(shape),
        out_shape=sds(shape, BF),
        compiler_params=params(1, 8),
        cost_estimate=cost(2),
        name="finish",
    )(gmix, tokens, *parts, vec)


def shift(a, axis, s):
    n = lax.axis_size(axis)
    return lax.ppermute(a, axis, [(i, (i + s) % n) for i in range(n)])


def fetch(a, axis):
    one, three, two = [shift(a, axis, 4 - s) for s in (1, 3, 2)]
    return [a, one, two, three]


def send(parts, axis):
    two, one, three = [shift(parts[s], axis, s) for s in (2, 1, 3)]
    return [parts[0], one, two, three]


def add2(a, b):
    return (a.astype(F32) + b.astype(F32)).astype(BF)


def tie(*arrays):
    return lax.optimization_barrier(arrays)


def fold(a, axis):
    got = send([a[s] for s in range(a.shape[0])], axis)
    return sum(v.astype(F32) for v in got)


def local(
    tokens, patch_counts, attn_routes, mlp_routes, gain1, bias1, gain2, bias2, wkv, rattn, rmlp,
    wq, wo, wup, wdown, cotangent,
):
    tokens = tokens.reshape(MB, SQ, D)
    cot = cotangent.reshape(MB, SQ, D)
    index = [lax.axis_index(a) for a in ("x", "c", "z", "y")]
    sc = jnp.stack(index + [patch_counts[0, 0], patch_counts[1, 0], 0, 0]).astype(jnp.int32)

    shared, own, mlp_shard, joined = pack(
        wkv, rattn, rmlp, gain1, bias1, gain2, bias2, wq, wo, wup, wdown,
        *[jnp.moveaxis(r.reshape(MB, SQ, 4), 1, 2) for r in (attn_routes, mlp_routes)],
        tokens,
        cot,
    )
    got = fetch(shared, "x")
    kv12 = jnp.concatenate([v[0:3, 0:896] for v in got], 0)
    shard = jnp.concatenate([own[:, 0:12], kv12[:, :768].reshape(3, 4, 768)], 1).reshape(48, 768)
    shard = jnp.concatenate([shard, jnp.pad(kv12[:, 768:], ((0, 36), (0, 0)))], 1)
    zs = jnp.stack(fetch(shard, "z"))
    zs, sc = tie(zs, sc)
    tall = lax.all_gather(joined, "x", axis=0)
    posr, posc = plan(sc, got)
    pieces = fetch(zs, "y")
    both = tie(*pieces, posr, posc)
    pieces, posr, posc = list(both[:4]), both[4], both[5]
    pieces = pieces + [shift(p, "c", 1) for p in pieces]
    *pieces, mlp_shard, tall = tie(*pieces, mlp_shard, tall)
    wmlp = lax.all_gather(mlp_shard, TOKS, axis=0).reshape(32, EXP, 112, D)

    parts, saved, (fq, fo, fkvt, sm, vec) = attend(sc, tall, posr, posc, pieces)
    mixed, mlp_in = mix(tokens, send(parts, "x"), vec)
    xs = fetch(mlp_in, "x")
    outp, gradp, rm, (keep, give, down) = experts(sc, xs, tall, posr, posc, sm, wmlp)
    down = lax.psum_scatter(down, TOKS, scatter_dimension=0, tiled=True)
    give = shift(give, "c", 1)
    gradp = send(gradp, "x")
    up = add2(keep, give)
    *gradp, up = tie(*gradp, up)
    up = lax.all_to_all(up, ("z", "y"), 0, 0, tiled=True)
    gmix, gmixb, gv = turn(mixed, cot, gradp, vec)
    gms = fetch(gmixb, "x")
    back, (ta, ta1) = attend_back(sc, gms, tall, posr, saved, fq, fo, fkvt, sm, vec, gv, rm)
    ta1 = shift(ta1, "c", 1)
    ta1, back, outp = tie(ta1, back, outp)
    ta, up = tie(add2(ta, ta1), up)
    ta = lax.all_to_all(ta, ("z", "y"), 0, 0, tiled=True)
    back = send(back, "x")
    outp, back = tie(outp, back)
    outp = send(outp, "x")
    dup = jnp.sum(up.astype(F32), 0)[:, 0:12]
    tokens_grad = finish(gmix, tokens, back, vec)
    ta, dup, tokens_grad = tie(ta, dup, tokens_grad)
    ta = jnp.sum(ta.astype(F32), 0)
    ta, *outp = tie(ta, *outp)
    result = mixed
    for o in outp:
        result = result + o.astype(F32)
    result = result.astype(BF)
    t3 = ta.reshape(3, 16, 896)
    kv = jnp.concatenate([t3[:, 12:16, :768].reshape(12, 768), ta[0:12, 768:]], 1)
    small = fold(kv.astype(BF).reshape(4, 3, 896), "x")
    small, down = tie(small, down)

    ddown = down.astype(F32).reshape(EXP, 48, D)
    dq, do = t3[:, :12, :D], t3[:, :12, D:768]
    shape = (MB, 1, SQ, D)
    return (
        result.reshape(shape),
        tokens_grad.reshape(shape),
        small[:, 792],
        small[:, 793],
        small[:, 794],
        small[:, 795],
        small[:, 0:768],
        small[:, 768:780],
        small[:, 780:792],
        dq,
        do,
        dup,
        ddown,
    )


def solution(mesh):
    fine = Mesh(mesh.devices.reshape(4, 4, 2, 4), ("z", "y", "c", "x"))
    every = TOKS + ("x",)
    act = P(None, TOKS, "x", None)
    row, mat, own = P(every), P(every, None), P("x", TOKS, None)
    return jax.shard_map(
        local,
        mesh=fine,
        in_specs=(
            act, P(None, TOKS), act, act, row, row, row, row, mat, mat, mat, own, own, own, own, act,
        ),
        out_specs=(act, act, row, row, row, row, mat, mat, mat, own, own, own, own),
        check_vma=False,
    )
```
